32 devices in a mesh: wide: 8 (over z, y), narrow: 4 (over x, core).
Axes of the slice: x: 2, y: 2, z: 4, core: 2. Of those that a mesh axis runs over, the one named last changes fastest.
Arguments:
- diag_block: float32 [32, 512, 512], P('wide', None, 'narrow'), as said below
- panel: float32 [32, 1024, 512], P('wide', None, 'narrow'), may hold values from -2 to 2
- panel_count: int32 [32], P('wide'), may hold values from 1 to 8, 144 in all
- pair_owner: int32 [1152, 1], P('wide'), may hold values from 0 to 7; in each aligned block of 144 rows (0 to 143, 144 to 287, ...) at most 18 rows name the same one
- pair_slot: int32 [1152], P('wide'), may hold values from 0 to 7
- ancestor: float32 [64, 128, 128], P(('wide', 'narrow')), may hold values from -6 to 6
Outputs:
- factor: float32 [32, 512, 512], P('wide', None, 'narrow')
- lower_panel: float32 [32, 1024, 512], P('wide', None, 'narrow')
- updated: float32 [64, 128, 128], P(('wide', 'narrow'))
The draws below stay inside these ranges and needn't reach their ends.
Inputs may be any that keep to these rules, and one draw needn't show every extreme that they name: Each diag_block[s] is symmetric, and its least eigenvalue is 0.2 or more. `pair_owner`: among the rows of one index of wide no owner is named more than 18 times, a bound that some block reaches.
All inputs are finite; a program needn't handle non-finite values. No bound on the sum of `panel_count` on one device may be relied on, other than what follows from the above.
Results may differ from the reference program's by a relative error of at most 0.00016.
Values sent between devices are 32-bit elements; how exact they have to be, the bound alone decides.
No kernel may reach another device: no remote copies, remote signals or barrier semaphores. Data moves between devices by JAX's collectives and lax.ppermute only.
A program may use at most 128 MiB of HBM per device.

```python
import math
import jax
import jax.numpy as jnp
import numpy as np
from jax import lax

W = 512
B = 128
P_SIZE = 8
T_DEV = 2
SUPERS = 32
TILES = 64
NPAIR = 36
ROWS_DEV = 144
CAP = 18
N_WIDE = 8
N_NARROW = 4


def draw_diag_block(key, part):
    first_key = jax.random.fold_in(jax.random.fold_in(key, 7), 0)
    factors = jax.random.normal(first_key, (SUPERS, W, W), jnp.float32)
    scales = jnp.ones((SUPERS, W, 1), jnp.float32)
    gram = jnp.einsum('sik,sjk->sij', factors, factors, precision=lax.Precision.HIGHEST) * (1.0 / W)
    gram = 0.5 * (gram + jnp.swapaxes(gram, 1, 2))
    identity = jnp.eye(W, dtype=jnp.float32)
    shifted = gram + 0.2 * identity
    return shifted * jnp.swapaxes(scales, 1, 2)


def set_ends(drawn, own_key, smallest, largest):
    longest = drawn.shape.index(max(drawn.shape))
    spots = []
    for shift in (0, 1):
        where = [jax.random.randint(jax.random.fold_in(own_key, axis), (), 0, length) for axis, length in enumerate(drawn.shape)]
        where[longest] = (where[longest] + shift) % drawn.shape[longest]
        spots.append(tuple(where))
    return drawn.at[spots[0]].set(smallest).at[spots[1]].set(largest)


def steps_of(own_key, dims, shards, least, largest):
    def one(position, blocks):
        draws = jax.random.uniform(jax.random.fold_in(jax.random.fold_in(own_key, 6), position), (blocks,), jnp.float32, least / len(shards), largest / len(shards))
        return jnp.repeat(jnp.exp(draws), dims[position] // blocks).reshape((-1,) + (1,) * (len(dims) - position - 1))

    factor_of = one(*shards[0])
    for cut in shards[1:]:
        factor_of = factor_of * one(*cut)
    return factor_of


def length_profile(amount, total, bound, slope):
    portions = [(1 << 20) // math.isqrt(standing ** slope) + 1 for standing in range(2, amount + 1)]
    surplus, holding = total - bound - (amount - 1), [1] * (amount - 1)
    while surplus > 0:
        free = [i for i in range(amount - 1) if holding[i] < bound]
        whole, left = sum([portions[i] for i in free]), surplus
        for i in free:
            extra = min(bound - holding[i], max(1, left * portions[i] // whole), surplus)
            holding[i] = holding[i] + extra
            surplus = surplus - extra
    return np.array([bound] + holding)


def ragged(key, number_of, total, most, lean):
    if number_of == 2:
        one = jax.random.randint(key, (), max(1, total - most), min(most, total - 1) + 1)
        return jnp.stack([one, total - one])
    lengths = jnp.asarray(length_profile(number_of, total, most, lean), jnp.int32)
    couples = (number_of - 1) // 2
    giver, sink = lengths[1:1 + 2 * couples:2], lengths[2:2 + 2 * couples:2]
    margin = jnp.minimum(giver - 1, most - sink)
    passed = jax.random.randint(jax.random.fold_in(key, 1), (couples,), 0, 1 << 20) % (margin + 1)
    lengths = lengths.at[1:1 + 2 * couples:2].set(giver - passed).at[2:2 + 2 * couples:2].set(sink + passed)
    return lengths[jax.random.permutation(jax.random.fold_in(key, 2), number_of)]


def assign_block(rng, own, number, rows, count, top, limit, slope):
    sequence = jax.random.permutation(rng, count)
    packed, ordinary = portions_of(count, rows * top, limit, slope, True), portions_of(count, rows * top, limit, slope, False)
    places = jnp.arange(count)

    def named(sizes, rotation):
        used = int((sizes > 0).sum())
        fixed = max(1, used // 4)
        moved = fixed + (places - fixed + rotation * (used - fixed)) % max(1, count - fixed)
        return jnp.zeros((count,), jnp.int32).at[sequence[jnp.where(places < fixed, places, moved)]].set(jnp.asarray(sizes, jnp.int32))

    sizes = jnp.where(number % 4 == 0, named(packed, number // 4), named(ordinary, number - number // 4 - 1))
    mixed = jax.random.permutation(jax.random.fold_in(own, 3), count)
    giver, sink = mixed[0:count // 2 * 2:2], mixed[1:count // 2 * 2:2]
    margin = jnp.minimum(sizes[giver] - 1, limit - sizes[sink]) // 2
    margin = jnp.where((giver == sequence[0]) | (sink == sequence[0]) | (sizes[sink] == 0), 0, jnp.maximum(margin, 0))
    moved = jax.random.randint(jax.random.fold_in(own, 4), (count // 2,), 0, 1 << 20) % (margin + 1)
    sizes = sizes.at[giver].add(-moved).at[sink].add(moved)
    items = jnp.searchsorted(jnp.cumsum(sizes), jnp.arange(rows * top), side="right").astype(jnp.int32)
    table = items.reshape(top, rows).T
    table = table[jax.random.permutation(jax.random.fold_in(own, 1), rows)]
    rotation = jax.random.randint(jax.random.fold_in(own, 2), (rows, 1), 0, top)
    return jnp.take_along_axis(table, (jnp.arange(top)[None, :] + rotation) % top, axis=1)


def portions_of(number_of, total, bound, slope, full):
    portions = [(1 << 20) // math.isqrt(rank ** slope) + 1 for rank in range(1, number_of + 1)]
    largest = bound if full else min(bound, max(-(-total // number_of), total * portions[0] // sum(portions)))
    least = 1 if total - largest >= number_of - 1 else 0
    holding, rest = [largest] + [least] * (number_of - 1), total - largest - least * (number_of - 1)
    while rest > 0:
        movable = [i for i in range(1, number_of) if holding[i] < largest] or [i for i in range(1, number_of) if holding[i] < bound]
        pool, remaining = sum([portions[i] for i in movable]), rest
        for i in movable:
            addition = min(bound - holding[i], max(1, remaining * portions[i] // pool), rest)
            holding[i] = holding[i] + addition
            rest = rest - addition
    return np.array(holding)


def noise(own_key, shape, spread, reach, cuts=(), kind=jnp.bfloat16):
    drawn = spread * jax.random.normal(own_key, shape, jnp.float32)
    if cuts:
        drawn = drawn * steps_of(own_key, shape, cuts, -0.22, 0.18)
    return jnp.clip(drawn, -reach, reach).astype(kind)


def setup_inputs(seed: int = 0) -> dict:
    key_of = jax.random.split(jax.random.key(seed), 7)
    diag_block = draw_diag_block(jax.random.fold_in(key_of[6], 71), 0)
    panel = noise(key_of[1], (SUPERS, P_SIZE * B, W), 0.15, 2.0, ((0, 8), (2, 4)), jnp.float32)
    panel_count = ragged(key_of[2], SUPERS, SUPERS * (P_SIZE + 1) // 2, P_SIZE, 2).astype(jnp.int32)
    pair_owner_keys = jax.random.split(jax.random.fold_in(key_of[3], 1), (SUPERS * NPAIR) // ROWS_DEV)
    pair_owner_turns = jax.random.permutation(jax.random.fold_in(key_of[3], 3), (SUPERS * NPAIR) // ROWS_DEV)
    pair_owner = jax.vmap(lambda own, number: assign_block(jax.random.fold_in(key_of[3], 2), own, number, ROWS_DEV, N_WIDE, 1, CAP, 2))(pair_owner_keys, pair_owner_turns).reshape((SUPERS * NPAIR, 1))
    pair_slot = set_ends(jax.random.randint(key_of[4], (SUPERS * NPAIR,), 0, T_DEV * N_NARROW), jax.random.fold_in(key_of[4], 1), 0, (T_DEV * N_NARROW) - 1).astype(jnp.int32)
    ancestor = noise(key_of[5], (TILES, B, B), 1.0, 6.0, ((0, 32),), jnp.float32)
    return dict(diag_block=diag_block, panel=panel, panel_count=panel_count, pair_owner=pair_owner, pair_slot=pair_slot, ancestor=ancestor)


def pair_lists(count):
    first = []
    second = []
    for outer in range(count):
        for inner in range(outer + 1):
            first.append(outer)
            second.append(inner)
    return (np.array(first, np.int32), np.array(second, np.int32))

def reference(diag_block, panel, panel_count, pair_owner, pair_slot, ancestor):
    factor = jnp.linalg.cholesky(diag_block)
    identity = jnp.broadcast_to(jnp.eye(W, dtype=jnp.float32), factor.shape)
    inverse = lax.linalg.triangular_solve(factor, identity, left_side=True, lower=True)
    lower_panel = jnp.einsum('srk,sck->src', panel, inverse, precision=lax.Precision.HIGHEST)
    block_index = jnp.arange(P_SIZE * B, dtype=jnp.int32) // B
    live = (block_index[None, :] < panel_count[:, None]).astype(jnp.float32)
    lower_panel = lower_panel * live[:, :, None]
    first, second = pair_lists(P_SIZE)
    target = pair_owner[:, 0] * (T_DEV * N_NARROW) + pair_slot
    target = target.reshape(SUPERS, NPAIR).astype(jnp.int32)

    def one_super(tiles, items):
        rows, goal = items
        blocks = rows.reshape(P_SIZE, B, W)
        contribution = jnp.einsum('pac,pbc->pab', blocks[first], blocks[second], precision=lax.Precision.HIGHEST)
        return (tiles.at[goal].add(contribution), None)
    summed, _ = lax.scan(one_super, jnp.zeros(ancestor.shape, jnp.float32), (lower_panel, target))
    return (factor, lower_panel, ancestor - summed)
```

```python
import functools

import jax
import jax.numpy as jnp
import numpy as np
from jax import lax
from jax.experimental import pallas as pl
from jax.experimental.pallas import tpu as pltpu
from jax.sharding import PartitionSpec as P

W = 512
B = 128
P_SIZE = 8
T_DEV = 2
NB = W // B
NPAIR = P_SIZE * (P_SIZE + 1) // 2
HIGHEST = lax.Precision.HIGHEST


def dot_nt(a, b):
    return lax.dot_general(
        a, b, (((1,), (1,)), ((), ())), precision=HIGHEST, preferred_element_type=jnp.float32
    )


def dot_nn(a, b):
    return lax.dot_general(
        a, b, (((1,), (0,)), ((), ())), precision=HIGHEST, preferred_element_type=jnp.float32
    )


def lane_of(x, c):
    return jnp.broadcast_to(x[:, c : c + 1], x.shape)


def row_of(x, r):
    return jnp.broadcast_to(x[r : r + 1, :], x.shape)


def inverse_factor(block):
    sub = lax.broadcasted_iota(jnp.int32, (8, B), 0)
    lane = lax.broadcasted_iota(jnp.int32, (8, B), 1)
    rows = [block[8 * q : 8 * q + 8, :] for q in range(B // 8)]
    done = []
    for p in range(B // 8):
        lo = 8 * p
        own = (lane >= lo) & (lane < lo + 8)
        cols = [lane_of(rows[p], lo + m) for m in range(8)]
        work = jnp.where(own, (lane - lo == sub).astype(jnp.float32), rows[p])
        final = jnp.zeros((8, B), jnp.float32)
        for k in range(8):
            pivot = row_of(cols[k], k)
            recip = 1.0 / pivot
            raw = row_of(work, k)
            final = jnp.where(sub == k, raw * lax.rsqrt(pivot), final)
            factor = cols[k]
            scaled = raw * recip
            work = jnp.where(sub == k, scaled, work - factor * scaled)
            for m in range(k + 1, 8):
                line = row_of(cols[m], k) * recip
                cols[m] = jnp.where(sub == k, line, cols[m] - factor * line)
        done.append(jnp.where(lane <= sub + lo, final, 0.0))
        lines = [row_of(work, m) for m in range(8)]
        for q in range(p + 1, B // 8):
            mult = [lane_of(rows[q], lo + m) for m in range(8)]
            new = jnp.where(own, 0.0, rows[q])
            for m in range(8):
                new = new - mult[m] * lines[m]
            rows[q] = new
    return jnp.concatenate(done, axis=0)


def factor_kernel(info, own_ref, r1, r2, r3, l0, l1, l2, l3, inv_out, a, l, mt, sems):
    me = info[0]
    ins = [own_ref.at[me], r1, r2, r3]
    copies = [pltpu.make_async_copy(ins[m], a.at[me ^ m], sems.at[m]) for m in range(NB)]
    for c in copies:
        c.start()
    for c in copies:
        c.wait()
    row = lax.broadcasted_iota(jnp.int32, (B, B), 0)
    col = lax.broadcasted_iota(jnp.int32, (B, B), 1)
    l[...] = jnp.zeros_like(l)
    mt[...] = jnp.zeros_like(mt)
    eye = (row == col).astype(jnp.float32)
    for k in range(NB):
        here = pl.ds(k * B, B)
        inv = inverse_factor(a[k, here, :])
        l[k, here, :] = jnp.where(row >= col, dot_nt(a[k, here, :], inv), 0.0)
        for i in range(k + 1, NB):
            below = dot_nt(a[k, pl.ds(i * B, B), :], inv)
            l[k, pl.ds(i * B, B), :] = below
            for j in range(k + 1, i + 1):
                a[j, pl.ds(i * B, B), :] -= dot_nt(below, l[k, pl.ds(j * B, B), :])
        mt[k, here, :] = dot_nt(eye, inv)
        for i in range(k):
            total = dot_nt(mt[i, pl.ds(i * B, B), :], l[i, here, :])
            for j in range(i + 1, k):
                total = total + dot_nt(mt[j, pl.ds(i * B, B), :], l[j, here, :])
            mt[k, pl.ds(i * B, B), :] = dot_nt(-total, inv)
    outs = [l0, l1, l2, l3]
    copies = [pltpu.make_async_copy(l.at[me ^ m], outs[m], sems.at[m]) for m in range(NB)]
    copies.append(pltpu.make_async_copy(mt, inv_out, sems.at[NB]))
    for c in copies:
        c.start()
    for c in copies:
        c.wait()


def panel_kernel(info, tgt_a, tgt_b, own_ref, r1, r2, r3, mt_ref, *rest):
    (x0, x1, x2, x3, keep_a, send_a, keep_b, send_b, p, x, mt, ta, tb, sems) = rest
    me = info[0]
    count = info[1]
    ins = [own_ref.at[me], r1, r2, r3]
    copies = [pltpu.make_async_copy(ins[m], p.at[me ^ m], sems.at[m]) for m in range(NB)]
    copies.append(pltpu.make_async_copy(mt_ref, mt, sems.at[NB]))
    for c in copies:
        c.start()
    ta[...] = jnp.zeros_like(ta)
    tb[...] = jnp.zeros_like(tb)
    for c in copies:
        c.wait()
    for i in range(P_SIZE):
        here = pl.ds(i * B, B)

        @pl.when(i < count)
        def _():
            for c in range(NB):
                left = jnp.concatenate([p[j, here, :] for j in range(c + 1)], axis=1)
                x[c, here, :] = dot_nn(left, mt[c, pl.ds(0, (c + 1) * B), :])

        @pl.when(i >= count)
        def _():
            for c in range(NB):
                x[c, here, :] = jnp.zeros((B, B), jnp.float32)

    outs = [x0, x1, x2, x3]
    copies = [pltpu.make_async_copy(x.at[me ^ m], outs[m], sems.at[m]) for m in range(NB)]
    for c in copies:
        c.start()
    half_a = ta.shape[1]
    for i in range(P_SIZE):

        @pl.when(i < count)
        def _():
            left = jnp.concatenate([x[c, pl.ds(i * B, B), :] for c in range(NB)], axis=1)
            for j in range(i + 1):
                right = jnp.concatenate([x[c, pl.ds(j * B, B), :] for c in range(NB)], axis=1)
                got = dot_nt(left, right)
                pair = i * (i + 1) // 2 + j
                at_a = tgt_a[pair]
                at_b = tgt_b[pair]
                ta[at_a] += got[:half_a]
                tb[at_b] += got[half_a:]

    half = ta.shape[0] // 2
    more = [
        pltpu.make_async_copy(ta.at[pl.ds(0, half)], keep_a, sems.at[NB]),
        pltpu.make_async_copy(ta.at[pl.ds(half, half)], send_a, sems.at[NB + 1]),
        pltpu.make_async_copy(tb.at[pl.ds(0, half)], keep_b, sems.at[NB + 2]),
        pltpu.make_async_copy(tb.at[pl.ds(half, half)], send_b, sems.at[NB + 3]),
    ]
    for c in more:
        c.start()
    for c in copies + more:
        c.wait()


SMEM = pl.BlockSpec(memory_space=pltpu.SMEM)
ANY = pl.BlockSpec(memory_space=pl.ANY)


def xor_pairs(size, mask):
    return [(i, i ^ mask) for i in range(size)]


def log2(n):
    return n.bit_length() - 1


def swap(x, axis, mask):
    return lax.ppermute(x, axis, xor_pairs(lax.axis_size(axis), mask))


def relative_index(owner, slot, wide_me, narrow_me, steps):
    away = {"wide": owner ^ wide_me, "narrow": (slot // T_DEV) ^ narrow_me}
    index = jnp.zeros_like(owner)
    for axis, mask in steps:
        index = index * 2 + ((away[axis] // mask) & 1)
    return index * T_DEV + slot % T_DEV


def local(split, diag_block, panel, panel_count, pair_owner, pair_slot, ancestor):
    narrow_count = lax.axis_size("narrow")
    wide_count = lax.axis_size("wide")
    me = lax.axis_index("narrow")
    wide_me = lax.axis_index("wide")
    assert narrow_count == NB and diag_block.shape[0] == NB
    masks = range(1, NB)
    own = lambda x, m: lax.dynamic_index_in_dim(x, me ^ m, 0, keepdims=False)
    diag_in = [swap(own(diag_block, m), "narrow", m) for m in masks]
    panel_in = [swap(own(panel, m), "narrow", m) for m in masks]

    narrow_steps = [("narrow", 1 << b) for b in range(log2(narrow_count))]
    wide_steps = [("wide", 1 << b) for b in range(log2(wide_count))]
    steps_a = narrow_steps + wide_steps
    steps_b = narrow_steps[:1] + wide_steps + narrow_steps[1:]
    owner = lax.dynamic_slice_in_dim(pair_owner[:, 0], me * NPAIR, NPAIR)
    slot = lax.dynamic_slice_in_dim(pair_slot, me * NPAIR, NPAIR)
    tgt_a = relative_index(owner, slot, wide_me, me, steps_a)
    tgt_b = relative_index(owner, slot, wide_me, me, steps_b)
    info = jnp.stack([me, panel_count[me]]).astype(jnp.int32)

    slab = jax.ShapeDtypeStruct((W, B), jnp.float32)
    *l_parts, mt = pl.pallas_call(
        factor_kernel,
        out_shape=[slab] * NB + [jax.ShapeDtypeStruct((NB, W, B), jnp.float32)],
        in_specs=[SMEM] + [ANY] * NB,
        out_specs=[ANY] * (NB + 1),
        scratch_shapes=[pltpu.VMEM((NB, W, B), jnp.float32)] * 3 + [pltpu.SemaphoreType.DMA((NB + 1,))],
        compiler_params=pltpu.CompilerParams(vmem_limit_bytes=32 * 2**20),
        cost_estimate=pl.CostEstimate(flops=2 * 10**8, bytes_accessed=4 * 10**6, transcendentals=0),
        name="factor",
    )(info, diag_block, *diag_in)

    rows = P_SIZE * B
    blocks = wide_count * narrow_count * T_DEV
    slab = jax.ShapeDtypeStruct((rows, B), jnp.float32)
    part_a = jax.ShapeDtypeStruct((blocks // 2, split, B), jnp.float32)
    part_b = jax.ShapeDtypeStruct((blocks // 2, B - split, B), jnp.float32)
    *x_parts, keep_a, send_a, keep_b, send_b = pl.pallas_call(
        panel_kernel,
        out_shape=[slab] * NB + [part_a, part_a, part_b, part_b],
        in_specs=[SMEM] * 3 + [ANY] * (NB + 1),
        out_specs=[ANY] * (NB + 4),
        scratch_shapes=[
            pltpu.VMEM((NB, rows, B), jnp.float32),
            pltpu.VMEM((NB, rows, B), jnp.float32),
            pltpu.VMEM((NB, W, B), jnp.float32),
            pltpu.VMEM((blocks, split, B), jnp.float32),
            pltpu.VMEM((blocks, B - split, B), jnp.float32),
            pltpu.SemaphoreType.DMA((NB + 4,)),
        ],
        compiler_params=pltpu.CompilerParams(vmem_limit_bytes=52 * 2**20),
        cost_estimate=pl.CostEstimate(flops=10**9, bytes_accessed=10 * 10**6, transcendentals=0),
        name="panel",
    )(info, tgt_a, tgt_b, panel, *panel_in, mt)

    def reduce(keep, send, steps):
        for n, (axis, mask) in enumerate(steps):
            got = swap(send, axis, mask)
            if n + 1 < len(steps):
                half = keep.shape[0] // 2
                send = keep[half:] + got[half:]
                keep = keep[:half] + got[:half]
            else:
                keep = keep + got
        return keep

    sum_a = reduce(keep_a, send_a, steps_a)
    sum_b = reduce(keep_b, send_b, steps_b)
    updated = ancestor - jnp.concatenate([sum_a, sum_b], axis=1)

    def give_back(parts):
        back = [parts[0]] + [swap(parts[m], "narrow", m) for m in masks]
        out = jnp.zeros((NB,) + parts[0].shape, jnp.float32)
        for m in range(NB):
            out = lax.dynamic_update_index_in_dim(out, back[m], me ^ m, 0)
        return out

    return (give_back(l_parts), give_back(x_parts), updated)


def solution(mesh):
    placed = (
        P("wide", None, "narrow"),
        P("wide", None, "narrow"),
        P("wide"),
        P("wide", None),
        P("wide"),
        P(("wide", "narrow"), None, None),
    )
    return jax.shard_map(
        functools.partial(local, 64),
        mesh=mesh,
        in_specs=placed,
        out_specs=(
            P("wide", None, "narrow"),
            P("wide", None, "narrow"),
            P(("wide", "narrow"), None, None),
        ),
        check_vma=False,
    )
```

```python
import functools

import jax
import jax.numpy as jnp
import numpy as np
from jax import lax
from jax.experimental import pallas as pl
from jax.experimental.pallas import tpu as pltpu
from jax.sharding import PartitionSpec as P

W = 512
B = 128
P_SIZE = 8
T_DEV = 2
NB = W // B
NPAIR = P_SIZE * (P_SIZE + 1) // 2
HIGHEST = lax.Precision.HIGHEST


def dot_nt(a, b):
    return lax.dot_general(
        a, b, (((1,), (1,)), ((), ())), precision=HIGHEST, preferred_element_type=jnp.float32
    )


def dot_nn(a, b):
    return lax.dot_general(
        a, b, (((1,), (0,)), ((), ())), precision=HIGHEST, preferred_element_type=jnp.float32
    )


def lane_of(x, c):
    return jnp.broadcast_to(x[:, c : c + 1], x.shape)


def row_of(x, r):
    return jnp.broadcast_to(x[r : r + 1, :], x.shape)


def inverse_factor(block):
    sub = lax.broadcasted_iota(jnp.int32, (8, B), 0)
    lane = lax.broadcasted_iota(jnp.int32, (8, B), 1)
    total, strip = B // 8, 2
    rows = [block[8 * q : 8 * q + 8, :] for q in range(total)]
    done = [None] * total
    for b in range(0, total, strip):
        mine = range(b, b + strip)
        near = range(b + strip, min(b + 2 * strip, total))
        far = range(b + 2 * strip, total)
        in_strip = (lane >= 8 * b) & (lane < 8 * (b + strip))
        ahead = {q: [lane_of(rows[q], 8 * b + m) for m in range(8 * strip)] for q in near}
        for p in mine:
            lo = 8 * p
            own = (lane >= lo) & (lane < lo + 8)
            cols = [lane_of(rows[p], lo + m) for m in range(8)]
            others = [q for q in mine if q != p]
            mult = {q: [lane_of(rows[q], lo + m) for m in range(8)] for q in others}
            work = jnp.where(own, (lane - lo == sub).astype(jnp.float32), rows[p])
            final = jnp.zeros((8, B), jnp.float32)
            for k in range(0, 8, 2):
                f0, f1 = cols[k], cols[k + 1]
                a, h, c = row_of(f0, k), row_of(f0, k + 1), row_of(f1, k + 1)
                det = a * c - h * h
                recip = 1.0 / det
                ar, hr, cr = a * recip, h * recip, c * recip
                first, second = sub == k, sub == k + 1

                def eliminate(v):
                    r0, r1 = row_of(v, k), row_of(v, k + 1)
                    s0, s1 = cr * r0 - hr * r1, ar * r1 - hr * r0
                    return r0, r1, jnp.where(first, s0, jnp.where(second, s1, v - f0 * s0 - f1 * s1))

                for m in range(k + 2, 8):
                    cols[m] = eliminate(cols[m])[2]
                r0, r1, work = eliminate(work)
                root = lax.rsqrt(a)
                lower = (a * r1 - h * r0) * (root * lax.rsqrt(det))
                final = jnp.where(first, r0 * root, jnp.where(second, lower, final))
            done[p] = jnp.where(lane <= sub + lo, final, 0.0)
            rows[p] = work
            lines = [row_of(work, m) for m in range(8)]
            for q in others:
                new = jnp.where(own, 0.0, rows[q])
                for m in range(8):
                    new = new - mult[q][m] * lines[m]
                rows[q] = new
        lines = [row_of(rows[q], m) for q in mine for m in range(8)]
        for q in near:
            parts = [ahead[q][m] * lines[m] for m in range(4)]
            for m in range(4, 8 * strip):
                parts[m % 4] = parts[m % 4] + ahead[q][m] * lines[m]
            rows[q] = jnp.where(in_strip, 0.0, rows[q]) - ((parts[0] + parts[1]) + (parts[2] + parts[3]))
        if far:
            stack = jnp.concatenate([rows[q] for q in far], axis=0)
            lane_far = lax.broadcasted_iota(jnp.int32, stack.shape, 1)
            in_far = (lane_far >= 8 * b) & (lane_far < 8 * (b + strip))
            zero = jnp.zeros((8, B), jnp.float32)
            tall = jnp.concatenate([rows[q] if q in mine else zero for q in range(total)], axis=0)
            stack = jnp.where(in_far, 0.0, stack) - dot_nn(jnp.where(in_far, stack, 0.0), tall)
            for n, q in enumerate(far):
                rows[q] = stack[8 * n : 8 * n + 8]
    return jnp.concatenate(done, axis=0)


def split_bf16(v):
    high = v.astype(jnp.bfloat16)
    return high, (v - high.astype(jnp.float32)).astype(jnp.bfloat16)


def dot3(left, right, contract):
    dot = lambda a, b: lax.dot_general(
        a, b, (contract, ((), ())), preferred_element_type=jnp.float32
    )
    return dot(left[0], right[0]) + (dot(left[0], right[1]) + dot(left[1], right[0]))


def factor_kernel(info, own_ref, r1, r2, r3, l0, l1, l2, l3, inv_out, a, l, mt, sems):
    me = info[0]
    side = me // 2
    far_rows = pl.ds((1 - side) * (W // 2), W // 2)
    places = [a.at[me], a.at[me ^ 1], a.at[me ^ 2, far_rows], a.at[me ^ 3, far_rows]]
    ins = [own_ref.at[me], r1, r2, r3]
    copies = [pltpu.make_async_copy(ins[m], places[m], sems.at[m]) for m in range(NB)]
    for c in copies:
        c.start()
    for c in copies:
        c.wait()

    @pl.when(side == 1)
    def _():
        for j in range(NB // 2):
            for i in range(NB // 2, NB):
                a[j, pl.ds(i * B, B), :] = a[i, pl.ds(j * B, B), :].T

    row = lax.broadcasted_iota(jnp.int32, (B, B), 0)
    col = lax.broadcasted_iota(jnp.int32, (B, B), 1)
    l[...] = jnp.zeros_like(l)
    mt[...] = jnp.zeros_like(mt)
    eye = (row == col).astype(jnp.float32)
    for k in range(NB):
        here = pl.ds(k * B, B)
        inv = inverse_factor(a[k, here, :])
        l[k, here, :] = jnp.where(row >= col, dot_nt(a[k, here, :], inv), 0.0)
        for i in range(k + 1, NB):
            below = dot_nt(a[k, pl.ds(i * B, B), :], inv)
            l[k, pl.ds(i * B, B), :] = below
            for j in range(k + 1, i + 1):
                a[j, pl.ds(i * B, B), :] -= dot_nt(below, l[k, pl.ds(j * B, B), :])
        mt[k, here, :] = dot_nt(eye, inv)
        for i in range(k):
            total = dot_nt(mt[i, pl.ds(i * B, B), :], l[i, here, :])
            for j in range(i + 1, k):
                total = total + dot_nt(mt[j, pl.ds(i * B, B), :], l[j, here, :])
            mt[k, pl.ds(i * B, B), :] = dot_nt(-total, inv)
    outs = [l0, l1, l2, l3]
    copies = [pltpu.make_async_copy(l.at[me ^ m], outs[m], sems.at[m]) for m in range(NB)]
    copies.append(pltpu.make_async_copy(mt, inv_out, sems.at[NB]))
    for c in copies:
        c.start()
    for c in copies:
        c.wait()


def panel_kernel(info, tgt_a, tgt_b, own_ref, r1, r2, r3, mt_ref, *rest):
    (x0, x1, x2, x3, keep_a, send_a, keep_b, send_b, p, x, mt, xh, xl, ta, tb, sems) = rest
    me = info[0]
    count = info[1]
    ins = [own_ref.at[me], r1, r2, r3]
    copies = [pltpu.make_async_copy(ins[m], p.at[me ^ m], sems.at[m]) for m in range(NB)]
    copies.append(pltpu.make_async_copy(mt_ref, mt, sems.at[NB]))
    for c in copies:
        c.start()
    ta[...] = jnp.zeros_like(ta)
    tb[...] = jnp.zeros_like(tb)
    for c in copies:
        c.wait()
    rows = P_SIZE * B
    live = lax.broadcasted_iota(jnp.int32, (rows, B), 0) < count * B
    parts = [split_bf16(jnp.where(live, p[c], 0.0)) for c in range(NB)]
    for c in range(0, NB, 2):
        left = [jnp.concatenate([parts[j][n] for j in range(c + 2)], axis=1) for n in range(2)]
        right = split_bf16(
            jnp.concatenate([mt[c, pl.ds(0, (c + 2) * B), :], mt[c + 1, pl.ds(0, (c + 2) * B), :]], axis=1)
        )
        got = dot3(left, right, ((1,), (0,)))
        x[c] = got[:, :B]
        x[c + 1] = got[:, B:]
        high, low = split_bf16(got)
        xh[:, pl.ds(c * B, 2 * B)] = high
        xl[:, pl.ds(c * B, 2 * B)] = low

    outs = [x0, x1, x2, x3]
    copies = [pltpu.make_async_copy(x.at[me ^ m], outs[m], sems.at[m]) for m in range(NB)]
    for c in copies:
        c.start()
    half_a = ta.shape[1]
    for j in range(0, P_SIZE, 2):

        @pl.when(j < count)
        def _():
            left = (xh[pl.ds(j * B, rows - j * B), :], xl[pl.ds(j * B, rows - j * B), :])
            right = (xh[pl.ds(j * B, 2 * B), :], xl[pl.ds(j * B, 2 * B), :])
            got = dot3(left, right, ((1,), (1,)))
            for i in range(j, P_SIZE):
                for n in range(2 if i > j else 1):
                    block = got[(i - j) * B : (i - j + 1) * B, n * B : (n + 1) * B]
                    pair = i * (i + 1) // 2 + j + n
                    at_a = tgt_a[pair]
                    at_b = tgt_b[pair]
                    ta[at_a] += block[:half_a]
                    tb[at_b] += block[half_a:]

    half = ta.shape[0] // 2
    more = [
        pltpu.make_async_copy(ta.at[pl.ds(0, half)], keep_a, sems.at[NB]),
        pltpu.make_async_copy(ta.at[pl.ds(half, half)], send_a, sems.at[NB + 1]),
        pltpu.make_async_copy(tb.at[pl.ds(0, half)], keep_b, sems.at[NB + 2]),
        pltpu.make_async_copy(tb.at[pl.ds(half, half)], send_b, sems.at[NB + 3]),
    ]
    for c in more:
        c.start()
    for c in copies + more:
        c.wait()


SMEM = pl.BlockSpec(memory_space=pltpu.SMEM)
ANY = pl.BlockSpec(memory_space=pl.ANY)


def xor_pairs(size, mask):
    return [(i, i ^ mask) for i in range(size)]


def log2(n):
    return n.bit_length() - 1


def swap(x, axis, mask):
    return lax.ppermute(x, axis, xor_pairs(lax.axis_size(axis), mask))


def relative_index(owner, slot, wide_me, narrow_me, steps):
    away = {"wide": owner ^ wide_me, "narrow": (slot // T_DEV) ^ narrow_me}
    index = jnp.zeros_like(owner)
    for axis, mask in steps:
        index = index * 2 + ((away[axis] // mask) & 1)
    return index * T_DEV + slot % T_DEV


def local(split, diag_block, panel, panel_count, pair_owner, pair_slot, ancestor):
    narrow_count = lax.axis_size("narrow")
    wide_count = lax.axis_size("wide")
    me = lax.axis_index("narrow")
    wide_me = lax.axis_index("wide")
    assert narrow_count == NB and diag_block.shape[0] == NB
    masks = range(1, NB)
    own = lambda x, m: lax.dynamic_index_in_dim(x, me ^ m, 0, keepdims=False)
    half_of = lambda x, m: lax.dynamic_slice(
        x, (me ^ m, (me // 2) * (W // 2), 0), (1, W // 2, B)
    ).reshape(W // 2, B)
    diag_in = [swap(own(diag_block, m) if m == 1 else half_of(diag_block, m), "narrow", m) for m in masks]
    diag_in[0], panel = lax.optimization_barrier((diag_in[0], panel))
    panel_in = [swap(own(panel, m), "narrow", m) for m in masks]

    narrow_steps = [("narrow", 1 << b) for b in range(log2(narrow_count))]
    wide_steps = [("wide", 1 << b) for b in range(log2(wide_count))]
    steps_a = narrow_steps[:1] + wide_steps + narrow_steps[1:]
    steps_b = narrow_steps[:1] + wide_steps[1:] + wide_steps[:1] + narrow_steps[1:]
    owner = lax.dynamic_slice_in_dim(pair_owner[:, 0], me * NPAIR, NPAIR)
    slot = lax.dynamic_slice_in_dim(pair_slot, me * NPAIR, NPAIR)
    tgt_a = relative_index(owner, slot, wide_me, me, steps_a)
    tgt_b = relative_index(owner, slot, wide_me, me, steps_b)
    info = jnp.stack([me, panel_count[me]]).astype(jnp.int32)

    slab = jax.ShapeDtypeStruct((W, B), jnp.float32)
    *l_parts, mt = pl.pallas_call(
        factor_kernel,
        out_shape=[slab] * NB + [jax.ShapeDtypeStruct((NB, W, B), jnp.float32)],
        in_specs=[SMEM] + [ANY] * NB,
        out_specs=[ANY] * (NB + 1),
        scratch_shapes=[pltpu.VMEM((NB, W, B), jnp.float32)] * 3 + [pltpu.SemaphoreType.DMA((NB + 1,))],
        compiler_params=pltpu.CompilerParams(vmem_limit_bytes=32 * 2**20),
        cost_estimate=pl.CostEstimate(flops=2 * 10**8, bytes_accessed=4 * 10**6, transcendentals=0),
        name="factor",
    )(info, diag_block, *diag_in)

    rows = P_SIZE * B
    blocks = wide_count * narrow_count * T_DEV
    slab = jax.ShapeDtypeStruct((rows, B), jnp.float32)
    part_a = jax.ShapeDtypeStruct((blocks // 2, split, B), jnp.float32)
    part_b = jax.ShapeDtypeStruct((blocks // 2, B - split, B), jnp.float32)
    *x_parts, keep_a, send_a, keep_b, send_b = pl.pallas_call(
        panel_kernel,
        out_shape=[slab] * NB + [part_a, part_a, part_b, part_b],
        in_specs=[SMEM] * 3 + [ANY] * (NB + 1),
        out_specs=[ANY] * (NB + 4),
        scratch_shapes=[
            pltpu.VMEM((NB, rows, B), jnp.float32),
            pltpu.VMEM((NB, rows, B), jnp.float32),
            pltpu.VMEM((NB, W, B), jnp.float32),
            pltpu.VMEM((rows, W), jnp.bfloat16),
            pltpu.VMEM((rows, W), jnp.bfloat16),
            pltpu.VMEM((blocks, split, B), jnp.float32),
            pltpu.VMEM((blocks, B - split, B), jnp.float32),
            pltpu.SemaphoreType.DMA((NB + 4,)),
        ],
        compiler_params=pltpu.CompilerParams(vmem_limit_bytes=52 * 2**20),
        cost_estimate=pl.CostEstimate(flops=10**9, bytes_accessed=10 * 10**6, transcendentals=0),
        name="panel",
    )(info, tgt_a, tgt_b, panel, *panel_in, mt)

    def reduce(keep, send, steps):
        for n, (axis, mask) in enumerate(steps):
            got = swap(send, axis, mask)
            if n + 1 < len(steps):
                half = keep.shape[0] // 2
                send = keep[half:] + got[half:]
                keep = keep[:half] + got[:half]
            else:
                keep = keep + got
        return keep

    sum_a = reduce(keep_a, send_a, steps_a)
    sum_b = reduce(keep_b, send_b, steps_b)
    updated = ancestor - jnp.concatenate([sum_a, sum_b], axis=1)

    def give_back(parts):
        back = [parts[0]] + [swap(parts[m], "narrow", m) for m in masks]
        out = jnp.zeros((NB,) + parts[0].shape, jnp.float32)
        for m in range(NB):
            out = lax.dynamic_update_index_in_dim(out, back[m], me ^ m, 0)
        return out

    return (give_back(l_parts), give_back(x_parts), updated)


def solution(mesh):
    placed = (
        P("wide", None, "narrow"),
        P("wide", None, "narrow"),
        P("wide"),
        P("wide", None),
        P("wide"),
        P(("wide", "narrow"), None, None),
    )
    return jax.shard_map(
        functools.partial(local, 72),
        mesh=mesh,
        in_specs=placed,
        out_specs=(
            P("wide", None, "narrow"),
            P("wide", None, "narrow"),
            P(("wide", "narrow"), None, None),
        ),
        check_vma=False,
    )
```

```python
import jax
import jax.numpy as jnp
import numpy as np
from jax import lax
from jax.experimental import pallas as pl
from jax.experimental.pallas import tpu as pltpu
from jax.sharding import PartitionSpec as P

W = 512
B = 128
P_SIZE = 8
T_DEV = 2
NB = W // B
NPAIR = P_SIZE * (P_SIZE + 1) // 2
HIGHEST = lax.Precision.HIGHEST


def dot_nt(a, b):
    return lax.dot_general(
        a, b, (((1,), (1,)), ((), ())), precision=HIGHEST, preferred_element_type=jnp.float32
    )


def dot_nn(a, b):
    return lax.dot_general(
        a, b, (((1,), (0,)), ((), ())), precision=HIGHEST, preferred_element_type=jnp.float32
    )


def lane_of(x, c):
    return jnp.broadcast_to(x[:, c : c + 1], x.shape)


def row_of(x, r):
    return jnp.broadcast_to(x[r : r + 1, :], x.shape)


def inverse_factor(block):
    sub = lax.broadcasted_iota(jnp.int32, (8, B), 0)
    lane = lax.broadcasted_iota(jnp.int32, (8, B), 1)
    total, strip = B // 8, 2
    rows = [block[8 * q : 8 * q + 8, :] for q in range(total)]
    done = [None] * total
    for b in range(0, total, strip):
        mine = range(b, b + strip)
        near = range(b + strip, min(b + 2 * strip, total))
        far = range(b + 2 * strip, total)
        in_strip = (lane >= 8 * b) & (lane < 8 * (b + strip))
        ahead = {q: [lane_of(rows[q], 8 * b + m) for m in range(8 * strip)] for q in near}
        for p in mine:
            lo = 8 * p
            own = (lane >= lo) & (lane < lo + 8)
            cols = [lane_of(rows[p], lo + m) for m in range(8)]
            others = [q for q in mine if q != p]
            mult = {q: [lane_of(rows[q], lo + m) for m in range(8)] for q in others}
            work = jnp.where(own, (lane - lo == sub).astype(jnp.float32), rows[p])
            final = jnp.zeros((8, B), jnp.float32)
            for k in range(0, 8, 2):
                f0, f1 = cols[k], cols[k + 1]
                a, h, c = row_of(f0, k), row_of(f0, k + 1), row_of(f1, k + 1)
                det = a * c - h * h
                recip = 1.0 / det
                ar, hr, cr = a * recip, h * recip, c * recip
                first, second = sub == k, sub == k + 1

                def eliminate(v):
                    r0, r1 = row_of(v, k), row_of(v, k + 1)
                    s0, s1 = cr * r0 - hr * r1, ar * r1 - hr * r0
                    return r0, r1, jnp.where(first, s0, jnp.where(second, s1, v - f0 * s0 - f1 * s1))

                for m in range(k + 2, 8):
                    cols[m] = eliminate(cols[m])[2]
                r0, r1, work = eliminate(work)
                root = lax.rsqrt(a)
                lower = (a * r1 - h * r0) * (root * lax.rsqrt(det))
                final = jnp.where(first, r0 * root, jnp.where(second, lower, final))
            done[p] = jnp.where(lane <= sub + lo, final, 0.0)
            rows[p] = work
            lines = [row_of(work, m) for m in range(8)]
            for q in others:
                new = jnp.where(own, 0.0, rows[q])
                for m in range(8):
                    new = new - mult[q][m] * lines[m]
                rows[q] = new
        lines = [row_of(rows[q], m) for q in mine for m in range(8)]
        for q in near:
            parts = [ahead[q][m] * lines[m] for m in range(4)]
            for m in range(4, 8 * strip):
                parts[m % 4] = parts[m % 4] + ahead[q][m] * lines[m]
            rows[q] = jnp.where(in_strip, 0.0, rows[q]) - ((parts[0] + parts[1]) + (parts[2] + parts[3]))
        if far:
            stack = jnp.concatenate([rows[q] for q in far], axis=0)
            lane_far = lax.broadcasted_iota(jnp.int32, stack.shape, 1)
            in_far = (lane_far >= 8 * b) & (lane_far < 8 * (b + strip))
            zero = jnp.zeros((8, B), jnp.float32)
            tall = jnp.concatenate([rows[q] if q in mine else zero for q in range(total)], axis=0)
            stack = jnp.where(in_far, 0.0, stack) - dot_nn(jnp.where(in_far, stack, 0.0), tall)
            for n, q in enumerate(far):
                rows[q] = stack[8 * n : 8 * n + 8]
    return jnp.concatenate(done, axis=0)


def split_bf16(v):
    high = v.astype(jnp.bfloat16)
    return high, (v - high.astype(jnp.float32)).astype(jnp.bfloat16)


def dot3(left, right, contract):
    dot = lambda a, b: lax.dot_general(
        a, b, (contract, ((), ())), preferred_element_type=jnp.float32
    )
    return dot(left[0], right[0]) + (dot(left[0], right[1]) + dot(left[1], right[0]))


def factor_kernel(info, own_ref, r1, r2, r3, l0, l1, l2, l3, inv_out, a, l, mt, sems):
    me = info[0]
    side = me // 2
    far_rows = pl.ds((1 - side) * (W // 2), W // 2)
    places = [a.at[me], a.at[me ^ 1], a.at[me ^ 2, far_rows], a.at[me ^ 3, far_rows]]
    ins = [own_ref.at[me], r1, r2, r3]
    copies = [pltpu.make_async_copy(ins[m], places[m], sems.at[m]) for m in range(NB)]
    for c in copies:
        c.start()
    for c in copies:
        c.wait()

    @pl.when(side == 1)
    def _():
        for j in range(NB // 2):
            for i in range(NB // 2, NB):
                a[j, pl.ds(i * B, B), :] = a[i, pl.ds(j * B, B), :].T

    row = lax.broadcasted_iota(jnp.int32, (B, B), 0)
    col = lax.broadcasted_iota(jnp.int32, (B, B), 1)
    l[...] = jnp.zeros_like(l)
    mt[...] = jnp.zeros_like(mt)
    eye = (row == col).astype(jnp.float32)
    for k in range(NB):
        here = pl.ds(k * B, B)
        inv = inverse_factor(a[k, here, :])
        l[k, here, :] = jnp.where(row >= col, dot_nt(a[k, here, :], inv), 0.0)
        for i in range(k + 1, NB):
            below = dot_nt(a[k, pl.ds(i * B, B), :], inv)
            l[k, pl.ds(i * B, B), :] = below
            for j in range(k + 1, i + 1):
                a[j, pl.ds(i * B, B), :] -= dot_nt(below, l[k, pl.ds(j * B, B), :])
        mt[k, here, :] = dot_nt(eye, inv)
        for i in range(k):
            total = dot_nt(mt[i, pl.ds(i * B, B), :], l[i, here, :])
            for j in range(i + 1, k):
                total = total + dot_nt(mt[j, pl.ds(i * B, B), :], l[j, here, :])
            mt[k, pl.ds(i * B, B), :] = dot_nt(-total, inv)
    outs = [l0, l1, l2, l3]
    copies = [pltpu.make_async_copy(l.at[me ^ m], outs[m], sems.at[m]) for m in range(NB)]
    copies.append(pltpu.make_async_copy(mt, inv_out, sems.at[NB]))
    for c in copies:
        c.start()
    for c in copies:
        c.wait()


def panel_kernel(info, tgt_a, tgt_b, own_ref, r1, r2, r3, mt_ref, *rest):
    (x0, x1, x2, x3, keep, send, p, x, mt, xh, xl, total, sems) = rest
    me = info[0]
    count = info[1]
    ins = [own_ref.at[me], r1, r2, r3]
    copies = [pltpu.make_async_copy(ins[m], p.at[me ^ m], sems.at[m]) for m in range(NB)]
    copies.append(pltpu.make_async_copy(mt_ref, mt, sems.at[NB]))
    for c in copies:
        c.start()
    total[...] = jnp.zeros_like(total)
    for c in copies:
        c.wait()
    rows = P_SIZE * B
    live = lax.broadcasted_iota(jnp.int32, (rows, B), 0) < count * B
    parts = [split_bf16(jnp.where(live, p[c], 0.0)) for c in range(NB)]
    for c in range(0, NB, 2):
        left = [jnp.concatenate([parts[j][n] for j in range(c + 2)], axis=1) for n in range(2)]
        right = split_bf16(
            jnp.concatenate([mt[c, pl.ds(0, (c + 2) * B), :], mt[c + 1, pl.ds(0, (c + 2) * B), :]], axis=1)
        )
        got = dot3(left, right, ((1,), (0,)))
        x[c] = got[:, :B]
        x[c + 1] = got[:, B:]
        high, low = split_bf16(got)
        xh[:, pl.ds(c * B, 2 * B)] = high
        xl[:, pl.ds(c * B, 2 * B)] = low

    outs = [x0, x1, x2, x3]
    copies = [pltpu.make_async_copy(x.at[me ^ m], outs[m], sems.at[m]) for m in range(NB)]
    for c in copies:
        c.start()
    strip = total.shape[2]
    for j in range(0, P_SIZE, 2):

        @pl.when(j < count)
        def _():
            left = (xh[pl.ds(j * B, rows - j * B), :], xl[pl.ds(j * B, rows - j * B), :])
            right = (xh[pl.ds(j * B, 2 * B), :], xl[pl.ds(j * B, 2 * B), :])
            got = dot3(left, right, ((1,), (1,)))
            for i in range(j, P_SIZE):
                for n in range(2 if i > j else 1):
                    block = got[(i - j) * B : (i - j + 1) * B, n * B : (n + 1) * B]
                    pair = i * (i + 1) // 2 + j + n
                    at_a = tgt_a[pair]
                    at_b = tgt_b[pair]
                    total[0, at_a] += block[:strip]
                    total[1, at_b] += block[strip:]

    half = total.shape[1] // 2
    more = []
    for n in range(2):
        at = NB + 2 * n
        more.append(pltpu.make_async_copy(total.at[n, pl.ds(half, half)], send.at[n], sems.at[at]))
        more.append(pltpu.make_async_copy(total.at[n, pl.ds(0, half)], keep.at[n], sems.at[at + 1]))
    for c in more:
        c.start()
    for c in copies + more:
        c.wait()


SMEM = pl.BlockSpec(memory_space=pltpu.SMEM)
ANY = pl.BlockSpec(memory_space=pl.ANY)


def xor_pairs(size, mask):
    return [(i, i ^ mask) for i in range(size)]


def log2(n):
    return n.bit_length() - 1


def swap(x, axis, mask):
    return lax.ppermute(x, axis, xor_pairs(lax.axis_size(axis), mask))


def relative_index(owner, slot, wide_me, narrow_me, steps):
    away = {"wide": owner ^ wide_me, "narrow": (slot // T_DEV) ^ narrow_me}
    index = jnp.zeros_like(owner)
    for axis, mask in steps:
        index = index * 2 + ((away[axis] // mask) & 1)
    return index * T_DEV + slot % T_DEV


def local(diag_block, panel, panel_count, pair_owner, pair_slot, ancestor):
    narrow_count = lax.axis_size("narrow")
    wide_count = lax.axis_size("wide")
    me = lax.axis_index("narrow")
    wide_me = lax.axis_index("wide")
    assert narrow_count == NB and diag_block.shape[0] == NB
    masks = range(1, NB)
    own = lambda x, m: lax.dynamic_index_in_dim(x, me ^ m, 0, keepdims=False)
    half_of = lambda x, m: lax.dynamic_slice(
        x, (me ^ m, (me // 2) * (W // 2), 0), (1, W // 2, B)
    ).reshape(W // 2, B)
    diag_in = [swap(own(diag_block, m) if m == 1 else half_of(diag_block, m), "narrow", m) for m in masks]
    panel_out = [own(panel, m) for m in masks]
    diag_in, panel_out = lax.optimization_barrier((diag_in, panel_out))
    panel_in = [swap(panel_out[m - 1], "narrow", m) for m in masks]

    narrow_steps = [("narrow", 1 << b) for b in range(log2(narrow_count))]
    wide_steps = [("wide", 1 << b) for b in range(log2(wide_count))]
    first, last = narrow_steps[:1], wide_steps[2:] + narrow_steps[1:]
    steps_a = first + wide_steps[:2] + last
    steps_b = first + wide_steps[1::-1] + last
    owner = lax.dynamic_slice_in_dim(pair_owner[:, 0], me * NPAIR, NPAIR)
    slot = lax.dynamic_slice_in_dim(pair_slot, me * NPAIR, NPAIR)
    tgt_a = relative_index(owner, slot, wide_me, me, steps_a)
    tgt_b = relative_index(owner, slot, wide_me, me, steps_b)
    info = jnp.stack([me, panel_count[me]]).astype(jnp.int32)

    slab = jax.ShapeDtypeStruct((W, B), jnp.float32)
    *l_parts, mt = pl.pallas_call(
        factor_kernel,
        out_shape=[slab] * NB + [jax.ShapeDtypeStruct((NB, W, B), jnp.float32)],
        in_specs=[SMEM] + [ANY] * NB,
        out_specs=[ANY] * (NB + 1),
        scratch_shapes=[pltpu.VMEM((NB, W, B), jnp.float32)] * 3 + [pltpu.SemaphoreType.DMA((NB + 1,))],
        compiler_params=pltpu.CompilerParams(vmem_limit_bytes=32 * 2**20),
        cost_estimate=pl.CostEstimate(flops=2 * 10**8, bytes_accessed=4 * 10**6, transcendentals=0),
        name="factor",
    )(info, diag_block, *diag_in)

    rows = P_SIZE * B
    blocks = wide_count * narrow_count * T_DEV
    slab = jax.ShapeDtypeStruct((rows, B), jnp.float32)
    part = jax.ShapeDtypeStruct((2, blocks // 2, B // 2, B), jnp.float32)
    *x_parts, keep, send = pl.pallas_call(
        panel_kernel,
        out_shape=[slab] * NB + [part, part],
        in_specs=[SMEM] * 3 + [ANY] * (NB + 1),
        out_specs=[ANY] * (NB + 2),
        scratch_shapes=[
            pltpu.VMEM((NB, rows, B), jnp.float32),
            pltpu.VMEM((NB, rows, B), jnp.float32),
            pltpu.VMEM((NB, W, B), jnp.float32),
            pltpu.VMEM((rows, W), jnp.bfloat16),
            pltpu.VMEM((rows, W), jnp.bfloat16),
            pltpu.VMEM((2, blocks, B // 2, B), jnp.float32),
            pltpu.SemaphoreType.DMA((NB + 4,)),
        ],
        compiler_params=pltpu.CompilerParams(vmem_limit_bytes=52 * 2**20),
        cost_estimate=pl.CostEstimate(flops=10**9, bytes_accessed=10 * 10**6, transcendentals=0),
        name="panel",
    )(info, tgt_a, tgt_b, panel, *panel_in, mt)

    l_back = [swap(l_parts[m], "narrow", m) for m in masks]
    x_back = [swap(x_parts[m], "narrow", m) for m in masks]

    got = swap(send, "narrow", 1)
    half = blocks // 4
    upper = lambda u, n: u[n, half:]
    lower = lambda u, n: u[n, :half]
    send_a = upper(keep, 0) + upper(got, 0)
    send_b = upper(keep, 1) + upper(got, 1)
    keep_a = lower(keep, 0) + lower(got, 0)
    keep_b = lower(keep, 1) + lower(got, 1)
    for n in (1, 2):
        if n == 2:
            send_a, send_b, l_back[1], l_back[2] = lax.optimization_barrier(
                (send_a, send_b, l_back[1], l_back[2])
            )
        else:
            send_a, send_b = lax.optimization_barrier((send_a, send_b))
        got_a = swap(send_a, *steps_a[n])
        got_b = swap(send_b, *steps_b[n])
        half = half // 2
        send_a, send_b = keep_a[half:] + got_a[half:], keep_b[half:] + got_b[half:]
        keep_a, keep_b = keep_a[:half] + got_a[:half], keep_b[:half] + got_b[:half]
    send = jnp.stack([send_a, send_b], axis=1)
    keep = jnp.stack([keep_a, keep_b], axis=1)
    for n in range(3, len(steps_a)):
        if n == 3:
            send, x_back[1] = lax.optimization_barrier((send, x_back[1]))
        if n == len(steps_a) - 1:
            send, x_back[2], x_back[0] = lax.optimization_barrier((send, x_back[2], x_back[0]))
        got = swap(send, *steps_a[n])
        if n + 1 < len(steps_a):
            half = half // 2
            send = keep[half:] + got[half:]
            keep = keep[:half] + got[:half]
    updated = ancestor - (keep + got).reshape(ancestor.shape)

    def give_back(own_part, others):
        back = [own_part] + others
        out = jnp.zeros((NB,) + own_part.shape, jnp.float32)
        for m in range(NB):
            out = lax.dynamic_update_index_in_dim(out, back[m], me ^ m, 0)
        return out

    return (give_back(l_parts[0], l_back), give_back(x_parts[0], x_back), updated)


def solution(mesh):
    placed = (
        P("wide", None, "narrow"),
        P("wide", None, "narrow"),
        P("wide"),
        P("wide", None),
        P("wide"),
        P(("wide", "narrow"), None, None),
    )
    return jax.shard_map(
        local,
        mesh=mesh,
        in_specs=placed,
        out_specs=(
            P("wide", None, "narrow"),
            P("wide", None, "narrow"),
            P(("wide", "narrow"), None, None),
        ),
        check_vma=False,
    )
```

```python
import jax
import jax.numpy as jnp
import numpy as np
from jax import lax
from jax.experimental import pallas as pl
from jax.experimental.pallas import tpu as pltpu
from jax.sharding import PartitionSpec as P

W = 512
B = 128
P_SIZE = 8
T_DEV = 2
NB = W // B
NPAIR = P_SIZE * (P_SIZE + 1) // 2
HIGHEST = lax.Precision.HIGHEST


def dot_nt(a, b):
    return lax.dot_general(
        a, b, (((1,), (1,)), ((), ())), precision=HIGHEST, preferred_element_type=jnp.float32
    )


def dot_nn(a, b):
    return lax.dot_general(
        a, b, (((1,), (0,)), ((), ())), precision=HIGHEST, preferred_element_type=jnp.float32
    )


def lane_of(x, c):
    return jnp.broadcast_to(x[:, c : c + 1], x.shape)


def row_of(x, r):
    return jnp.broadcast_to(x[r : r + 1, :], x.shape)


def inverse_factor(block):
    sub = lax.broadcasted_iota(jnp.int32, (8, B), 0)
    lane = lax.broadcasted_iota(jnp.int32, (8, B), 1)
    total, strip = B // 8, 2
    rows = [block[8 * q : 8 * q + 8, :] for q in range(total)]
    done = [None] * total
    for b in range(0, total, strip):
        mine = range(b, b + strip)
        near = range(b + strip, min(b + 2 * strip, total))
        far = range(b + 2 * strip, total)
        in_strip = (lane >= 8 * b) & (lane < 8 * (b + strip))
        ahead = {q: [lane_of(rows[q], 8 * b + m) for m in range(8 * strip)] for q in near}
        for p in mine:
            lo = 8 * p
            own = (lane >= lo) & (lane < lo + 8)
            cols = [lane_of(rows[p], lo + m) for m in range(8)]
            others = [q for q in mine if q != p]
            mult = {q: [lane_of(rows[q], lo + m) for m in range(8)] for q in others}
            work = jnp.where(own, (lane - lo == sub).astype(jnp.float32), rows[p])
            final = jnp.zeros((8, B), jnp.float32)
            for k in range(0, 8, 2):
                f0, f1 = cols[k], cols[k + 1]
                a, h, c = row_of(f0, k), row_of(f0, k + 1), row_of(f1, k + 1)
                det = a * c - h * h
                recip = 1.0 / det
                ar, hr, cr = a * recip, h * recip, c * recip
                first, second = sub == k, sub == k + 1

                def eliminate(v):
                    r0, r1 = row_of(v, k), row_of(v, k + 1)
                    s0, s1 = cr * r0 - hr * r1, ar * r1 - hr * r0
                    return r0, r1, jnp.where(first, s0, jnp.where(second, s1, v - f0 * s0 - f1 * s1))

                for m in range(k + 2, 8):
                    cols[m] = eliminate(cols[m])[2]
                r0, r1, work = eliminate(work)
                root = lax.rsqrt(a)
                lower = (a * r1 - h * r0) * (root * lax.rsqrt(det))
                final = jnp.where(first, r0 * root, jnp.where(second, lower, final))
            done[p] = jnp.where(lane <= sub + lo, final, 0.0)
            rows[p] = work
            lines = [row_of(work, m) for m in range(8)]
            for q in others:
                new = jnp.where(own, 0.0, rows[q])
                for m in range(8):
                    new = new - mult[q][m] * lines[m]
                rows[q] = new
        lines = [row_of(rows[q], m) for q in mine for m in range(8)]
        for q in near:
            parts = [ahead[q][m] * lines[m] for m in range(4)]
            for m in range(4, 8 * strip):
                parts[m % 4] = parts[m % 4] + ahead[q][m] * lines[m]
            rows[q] = jnp.where(in_strip, 0.0, rows[q]) - ((parts[0] + parts[1]) + (parts[2] + parts[3]))
        if far:
            stack = jnp.concatenate([rows[q] for q in far], axis=0)
            lane_far = lax.broadcasted_iota(jnp.int32, stack.shape, 1)
            in_far = (lane_far >= 8 * b) & (lane_far < 8 * (b + strip))
            zero = jnp.zeros((8, B), jnp.float32)
            tall = jnp.concatenate([rows[q] if q in mine else zero for q in range(total)], axis=0)
            stack = jnp.where(in_far, 0.0, stack) - dot_nn(jnp.where(in_far, stack, 0.0), tall)
            for n, q in enumerate(far):
                rows[q] = stack[8 * n : 8 * n + 8]
    return jnp.concatenate(done, axis=0)


def split_bf16(v):
    high = v.astype(jnp.bfloat16)
    return high, (v - high.astype(jnp.float32)).astype(jnp.bfloat16)


def dot3(left, right, contract):
    dot = lambda a, b: lax.dot_general(
        a, b, (contract, ((), ())), preferred_element_type=jnp.float32
    )
    return dot(left[0], right[0]) + (dot(left[0], right[1]) + dot(left[1], right[0]))


def factor_kernel(info, own_ref, r1, r2, r3, l0, l1, l2, l3, mt, a, l, sems):
    me = info[0]
    side = me // 2
    far_rows = pl.ds((1 - side) * (W // 2), W // 2)
    places = [a.at[me], a.at[me ^ 1], a.at[me ^ 2, far_rows], a.at[me ^ 3, far_rows]]
    ins = [own_ref.at[me], r1, r2, r3]
    copies = [pltpu.make_async_copy(ins[m], places[m], sems.at[m]) for m in range(NB)]
    for c in copies:
        c.start()
    for c in copies:
        c.wait()

    @pl.when(side == 1)
    def _():
        for j in range(NB // 2):
            for i in range(NB // 2, NB):
                a[j, pl.ds(i * B, B), :] = a[i, pl.ds(j * B, B), :].T

    row = lax.broadcasted_iota(jnp.int32, (B, B), 0)
    col = lax.broadcasted_iota(jnp.int32, (B, B), 1)
    l[...] = jnp.zeros_like(l)
    mt[...] = jnp.zeros_like(mt)
    eye = (row == col).astype(jnp.float32)
    for k in range(NB):
        here = pl.ds(k * B, B)
        inv = inverse_factor(a[k, here, :])
        l[k, here, :] = jnp.where(row >= col, dot_nt(a[k, here, :], inv), 0.0)
        for i in range(k + 1, NB):
            below = dot_nt(a[k, pl.ds(i * B, B), :], inv)
            l[k, pl.ds(i * B, B), :] = below
            for j in range(k + 1, i + 1):
                a[j, pl.ds(i * B, B), :] -= dot_nt(below, l[k, pl.ds(j * B, B), :])
        mt[k, here, :] = dot_nt(eye, inv)
        for i in range(k):
            total = dot_nt(mt[i, pl.ds(i * B, B), :], l[i, here, :])
            for j in range(i + 1, k):
                total = total + dot_nt(mt[j, pl.ds(i * B, B), :], l[j, here, :])
            mt[k, pl.ds(i * B, B), :] = dot_nt(-total, inv)
    outs = [l0, l1, l2, l3]
    copies = [pltpu.make_async_copy(l.at[me ^ m], outs[m], sems.at[m]) for m in range(NB)]
    for c in copies:
        c.start()
    for c in copies:
        c.wait()


def panel_kernel(info, counts, tgt_a, tgt_b, own_ref, r1, r2, r3, mt, x0, x1, x2, x3, keep, send, xh, xl):
    me = info[0]
    count = counts[me]
    rows = P_SIZE * B
    ins = [own_ref.at[me], r1, r2, r3]
    outs = [x0, x1, x2, x3]
    live = lax.broadcasted_iota(jnp.int32, (rows, B), 0) < count * B
    parts = [split_bf16(jnp.where(live, ref[...], 0.0)) for ref in ins]
    left = [jnp.concatenate([part[n] for part in parts], axis=1) for n in range(2)]
    for c in range(0, NB, 2):
        right = [
            jnp.concatenate([mt[me ^ m, pl.ds((me ^ k) * B, B), :] for m in (c, c + 1)], axis=1)
            for k in range(NB)
        ]
        got = dot3(left, split_bf16(jnp.concatenate(right, axis=0)), ((1,), (0,)))
        outs[c][...] = got[:, :B]
        outs[c + 1][...] = got[:, B:]
        high, low = split_bf16(got)
        xh[:, pl.ds(c * B, 2 * B)] = high
        xl[:, pl.ds(c * B, 2 * B)] = low

    keep[...] = jnp.zeros_like(keep)
    send[...] = jnp.zeros_like(send)
    half, strip = keep.shape[1:3]
    for j in range(0, P_SIZE, 2):

        @pl.when(j < count)
        def _():
            left = (xh[pl.ds(j * B, rows - j * B), :], xl[pl.ds(j * B, rows - j * B), :])
            right = (xh[pl.ds(j * B, 2 * B), :], xl[pl.ds(j * B, 2 * B), :])
            got = dot3(left, right, ((1,), (1,)))
            for i in range(j, P_SIZE):
                for n in range(2 if i > j else 1):
                    block = got[(i - j) * B : (i - j + 1) * B, n * B : (n + 1) * B]
                    pair = i * (i + 1) // 2 + j + n
                    away = (tgt_a[pair] >= half).astype(jnp.float32)
                    for stream, tgt in enumerate((tgt_a, tgt_b)):
                        at = lax.rem(tgt[pair], half)
                        piece = block[stream * strip : (stream + 1) * strip]
                        keep[stream, at] += piece * (1.0 - away)
                        send[stream, at] += piece * away


SMEM = pl.BlockSpec(memory_space=pltpu.SMEM)
ANY = pl.BlockSpec(memory_space=pl.ANY)
VMEM = pl.BlockSpec(memory_space=pltpu.VMEM)


def xor_pairs(size, mask):
    return [(i, i ^ mask) for i in range(size)]


def log2(n):
    return n.bit_length() - 1


def swap(x, axis, mask):
    return lax.ppermute(x, axis, xor_pairs(lax.axis_size(axis), mask))


def relative_index(owner, slot, wide_me, narrow_me, steps):
    away = {"wide": owner ^ wide_me, "narrow": (slot // T_DEV) ^ narrow_me}
    index = jnp.zeros_like(owner)
    for axis, mask in steps:
        index = index * 2 + ((away[axis] // mask) & 1)
    return index * T_DEV + slot % T_DEV


def local(diag_block, panel, panel_count, pair_owner, pair_slot, ancestor):
    narrow_count = lax.axis_size("narrow")
    wide_count = lax.axis_size("wide")
    me = lax.axis_index("narrow")
    wide_me = lax.axis_index("wide")
    assert narrow_count == NB and diag_block.shape[0] == NB
    masks = range(1, NB)
    own = lambda x, m: lax.dynamic_index_in_dim(x, me ^ m, 0, keepdims=False)
    half_of = lambda x, m: lax.dynamic_slice(
        x, (me ^ m, (me // 2) * (W // 2), 0), (1, W // 2, B)
    ).reshape(W // 2, B)
    diag_in = [swap(own(diag_block, m) if m == 1 else half_of(diag_block, m), "narrow", m) for m in masks]
    panel_out = [own(panel, m) for m in masks]
    diag_in, panel_out = lax.optimization_barrier((diag_in, panel_out))
    panel_in = [swap(panel_out[m - 1], "narrow", m) for m in masks]

    narrow_steps = [("narrow", 1 << b) for b in range(log2(narrow_count))]
    wide_steps = [("wide", 1 << b) for b in range(log2(wide_count))]
    first, last = narrow_steps[:1], wide_steps[2:] + narrow_steps[1:]
    steps_a = first + wide_steps[:2] + last
    steps_b = first + wide_steps[1::-1] + last
    owner = lax.dynamic_slice_in_dim(pair_owner[:, 0], me * NPAIR, NPAIR)
    slot = lax.dynamic_slice_in_dim(pair_slot, me * NPAIR, NPAIR)
    tgt_a = relative_index(owner, slot, wide_me, me, steps_a)
    tgt_b = relative_index(owner, slot, wide_me, me, steps_b)
    info = me.astype(jnp.int32).reshape(1)

    slab = jax.ShapeDtypeStruct((W, B), jnp.float32)
    *l_parts, mt = pl.pallas_call(
        factor_kernel,
        out_shape=[slab] * NB + [jax.ShapeDtypeStruct((NB, W, B), jnp.float32)],
        in_specs=[SMEM] + [ANY] * NB,
        out_specs=[ANY] * NB + [VMEM],
        scratch_shapes=[pltpu.VMEM((NB, W, B), jnp.float32)] * 2 + [pltpu.SemaphoreType.DMA((NB,))],
        compiler_params=pltpu.CompilerParams(vmem_limit_bytes=32 * 2**20),
        cost_estimate=pl.CostEstimate(flops=2 * 10**8, bytes_accessed=4 * 10**6, transcendentals=0),
        name="factor",
    )(info, diag_block, *diag_in)

    rows = P_SIZE * B
    blocks = wide_count * narrow_count * T_DEV
    slab = jax.ShapeDtypeStruct((rows, B), jnp.float32)
    part = jax.ShapeDtypeStruct((2, blocks // 2, B // 2, B), jnp.float32)
    *x_parts, keep, send = pl.pallas_call(
        panel_kernel,
        out_shape=[slab] * NB + [part, part],
        in_specs=[SMEM] * 4 + [VMEM] * (NB + 1),
        out_specs=[VMEM] * (NB + 2),
        scratch_shapes=[pltpu.VMEM((rows, W), jnp.bfloat16)] * 2,
        compiler_params=pltpu.CompilerParams(vmem_limit_bytes=52 * 2**20),
        cost_estimate=pl.CostEstimate(flops=10**9, bytes_accessed=10 * 10**6, transcendentals=0),
        name="panel",
    )(info, panel_count, tgt_a, tgt_b, panel, *panel_in, mt)

    l_back = [swap(l_parts[m], "narrow", m) for m in masks]
    x_back = [swap(x_parts[m], "narrow", m) for m in masks]

    got = swap(send, "narrow", 1)
    half = blocks // 4
    upper = lambda u, n: u[n, half:]
    lower = lambda u, n: u[n, :half]
    send_a = upper(keep, 0) + upper(got, 0)
    send_b = upper(keep, 1) + upper(got, 1)
    keep_a = lower(keep, 0) + lower(got, 0)
    keep_b = lower(keep, 1) + lower(got, 1)
    for n in (1, 2):
        if n == 2:
            send_a, send_b, x_back[1] = lax.optimization_barrier((send_a, send_b, x_back[1]))
        else:
            send_a, send_b = lax.optimization_barrier((send_a, send_b))
        got_a = swap(send_a, *steps_a[n])
        got_b = swap(send_b, *steps_b[n])
        half = half // 2
        send_a, send_b = keep_a[half:] + got_a[half:], keep_b[half:] + got_b[half:]
        keep_a, keep_b = keep_a[:half] + got_a[:half], keep_b[:half] + got_b[:half]
    send = jnp.stack([send_a, send_b], axis=1)
    keep = jnp.stack([keep_a, keep_b], axis=1)
    for n in range(3, len(steps_a)):
        if n == 3:
            send, l_back[1] = lax.optimization_barrier((send, l_back[1]))
        if n == len(steps_a) - 1:
            send, x_back[2], x_back[0] = lax.optimization_barrier((send, x_back[2], x_back[0]))
        got = swap(send, *steps_a[n])
        if n + 1 < len(steps_a):
            half = half // 2
            send = keep[half:] + got[half:]
            keep = keep[:half] + got[:half]
    updated = ancestor - (keep + got).reshape(ancestor.shape)

    def give_back(own_part, others):
        back = [own_part] + others
        out = jnp.zeros((NB,) + own_part.shape, jnp.float32)
        for m in range(NB):
            out = lax.dynamic_update_index_in_dim(out, back[m], me ^ m, 0)
        return out

    return (give_back(l_parts[0], l_back), give_back(x_parts[0], x_back), updated)


def solution(mesh):
    placed = (
        P("wide", None, "narrow"),
        P("wide", None, "narrow"),
        P("wide"),
        P("wide", None),
        P("wide"),
        P(("wide", "narrow"), None, None),
    )
    return jax.shard_map(
        local,
        mesh=mesh,
        in_specs=placed,
        out_specs=(
            P("wide", None, "narrow"),
            P("wide", None, "narrow"),
            P(("wide", "narrow"), None, None),
        ),
        check_vma=False,
    )
```

```python
import jax
import jax.numpy as jnp
import numpy as np
from jax import lax
from jax.experimental import pallas as pl
from jax.experimental.pallas import tpu as pltpu
from jax.sharding import PartitionSpec as P

W = 512
B = 128
P_SIZE = 8
T_DEV = 2
NB = W // B
NPAIR = P_SIZE * (P_SIZE + 1) // 2
HIGHEST = lax.Precision.HIGHEST


def dot_nt(a, b):
    return lax.dot_general(
        a, b, (((1,), (1,)), ((), ())), precision=HIGHEST, preferred_element_type=jnp.float32
    )


def dot_nn(a, b):
    return lax.dot_general(
        a, b, (((1,), (0,)), ((), ())), precision=HIGHEST, preferred_element_type=jnp.float32
    )


def lane_of(x, c):
    return jnp.broadcast_to(x[:, c : c + 1], x.shape)


def row_of(x, r):
    return jnp.broadcast_to(x[r : r + 1, :], x.shape)


def inverse_factor(block):
    sub = lax.broadcasted_iota(jnp.int32, (8, B), 0)
    lane = lax.broadcasted_iota(jnp.int32, (8, B), 1)
    total, strip = B // 8, 2
    rows = [block[8 * q : 8 * q + 8, :] for q in range(total)]
    done = [None] * total
    for b in range(0, total, strip):
        mine = range(b, b + strip)
        near = range(b + strip, min(b + 2 * strip, total))
        far = range(b + 2 * strip, total)
        in_strip = (lane >= 8 * b) & (lane < 8 * (b + strip))
        ahead = {q: [lane_of(rows[q], 8 * b + m) for m in range(8 * strip)] for q in near}
        for p in mine:
            lo = 8 * p
            own = (lane >= lo) & (lane < lo + 8)
            cols = [lane_of(rows[p], lo + m) for m in range(8)]
            others = [q for q in mine if q != p]
            mult = {q: [lane_of(rows[q], lo + m) for m in range(8)] for q in others}
            work = jnp.where(own, (lane - lo == sub).astype(jnp.float32), rows[p])
            final = jnp.zeros((8, B), jnp.float32)
            for k in range(0, 8, 2):
                f0, f1 = cols[k], cols[k + 1]
                a, h, c = row_of(f0, k), row_of(f0, k + 1), row_of(f1, k + 1)
                det = a * c - h * h
                recip = 1.0 / det
                ar, hr, cr = a * recip, h * recip, c * recip
                first, second = sub == k, sub == k + 1

                def eliminate(v):
                    r0, r1 = row_of(v, k), row_of(v, k + 1)
                    s0, s1 = cr * r0 - hr * r1, ar * r1 - hr * r0
                    return r0, r1, jnp.where(first, s0, jnp.where(second, s1, v - f0 * s0 - f1 * s1))

                for m in range(k + 2, 8):
                    cols[m] = eliminate(cols[m])[2]
                r0, r1, work = eliminate(work)
                root = lax.rsqrt(a)
                lower = (a * r1 - h * r0) * (root * lax.rsqrt(det))
                final = jnp.where(first, r0 * root, jnp.where(second, lower, final))
            done[p] = jnp.where(lane <= sub + lo, final, 0.0)
            rows[p] = work
            lines = [row_of(work, m) for m in range(8)]
            for q in others:
                new = jnp.where(own, 0.0, rows[q])
                for m in range(8):
                    new = new - mult[q][m] * lines[m]
                rows[q] = new
        lines = [row_of(rows[q], m) for q in mine for m in range(8)]
        for q in near:
            parts = [ahead[q][m] * lines[m] for m in range(4)]
            for m in range(4, 8 * strip):
                parts[m % 4] = parts[m % 4] + ahead[q][m] * lines[m]
            rows[q] = jnp.where(in_strip, 0.0, rows[q]) - ((parts[0] + parts[1]) + (parts[2] + parts[3]))
        if far:
            stack = jnp.concatenate([rows[q] for q in far], axis=0)
            lane_far = lax.broadcasted_iota(jnp.int32, stack.shape, 1)
            in_far = (lane_far >= 8 * b) & (lane_far < 8 * (b + strip))
            zero = jnp.zeros((8, B), jnp.float32)
            tall = jnp.concatenate([rows[q] if q in mine else zero for q in range(total)], axis=0)
            stack = jnp.where(in_far, 0.0, stack) - dot_nn(jnp.where(in_far, stack, 0.0), tall)
            for n, q in enumerate(far):
                rows[q] = stack[8 * n : 8 * n + 8]
    return jnp.concatenate(done, axis=0)


def split_bf16(v):
    high = v.astype(jnp.bfloat16)
    return high, (v - high.astype(jnp.float32)).astype(jnp.bfloat16)


def dot3(left, right, contract):
    dot = lambda a, b: lax.dot_general(
        a, b, (contract, ((), ())), preferred_element_type=jnp.float32
    )
    return dot(left[0], right[0]) + (dot(left[0], right[1]) + dot(left[1], right[0]))


def factor_kernel(info, own_ref, r1, r2, r3, l, mt, a, sems):
    me = info[0]
    side = me // 2
    far_rows = pl.ds((1 - side) * (W // 2), W // 2)
    places = [a.at[me], a.at[me ^ 1], a.at[me ^ 2, far_rows], a.at[me ^ 3, far_rows]]
    ins = [own_ref.at[me], r1, r2, r3]
    copies = [pltpu.make_async_copy(ins[m], places[m], sems.at[m]) for m in range(NB)]
    for c in copies:
        c.start()
    for c in copies:
        c.wait()

    @pl.when(side == 1)
    def _():
        for j in range(NB // 2):
            for i in range(NB // 2, NB):
                a[j, pl.ds(i * B, B), :] = a[i, pl.ds(j * B, B), :].T

    row = lax.broadcasted_iota(jnp.int32, (B, B), 0)
    col = lax.broadcasted_iota(jnp.int32, (B, B), 1)
    l[...] = jnp.zeros_like(l)
    mt[...] = jnp.zeros_like(mt)
    eye = (row == col).astype(jnp.float32)
    for k in range(NB):
        here = pl.ds(k * B, B)
        inv = inverse_factor(a[k, here, :])
        l[k, here, :] = jnp.where(row >= col, dot_nt(a[k, here, :], inv), 0.0)
        for i in range(k + 1, NB):
            below = dot_nt(a[k, pl.ds(i * B, B), :], inv)
            l[k, pl.ds(i * B, B), :] = below
            for j in range(k + 1, i + 1):
                a[j, pl.ds(i * B, B), :] -= dot_nt(below, l[k, pl.ds(j * B, B), :])
        mt[k, here, :] = dot_nt(eye, inv)
        for i in range(k):
            total = dot_nt(mt[i, pl.ds(i * B, B), :], l[i, here, :])
            for j in range(i + 1, k):
                total = total + dot_nt(mt[j, pl.ds(i * B, B), :], l[j, here, :])
            mt[k, pl.ds(i * B, B), :] = dot_nt(-total, inv)


def panel_kernel(
    info, counts, tgt_a, tgt_b, own_ref, r1, r2, r3, mt, l, own, near, far, keep, send_a, send_b, xh, xl
):
    me = info[0]
    count = counts[me]
    rows = P_SIZE * B
    ins = [own_ref.at[me], r1, r2, r3]
    outs = [own, near, far.at[0], far.at[1]]
    for m in range(NB):
        outs[m][pl.ds(rows, W), :] = l[me ^ m]
    live = lax.broadcasted_iota(jnp.int32, (rows, B), 0) < count * B
    parts = [split_bf16(jnp.where(live, ref[...], 0.0)) for ref in ins]
    left = [jnp.concatenate([part[n] for part in parts], axis=1) for n in range(2)]
    for c in range(0, NB, 2):
        right = [
            jnp.concatenate([mt[me ^ m, pl.ds((me ^ k) * B, B), :] for m in (c, c + 1)], axis=1)
            for k in range(NB)
        ]
        got = dot3(left, split_bf16(jnp.concatenate(right, axis=0)), ((1,), (0,)))
        outs[c][pl.ds(0, rows), :] = got[:, :B]
        outs[c + 1][pl.ds(0, rows), :] = got[:, B:]
        high, low = split_bf16(got)
        xh[:, pl.ds(c * B, 2 * B)] = high
        xl[:, pl.ds(c * B, 2 * B)] = low

    keep[...] = jnp.zeros_like(keep)
    send_a[...] = jnp.zeros_like(send_a)
    send_b[...] = jnp.zeros_like(send_b)
    half, strip = keep.shape[1:3]
    for j in range(0, P_SIZE, 2):

        @pl.when(j < count)
        def _():
            left = (xh[pl.ds(j * B, rows - j * B), :], xl[pl.ds(j * B, rows - j * B), :])
            right = (xh[pl.ds(j * B, 2 * B), :], xl[pl.ds(j * B, 2 * B), :])
            got = dot3(left, right, ((1,), (1,)))
            for i in range(j, P_SIZE):
                for n in range(2 if i > j else 1):
                    block = got[(i - j) * B : (i - j + 1) * B, n * B : (n + 1) * B]
                    pair = i * (i + 1) // 2 + j + n
                    away = (tgt_a[pair] >= half).astype(jnp.float32)
                    for stream, (tgt, send) in enumerate(((tgt_a, send_a), (tgt_b, send_b))):
                        at = lax.rem(tgt[pair], half)
                        piece = block[stream * strip : (stream + 1) * strip]
                        keep[stream, at] += piece * (1.0 - away)
                        send[at] += piece * away


SMEM = pl.BlockSpec(memory_space=pltpu.SMEM)
ANY = pl.BlockSpec(memory_space=pl.ANY)
VMEM = pl.BlockSpec(memory_space=pltpu.VMEM)


def xor_pairs(size, mask):
    return [(i, i ^ mask) for i in range(size)]


def log2(n):
    return n.bit_length() - 1


def swap(x, axis, mask):
    return lax.ppermute(x, axis, xor_pairs(lax.axis_size(axis), mask))


def relative_index(owner, slot, wide_me, narrow_me, steps):
    away = {"wide": owner ^ wide_me, "narrow": (slot // T_DEV) ^ narrow_me}
    index = jnp.zeros_like(owner)
    for axis, mask in steps:
        index = index * 2 + ((away[axis] // mask) & 1)
    return index * T_DEV + slot % T_DEV


def local(diag_block, panel, panel_count, pair_owner, pair_slot, ancestor):
    narrow_count = lax.axis_size("narrow")
    wide_count = lax.axis_size("wide")
    me = lax.axis_index("narrow")
    wide_me = lax.axis_index("wide")
    assert narrow_count == NB and diag_block.shape[0] == NB
    masks = range(1, NB)
    own = lambda x, m: lax.dynamic_index_in_dim(x, me ^ m, 0, keepdims=False)
    half_of = lambda x, m: lax.dynamic_slice(
        x, (me ^ m, (me // 2) * (W // 2), 0), (1, W // 2, B)
    ).reshape(W // 2, B)
    halves = [half_of(diag_block, m) for m in masks[1:]]
    halves, near_block = lax.optimization_barrier((halves, diag_block))
    diag_in = [swap(own(near_block, 1), "narrow", 1)]
    diag_in += [swap(part, "narrow", m) for m, part in zip(masks[1:], halves)]
    panel_out = [own(panel, m) for m in masks]
    diag_in, panel_out = lax.optimization_barrier((diag_in, panel_out))
    panel_in = [swap(panel_out[m - 1], "narrow", m) for m in masks]

    narrow_steps = [("narrow", 1 << b) for b in range(log2(narrow_count))]
    wide_steps = [("wide", 1 << b) for b in range(log2(wide_count))]
    first, last = narrow_steps[:1], wide_steps[2:] + narrow_steps[1:]
    steps_a = first + wide_steps[:2] + last
    steps_b = first + wide_steps[1::-1] + last
    owner = lax.dynamic_slice_in_dim(pair_owner[:, 0], me * NPAIR, NPAIR)
    slot = lax.dynamic_slice_in_dim(pair_slot, me * NPAIR, NPAIR)
    tgt_a = relative_index(owner, slot, wide_me, me, steps_a)
    tgt_b = relative_index(owner, slot, wide_me, me, steps_b)
    info = me.astype(jnp.int32).reshape(1)

    whole = jax.ShapeDtypeStruct((NB, W, B), jnp.float32)
    l, mt = pl.pallas_call(
        factor_kernel,
        out_shape=[whole, whole],
        in_specs=[SMEM] + [ANY] * NB,
        out_specs=[VMEM] * 2,
        scratch_shapes=[pltpu.VMEM((NB, W, B), jnp.float32), pltpu.SemaphoreType.DMA((NB,))],
        compiler_params=pltpu.CompilerParams(vmem_limit_bytes=16 * 2**20),
        cost_estimate=pl.CostEstimate(flops=2 * 10**8, bytes_accessed=4 * 10**6, transcendentals=0),
        name="factor",
    )(info, diag_block, *diag_in)

    rows = P_SIZE * B
    blocks = wide_count * narrow_count * T_DEV
    slab = jax.ShapeDtypeStruct((rows + W, B), jnp.float32)
    pair = jax.ShapeDtypeStruct((2, rows + W, B), jnp.float32)
    part = jax.ShapeDtypeStruct((blocks // 2, B // 2, B), jnp.float32)
    parts = jax.ShapeDtypeStruct((2, blocks // 2, B // 2, B), jnp.float32)
    home, near, far, keep, send_a, send_b = pl.pallas_call(
        panel_kernel,
        out_shape=[slab, slab, pair, parts, part, part],
        in_specs=[SMEM] * 4 + [VMEM] * (NB + 2),
        out_specs=[VMEM] * 6,
        scratch_shapes=[pltpu.VMEM((rows, W), jnp.bfloat16)] * 2,
        compiler_params=pltpu.CompilerParams(vmem_limit_bytes=20 * 2**20 + 4 * blocks * B * B),
        cost_estimate=pl.CostEstimate(flops=10**9, bytes_accessed=10 * 10**6, transcendentals=0),
        name="panel",
    )(info, panel_count, tgt_a, tgt_b, panel, *panel_in, mt, l)

    far = swap(far, "narrow", 2)
    near = swap(near, "narrow", 1)

    got_a, got_b = swap(send_a, "narrow", 1), swap(send_b, "narrow", 1)
    keep_a, keep_b = keep[0], keep[1]
    half = blocks // 4
    for n in (1, 2):
        send_a, send_b = keep_a[half:] + got_a[half:], keep_b[half:] + got_b[half:]
        keep_a, keep_b = keep_a[:half] + got_a[:half], keep_b[:half] + got_b[:half]
        if n == 2:
            send_a, send_b = lax.optimization_barrier((send_a, send_b))
        got_a, got_b = swap(send_a, *steps_a[n]), swap(send_b, *steps_b[n])
        half = half // 2

    def rows_of(n, size):
        at = slice(n * size, (n + 1) * size)
        return jnp.concatenate([keep_a[at] + got_a[at], keep_b[at] + got_b[at]], axis=1)

    rest = steps_a[3:]
    while len(rest) > 2:
        got = swap(rows_of(1, half), *rest.pop(0))
        total = rows_of(0, half) + got
        half = half // 2
        keep_a, keep_b = total[:, : B // 2], total[:, B // 2 :]
        got_a, got_b = jnp.zeros_like(keep_a), jnp.zeros_like(keep_b)
    (_, wide_mask), (_, narrow_mask) = rest
    both = wide_mask * narrow_count + narrow_mask
    got = [
        lax.ppermute(rows_of(3, T_DEV), ("wide", "narrow"), xor_pairs(wide_count * narrow_count, both)),
        swap(rows_of(2, T_DEV), *rest[0]),
        swap(rows_of(1, T_DEV), *rest[1]),
    ]
    got, far = lax.optimization_barrier((got, far))
    relayed = swap(far[1], "narrow", 1)
    updated = ancestor - (rows_of(0, T_DEV) + (got[0] + (got[1] + got[2])))

    def assemble(at, size):
        out = jnp.zeros((NB, size, B), jnp.float32)
        for m, piece in enumerate((home, near, far[0], relayed)):
            out = lax.dynamic_update_index_in_dim(out, piece[at : at + size], me ^ m, 0)
        return out

    return (assemble(rows, W), assemble(0, rows), updated)


def solution(mesh):
    placed = (
        P("wide", None, "narrow"),
        P("wide", None, "narrow"),
        P("wide"),
        P("wide", None),
        P("wide"),
        P(("wide", "narrow"), None, None),
    )
    return jax.shard_map(
        local,
        mesh=mesh,
        in_specs=placed,
        out_specs=(
            P("wide", None, "narrow"),
            P("wide", None, "narrow"),
            P(("wide", "narrow"), None, None),
        ),
        check_vma=False,
    )
```

```python
import jax
import jax.numpy as jnp
import numpy as np
from jax import lax
from jax.experimental import pallas as pl
from jax.experimental.pallas import tpu as pltpu
from jax.sharding import PartitionSpec as P

W = 512
B = 128
P_SIZE = 8
T_DEV = 2
NB = W // B
NPAIR = P_SIZE * (P_SIZE + 1) // 2
HIGHEST = lax.Precision.HIGHEST


def dot_nt(a, b):
    return lax.dot_general(
        a, b, (((1,), (1,)), ((), ())), precision=HIGHEST, preferred_element_type=jnp.float32
    )


def dot_nn(a, b):
    return lax.dot_general(
        a, b, (((1,), (0,)), ((), ())), precision=HIGHEST, preferred_element_type=jnp.float32
    )


def lane_of(x, c):
    return jnp.broadcast_to(x[:, c : c + 1], x.shape)


def row_of(x, r):
    return jnp.broadcast_to(x[r : r + 1, :], x.shape)


def inverse_factor(block):
    sub = lax.broadcasted_iota(jnp.int32, (8, B), 0)
    lane = lax.broadcasted_iota(jnp.int32, (8, B), 1)
    total, strip = B // 8, 2
    rows = [block[8 * q : 8 * q + 8, :] for q in range(total)]
    done = [None] * total
    for b in range(0, total, strip):
        mine = range(b, b + strip)
        near = range(b + strip, min(b + 2 * strip, total))
        far = range(b + 2 * strip, total)
        in_strip = (lane >= 8 * b) & (lane < 8 * (b + strip))
        ahead = {q: [lane_of(rows[q], 8 * b + m) for m in range(8 * strip)] for q in near}
        for p in mine:
            lo = 8 * p
            own = (lane >= lo) & (lane < lo + 8)
            cols = [lane_of(rows[p], lo + m) for m in range(8)]
            others = [q for q in mine if q != p]
            mult = {q: [lane_of(rows[q], lo + m) for m in range(8)] for q in others}
            work = jnp.where(own, (lane - lo == sub).astype(jnp.float32), rows[p])
            final = jnp.zeros((8, B), jnp.float32)
            for k in range(0, 8, 2):
                f0, f1 = cols[k], cols[k + 1]
                a, h, c = row_of(f0, k), row_of(f0, k + 1), row_of(f1, k + 1)
                det = a * c - h * h
                recip = 1.0 / det
                ar, hr, cr = a * recip, h * recip, c * recip
                first, second = sub == k, sub == k + 1

                def eliminate(v):
                    r0, r1 = row_of(v, k), row_of(v, k + 1)
                    s0, s1 = cr * r0 - hr * r1, ar * r1 - hr * r0
                    return r0, r1, jnp.where(first, s0, jnp.where(second, s1, v - f0 * s0 - f1 * s1))

                for m in range(k + 2, 8):
                    cols[m] = eliminate(cols[m])[2]
                r0, r1, work = eliminate(work)
                root = lax.rsqrt(a)
                lower = (a * r1 - h * r0) * (root * lax.rsqrt(det))
                final = jnp.where(first, r0 * root, jnp.where(second, lower, final))
            done[p] = jnp.where(lane <= sub + lo, final, 0.0)
            rows[p] = work
            lines = [row_of(work, m) for m in range(8)]
            for q in others:
                new = jnp.where(own, 0.0, rows[q])
                for m in range(8):
                    new = new - mult[q][m] * lines[m]
                rows[q] = new
        lines = [row_of(rows[q], m) for q in mine for m in range(8)]
        for q in near:
            parts = [ahead[q][m] * lines[m] for m in range(4)]
            for m in range(4, 8 * strip):
                parts[m % 4] = parts[m % 4] + ahead[q][m] * lines[m]
            rows[q] = jnp.where(in_strip, 0.0, rows[q]) - ((parts[0] + parts[1]) + (parts[2] + parts[3]))
        if far:
            stack = jnp.concatenate([rows[q] for q in far], axis=0)
            lane_far = lax.broadcasted_iota(jnp.int32, stack.shape, 1)
            in_far = (lane_far >= 8 * b) & (lane_far < 8 * (b + strip))
            zero = jnp.zeros((8, B), jnp.float32)
            tall = jnp.concatenate([rows[q] if q in mine else zero for q in range(total)], axis=0)
            stack = jnp.where(in_far, 0.0, stack) - dot_nn(jnp.where(in_far, stack, 0.0), tall)
            for n, q in enumerate(far):
                rows[q] = stack[8 * n : 8 * n + 8]
    return jnp.concatenate(done, axis=0)


def split_bf16(v):
    high = v.astype(jnp.bfloat16)
    return high, (v - high.astype(jnp.float32)).astype(jnp.bfloat16)


def dot3(left, right, contract):
    dot = lambda a, b: lax.dot_general(
        a, b, (contract, ((), ())), preferred_element_type=jnp.float32
    )
    return dot(left[0], right[0]) + (dot(left[0], right[1]) + dot(left[1], right[0]))


def factor_kernel(info, own_ref, r1, r2, r3, l, mt, a, sems):
    me = info[0]
    side = me // 2
    far_rows = pl.ds((1 - side) * (W // 2), W // 2)
    places = [a.at[me], a.at[me ^ 1], a.at[me ^ 2, far_rows], a.at[me ^ 3, far_rows]]
    ins = [own_ref.at[me], r1, r2, r3]
    copies = [pltpu.make_async_copy(ins[m], places[m], sems.at[m]) for m in range(NB)]
    for c in copies:
        c.start()
    for c in copies:
        c.wait()

    @pl.when(side == 1)
    def _():
        for j in range(NB // 2):
            for i in range(NB // 2, NB):
                a[j, pl.ds(i * B, B), :] = a[i, pl.ds(j * B, B), :].T

    row = lax.broadcasted_iota(jnp.int32, (B, B), 0)
    col = lax.broadcasted_iota(jnp.int32, (B, B), 1)
    l[...] = jnp.zeros_like(l)
    mt[...] = jnp.zeros_like(mt)
    eye = (row == col).astype(jnp.float32)
    for k in range(NB):
        here = pl.ds(k * B, B)
        inv = inverse_factor(a[k, here, :])
        l[k, here, :] = jnp.where(row >= col, dot_nt(a[k, here, :], inv), 0.0)
        for i in range(k + 1, NB):
            below = dot_nt(a[k, pl.ds(i * B, B), :], inv)
            l[k, pl.ds(i * B, B), :] = below
            for j in range(k + 1, i + 1):
                a[j, pl.ds(i * B, B), :] -= dot_nt(below, l[k, pl.ds(j * B, B), :])
        mt[k, here, :] = dot_nt(eye, inv)
        for i in range(k):
            total = dot_nt(mt[i, pl.ds(i * B, B), :], l[i, here, :])
            for j in range(i + 1, k):
                total = total + dot_nt(mt[j, pl.ds(i * B, B), :], l[j, here, :])
            mt[k, pl.ds(i * B, B), :] = dot_nt(-total, inv)


def panel_kernel(
    info, counts, tgt_a, tgt_b, own_ref, r1, r2, r3, mt, l, own, near, far_x, far_l, keep_a, keep_b, send_a, send_b, xh, xl
):
    me = info[0]
    count = counts[me]
    rows = P_SIZE * B
    ins = [own_ref.at[me], r1, r2, r3]
    outs = [own, near, far_x.at[0], far_x.at[1]]
    own[pl.ds(rows, W), :] = l[me]
    near[pl.ds(rows, W), :] = l[me ^ 1]
    far_l[0] = l[me ^ 2]
    far_l[1] = l[me ^ 3]
    live = lax.broadcasted_iota(jnp.int32, (rows, B), 0) < count * B
    parts = [split_bf16(jnp.where(live, ref[...], 0.0)) for ref in ins]
    left = [jnp.concatenate([part[n] for part in parts], axis=1) for n in range(2)]
    for c in range(0, NB, 2):
        right = [
            jnp.concatenate([mt[me ^ m, pl.ds((me ^ k) * B, B), :] for m in (c, c + 1)], axis=1)
            for k in range(NB)
        ]
        got = dot3(left, split_bf16(jnp.concatenate(right, axis=0)), ((1,), (0,)))
        outs[c][pl.ds(0, rows), :] = got[:, :B]
        outs[c + 1][pl.ds(0, rows), :] = got[:, B:]
        high, low = split_bf16(got)
        xh[:, pl.ds(c * B, 2 * B)] = high
        xl[:, pl.ds(c * B, 2 * B)] = low

    keep_a[...] = jnp.zeros_like(keep_a)
    keep_b[...] = jnp.zeros_like(keep_b)
    send_a[...] = jnp.zeros_like(send_a)
    send_b[...] = jnp.zeros_like(send_b)
    half, strip = keep_a.shape[:2]
    for j in range(0, P_SIZE, 2):

        @pl.when(j < count)
        def _():
            left = (xh[pl.ds(j * B, rows - j * B), :], xl[pl.ds(j * B, rows - j * B), :])
            right = (xh[pl.ds(j * B, 2 * B), :], xl[pl.ds(j * B, 2 * B), :])
            got = dot3(left, right, ((1,), (1,)))
            for i in range(j, P_SIZE):
                for n in range(2 if i > j else 1):
                    block = got[(i - j) * B : (i - j + 1) * B, n * B : (n + 1) * B]
                    pair = i * (i + 1) // 2 + j + n
                    away = (tgt_a[pair] >= half).astype(jnp.float32)
                    for tgt, keep, send, piece in (
                        (tgt_a, keep_a, send_a, block[:strip]),
                        (tgt_b, keep_b, send_b, block[strip:]),
                    ):
                        at = lax.rem(tgt[pair], half)
                        keep[at] += piece * (1.0 - away)
                        send[at] += piece * away


SMEM = pl.BlockSpec(memory_space=pltpu.SMEM)
ANY = pl.BlockSpec(memory_space=pl.ANY)
VMEM = pl.BlockSpec(memory_space=pltpu.VMEM)


def xor_pairs(size, mask):
    return [(i, i ^ mask) for i in range(size)]


def log2(n):
    return n.bit_length() - 1


def swap(x, axis, mask):
    return lax.ppermute(x, axis, xor_pairs(lax.axis_size(axis), mask))


def relative_index(owner, slot, wide_me, narrow_me, steps):
    away = {"wide": owner ^ wide_me, "narrow": (slot // T_DEV) ^ narrow_me}
    index = jnp.zeros_like(owner)
    for axis, mask in steps:
        index = index * 2 + ((away[axis] // mask) & 1)
    return index * T_DEV + slot % T_DEV


def local(diag_block, panel, panel_count, pair_owner, pair_slot, ancestor):
    narrow_count = lax.axis_size("narrow")
    wide_count = lax.axis_size("wide")
    me = lax.axis_index("narrow")
    wide_me = lax.axis_index("wide")
    assert narrow_count == NB and diag_block.shape[0] == NB
    masks = range(1, NB)
    own = lambda x, m: lax.dynamic_index_in_dim(x, me ^ m, 0, keepdims=False)
    half_of = lambda x, m: lax.dynamic_slice(
        x, (me ^ m, (me // 2) * (W // 2), 0), (1, W // 2, B)
    ).reshape(W // 2, B)
    halves = [half_of(diag_block, m) for m in masks[1:]]
    _, near_block = lax.optimization_barrier((halves, diag_block))
    diag_in = [swap(own(near_block, 1), "narrow", 1)]
    diag_in += [swap(part, "narrow", m) for m, part in zip(masks[1:], halves)]
    panel_out = [own(panel, m) for m in masks]
    _, panel_out = lax.optimization_barrier((diag_in, panel_out))
    panel_in = [swap(panel_out[m - 1], "narrow", m) for m in masks]

    narrow_steps = [("narrow", 1 << b) for b in range(log2(narrow_count))]
    wide_steps = [("wide", 1 << b) for b in range(log2(wide_count))]
    first, last = narrow_steps[:1], wide_steps[2:] + narrow_steps[1:]
    steps_a = first + wide_steps[:2] + last
    steps_b = first + wide_steps[1::-1] + last
    owner = lax.dynamic_slice_in_dim(pair_owner[:, 0], me * NPAIR, NPAIR)
    slot = lax.dynamic_slice_in_dim(pair_slot, me * NPAIR, NPAIR)
    tgt_a = relative_index(owner, slot, wide_me, me, steps_a)
    tgt_b = relative_index(owner, slot, wide_me, me, steps_b)
    info = me.astype(jnp.int32).reshape(1)

    whole = jax.ShapeDtypeStruct((NB, W, B), jnp.float32)
    l, mt = pl.pallas_call(
        factor_kernel,
        out_shape=[whole, whole],
        in_specs=[SMEM] + [ANY] * NB,
        out_specs=[VMEM] * 2,
        scratch_shapes=[pltpu.VMEM((NB, W, B), jnp.float32), pltpu.SemaphoreType.DMA((NB,))],
        compiler_params=pltpu.CompilerParams(vmem_limit_bytes=16 * 2**20),
        cost_estimate=pl.CostEstimate(flops=2 * 10**8, bytes_accessed=4 * 10**6, transcendentals=0),
        name="factor",
    )(info, diag_block, *diag_in)

    rows = P_SIZE * B
    blocks = wide_count * narrow_count * T_DEV
    slab = jax.ShapeDtypeStruct((rows + W, B), jnp.float32)
    pair_x = jax.ShapeDtypeStruct((2, rows, B), jnp.float32)
    pair_l = jax.ShapeDtypeStruct((2, W, B), jnp.float32)
    part = jax.ShapeDtypeStruct((blocks // 2, B // 2, B), jnp.float32)
    home, near, far_x, far_l, keep_a, keep_b, send_a, send_b = pl.pallas_call(
        panel_kernel,
        out_shape=[slab, slab, pair_x, pair_l] + [part] * 4,
        in_specs=[SMEM] * 4 + [VMEM] * (NB + 2),
        out_specs=[VMEM] * 8,
        scratch_shapes=[pltpu.VMEM((rows, W), jnp.bfloat16)] * 2,
        compiler_params=pltpu.CompilerParams(vmem_limit_bytes=20 * 2**20 + 4 * blocks * B * B),
        cost_estimate=pl.CostEstimate(flops=10**9, bytes_accessed=10 * 10**6, transcendentals=0),
        name="panel",
    )(info, panel_count, tgt_a, tgt_b, panel, *panel_in, mt, l)

    far_x = swap(far_x, "narrow", 2)
    far_l = swap(far_l, "narrow", 2)
    near = swap(near, "narrow", 1)

    got_a, got_b = swap(send_a, "narrow", 1), swap(send_b, "narrow", 1)
    half = blocks // 4
    for n in (1, 2):
        send_a = keep_a[half:] + got_a[half:]
        send_a, got_b = lax.optimization_barrier((send_a, got_b))
        send_b = keep_b[half:] + got_b[half:]
        keep_a, keep_b = keep_a[:half] + got_a[:half], keep_b[:half] + got_b[:half]
        if n == 2:
            send_a, send_b = lax.optimization_barrier((send_a, send_b))
        got_a, got_b = swap(send_a, *steps_a[n]), swap(send_b, *steps_b[n])
        half = half // 2
    send = jnp.concatenate([keep_a[half:] + got_a[half:], keep_b[half:] + got_b[half:]], axis=1)
    keep = jnp.concatenate([keep_a[:half] + got_a[:half], keep_b[:half] + got_b[:half]], axis=1)
    for n in range(3, len(steps_a)):
        if n == 3:
            send, far_x = lax.optimization_barrier((send, far_x))
        if n == len(steps_a) - 1:
            send, far_l = lax.optimization_barrier((send, far_l))
        got = swap(send, *steps_a[n])
        if n + 1 < len(steps_a):
            half = half // 2
            send = keep[half:] + got[half:]
            keep = keep[:half] + got[:half]
    relayed_x = swap(far_x[1], "narrow", 1)
    relayed_l = swap(far_l[1], "narrow", 1)
    updated = ancestor - (keep + got)

    def assemble(pieces):
        out = jnp.zeros((NB,) + pieces[0].shape, jnp.float32)
        for m, piece in enumerate(pieces):
            out = lax.dynamic_update_index_in_dim(out, piece, me ^ m, 0)
        return out

    return (
        assemble([home[rows:], near[rows:], far_l[0], relayed_l]),
        assemble([home[:rows], near[:rows], far_x[0], relayed_x]),
        updated,
    )


def solution(mesh):
    placed = (
        P("wide", None, "narrow"),
        P("wide", None, "narrow"),
        P("wide"),
        P("wide", None),
        P("wide"),
        P(("wide", "narrow"), None, None),
    )
    return jax.shard_map(
        local,
        mesh=mesh,
        in_specs=placed,
        out_specs=(
            P("wide", None, "narrow"),
            P("wide", None, "narrow"),
            P(("wide", "narrow"), None, None),
        ),
        check_vma=False,
    )
```

```python
import jax
import jax.numpy as jnp
import numpy as np
from jax import lax
from jax.experimental import pallas as pl
from jax.experimental.pallas import tpu as pltpu
from jax.sharding import PartitionSpec as P

W = 512
B = 128
P_SIZE = 8
T_DEV = 2
NB = W // B
NPAIR = P_SIZE * (P_SIZE + 1) // 2
HIGHEST = lax.Precision.HIGHEST


def dot_nt(a, b):
    return lax.dot_general(
        a, b, (((1,), (1,)), ((), ())), precision=HIGHEST, preferred_element_type=jnp.float32
    )


def dot_nn(a, b):
    return lax.dot_general(
        a, b, (((1,), (0,)), ((), ())), precision=HIGHEST, preferred_element_type=jnp.float32
    )


def lane_of(x, c):
    return jnp.broadcast_to(x[:, c : c + 1], x.shape)


def row_of(x, r):
    return jnp.broadcast_to(x[r : r + 1, :], x.shape)


def inverse_factor(block):
    sub = lax.broadcasted_iota(jnp.int32, (8, B), 0)
    lane = lax.broadcasted_iota(jnp.int32, (8, B), 1)
    total, strip = B // 8, 2
    rows = [block[8 * q : 8 * q + 8, :] for q in range(total)]
    done = [None] * total
    for b in range(0, total, strip):
        mine = range(b, b + strip)
        near = range(b + strip, min(b + 2 * strip, total))
        far = range(b + 2 * strip, total)
        in_strip = (lane >= 8 * b) & (lane < 8 * (b + strip))
        ahead = {q: [lane_of(rows[q], 8 * b + m) for m in range(8 * strip)] for q in near}
        for p in mine:
            lo = 8 * p
            own = (lane >= lo) & (lane < lo + 8)
            cols = [lane_of(rows[p], lo + m) for m in range(8)]
            others = [q for q in mine if q != p]
            mult = {q: [lane_of(rows[q], lo + m) for m in range(8)] for q in others}
            work = jnp.where(own, (lane - lo == sub).astype(jnp.float32), rows[p])
            final = jnp.zeros((8, B), jnp.float32)
            for k in range(0, 8, 2):
                f0, f1 = cols[k], cols[k + 1]
                a, h, c = row_of(f0, k), row_of(f0, k + 1), row_of(f1, k + 1)
                det = a * c - h * h
                recip = 1.0 / det
                ar, hr, cr = a * recip, h * recip, c * recip
                first, second = sub == k, sub == k + 1

                def eliminate(v):
                    r0, r1 = row_of(v, k), row_of(v, k + 1)
                    s0, s1 = cr * r0 - hr * r1, ar * r1 - hr * r0
                    return r0, r1, jnp.where(first, s0, jnp.where(second, s1, v - f0 * s0 - f1 * s1))

                for m in range(k + 2, 8):
                    cols[m] = eliminate(cols[m])[2]
                r0, r1, work = eliminate(work)
                root = lax.rsqrt(a)
                lower = (a * r1 - h * r0) * (root * lax.rsqrt(det))
                final = jnp.where(first, r0 * root, jnp.where(second, lower, final))
            done[p] = jnp.where(lane <= sub + lo, final, 0.0)
            rows[p] = work
            lines = [row_of(work, m) for m in range(8)]
            for q in others:
                new = jnp.where(own, 0.0, rows[q])
                for m in range(8):
                    new = new - mult[q][m] * lines[m]
                rows[q] = new
        lines = [row_of(rows[q], m) for q in mine for m in range(8)]
        for q in near:
            parts = [ahead[q][m] * lines[m] for m in range(4)]
            for m in range(4, 8 * strip):
                parts[m % 4] = parts[m % 4] + ahead[q][m] * lines[m]
            rows[q] = jnp.where(in_strip, 0.0, rows[q]) - ((parts[0] + parts[1]) + (parts[2] + parts[3]))
        if far:
            stack = jnp.concatenate([rows[q] for q in far], axis=0)
            lane_far = lax.broadcasted_iota(jnp.int32, stack.shape, 1)
            in_far = (lane_far >= 8 * b) & (lane_far < 8 * (b + strip))
            zero = jnp.zeros((8, B), jnp.float32)
            tall = jnp.concatenate([rows[q] if q in mine else zero for q in range(total)], axis=0)
            stack = jnp.where(in_far, 0.0, stack) - dot_nn(jnp.where(in_far, stack, 0.0), tall)
            for n, q in enumerate(far):
                rows[q] = stack[8 * n : 8 * n + 8]
    return jnp.concatenate(done, axis=0)


def split_bf16(v):
    high = v.astype(jnp.bfloat16)
    return high, (v - high.astype(jnp.float32)).astype(jnp.bfloat16)


def dot3(left, right, contract):
    dot = lambda a, b: lax.dot_general(
        a, b, (contract, ((), ())), preferred_element_type=jnp.float32
    )
    return dot(left[0], right[0]) + (dot(left[0], right[1]) + dot(left[1], right[0]))


def cut_kernel(info, blocks, near, far_a, far_b, sems):
    me = info[0]
    half = pl.ds((me // 2) * (W // 2), W // 2)
    copies = [
        pltpu.make_async_copy(blocks.at[me ^ 2, half], far_a, sems.at[0]),
        pltpu.make_async_copy(blocks.at[me ^ 3, half], far_b, sems.at[1]),
        pltpu.make_async_copy(blocks.at[me ^ 1], near, sems.at[2]),
    ]
    for c in copies:
        c.start()
    for c in copies:
        c.wait()


def factor_kernel(info, own_ref, r1, r2, r3, l0, l1, l2, l3, mt, a, l, sems):
    me = info[0]
    side = me // 2
    far_rows = pl.ds((1 - side) * (W // 2), W // 2)
    places = [a.at[me], a.at[me ^ 1], a.at[me ^ 2, far_rows], a.at[me ^ 3, far_rows]]
    ins = [own_ref.at[me], r1, r2, r3]
    copies = [pltpu.make_async_copy(ins[m], places[m], sems.at[m]) for m in range(NB)]
    for c in copies:
        c.start()
    for c in copies:
        c.wait()

    @pl.when(side == 1)
    def _():
        for j in range(NB // 2):
            for i in range(NB // 2, NB):
                a[j, pl.ds(i * B, B), :] = a[i, pl.ds(j * B, B), :].T

    row = lax.broadcasted_iota(jnp.int32, (B, B), 0)
    col = lax.broadcasted_iota(jnp.int32, (B, B), 1)
    l[...] = jnp.zeros_like(l)
    mt[...] = jnp.zeros_like(mt)
    eye = (row == col).astype(jnp.float32)
    for k in range(NB):
        here = pl.ds(k * B, B)
        inv = inverse_factor(a[k, here, :])
        l[k, here, :] = jnp.where(row >= col, dot_nt(a[k, here, :], inv), 0.0)
        for i in range(k + 1, NB):
            below = dot_nt(a[k, pl.ds(i * B, B), :], inv)
            l[k, pl.ds(i * B, B), :] = below
            for j in range(k + 1, i + 1):
                a[j, pl.ds(i * B, B), :] -= dot_nt(below, l[k, pl.ds(j * B, B), :])
        mt[k, here, :] = dot_nt(eye, inv)
        for i in range(k):
            total = dot_nt(mt[i, pl.ds(i * B, B), :], l[i, here, :])
            for j in range(i + 1, k):
                total = total + dot_nt(mt[j, pl.ds(i * B, B), :], l[j, here, :])
            mt[k, pl.ds(i * B, B), :] = dot_nt(-total, inv)
    outs = [l0, l1, l2, l3]
    copies = [pltpu.make_async_copy(l.at[me ^ m], outs[m], sems.at[m]) for m in range(NB)]
    for c in copies:
        c.start()
    for c in copies:
        c.wait()


def panel_kernel(info, counts, tgt_a, tgt_b, own_ref, r1, r2, r3, mt, x0, x1, x2, x3, keep, send, xh, xl):
    me = info[0]
    count = counts[me]
    rows = P_SIZE * B
    ins = [own_ref.at[me], r1, r2, r3]
    outs = [x0, x1, x2, x3]
    live = lax.broadcasted_iota(jnp.int32, (rows, B), 0) < count * B
    parts = [split_bf16(jnp.where(live, ref[...], 0.0)) for ref in ins]
    left = [jnp.concatenate([part[n] for part in parts], axis=1) for n in range(2)]
    for c in range(0, NB, 2):
        right = [
            jnp.concatenate([mt[me ^ m, pl.ds((me ^ k) * B, B), :] for m in (c, c + 1)], axis=1)
            for k in range(NB)
        ]
        got = dot3(left, split_bf16(jnp.concatenate(right, axis=0)), ((1,), (0,)))
        outs[c][...] = got[:, :B]
        outs[c + 1][...] = got[:, B:]
        high, low = split_bf16(got)
        xh[:, pl.ds(c * B, 2 * B)] = high
        xl[:, pl.ds(c * B, 2 * B)] = low

    keep[...] = jnp.zeros_like(keep)
    send[...] = jnp.zeros_like(send)
    half, strip = keep.shape[1:3]
    for j in range(0, P_SIZE, 2):

        @pl.when(j < count)
        def _():
            left = (xh[pl.ds(j * B, rows - j * B), :], xl[pl.ds(j * B, rows - j * B), :])
            right = (xh[pl.ds(j * B, 2 * B), :], xl[pl.ds(j * B, 2 * B), :])
            got = dot3(left, right, ((1,), (1,)))
            for i in range(j, P_SIZE):
                for n in range(2 if i > j else 1):
                    block = got[(i - j) * B : (i - j + 1) * B, n * B : (n + 1) * B]
                    pair = i * (i + 1) // 2 + j + n
                    away = (tgt_a[pair] >= half).astype(jnp.float32)
                    for stream, tgt in enumerate((tgt_a, tgt_b)):
                        at = lax.rem(tgt[pair], half)
                        piece = block[stream * strip : (stream + 1) * strip]
                        keep[stream, at] += piece * (1.0 - away)
                        send[stream, at] += piece * away


SMEM = pl.BlockSpec(memory_space=pltpu.SMEM)
ANY = pl.BlockSpec(memory_space=pl.ANY)
VMEM = pl.BlockSpec(memory_space=pltpu.VMEM)


def xor_pairs(size, mask):
    return [(i, i ^ mask) for i in range(size)]


def log2(n):
    return n.bit_length() - 1


def swap(x, axis, mask):
    return lax.ppermute(x, axis, xor_pairs(lax.axis_size(axis), mask))


def relative_index(owner, slot, wide_me, narrow_me, steps):
    away = {"wide": owner ^ wide_me, "narrow": (slot // T_DEV) ^ narrow_me}
    index = jnp.zeros_like(owner)
    for axis, mask in steps:
        index = index * 2 + ((away[axis] // mask) & 1)
    return index * T_DEV + slot % T_DEV


def local(diag_block, panel, panel_count, pair_owner, pair_slot, ancestor):
    narrow_count = lax.axis_size("narrow")
    wide_count = lax.axis_size("wide")
    me = lax.axis_index("narrow")
    wide_me = lax.axis_index("wide")
    assert narrow_count == NB and diag_block.shape[0] == NB
    masks = range(1, NB)
    own = lambda x, m: lax.dynamic_index_in_dim(x, me ^ m, 0, keepdims=False)
    info = me.astype(jnp.int32).reshape(1)
    cut = [jax.ShapeDtypeStruct((rows, B), jnp.float32) for rows in (W, W // 2, W // 2)]
    cut = pl.pallas_call(
        cut_kernel,
        out_shape=cut,
        in_specs=[SMEM, pl.BlockSpec(memory_space=pltpu.HBM)],
        out_specs=[VMEM] * 3,
        scratch_shapes=[pltpu.SemaphoreType.DMA((3,))],
        compiler_params=pltpu.CompilerParams(vmem_limit_bytes=8 * 2**20),
        cost_estimate=pl.CostEstimate(flops=0, bytes_accessed=2**20, transcendentals=0),
        name="cut",
    )(info, diag_block)
    diag_in = [swap(part, "narrow", m) for m, part in zip(masks, cut)]
    panel_out = [own(panel, m) for m in masks]
    diag_in, panel_out = lax.optimization_barrier((diag_in, panel_out))
    panel_in = [swap(panel_out[m - 1], "narrow", m) for m in masks]

    narrow_steps = [("narrow", 1 << b) for b in range(log2(narrow_count))]
    wide_steps = [("wide", 1 << b) for b in range(log2(wide_count))]
    first, last = narrow_steps[:1], wide_steps[2:] + narrow_steps[1:]
    steps_a = first + wide_steps[:2] + last
    steps_b = first + wide_steps[1::-1] + last
    owner = lax.dynamic_slice_in_dim(pair_owner[:, 0], me * NPAIR, NPAIR)
    slot = lax.dynamic_slice_in_dim(pair_slot, me * NPAIR, NPAIR)
    tgt_a = relative_index(owner, slot, wide_me, me, steps_a)
    tgt_b = relative_index(owner, slot, wide_me, me, steps_b)

    slab = jax.ShapeDtypeStruct((W, B), jnp.float32)
    *l_parts, mt = pl.pallas_call(
        factor_kernel,
        out_shape=[slab] * NB + [jax.ShapeDtypeStruct((NB, W, B), jnp.float32)],
        in_specs=[SMEM] + [ANY] * NB,
        out_specs=[ANY] * NB + [VMEM],
        scratch_shapes=[pltpu.VMEM((NB, W, B), jnp.float32)] * 2 + [pltpu.SemaphoreType.DMA((NB,))],
        compiler_params=pltpu.CompilerParams(vmem_limit_bytes=32 * 2**20),
        cost_estimate=pl.CostEstimate(flops=2 * 10**8, bytes_accessed=4 * 10**6, transcendentals=0),
        name="factor",
    )(info, diag_block, *diag_in)

    rows = P_SIZE * B
    blocks = wide_count * narrow_count * T_DEV
    slab = jax.ShapeDtypeStruct((rows, B), jnp.float32)
    part = jax.ShapeDtypeStruct((2, blocks // 2, B // 2, B), jnp.float32)
    *x_parts, keep, send = pl.pallas_call(
        panel_kernel,
        out_shape=[slab] * NB + [part, part],
        in_specs=[SMEM] * 4 + [VMEM] * (NB + 1),
        out_specs=[VMEM] * (NB + 2),
        scratch_shapes=[pltpu.VMEM((rows, W), jnp.bfloat16)] * 2,
        compiler_params=pltpu.CompilerParams(vmem_limit_bytes=20 * 2**20 + 4 * blocks * B * B),
        cost_estimate=pl.CostEstimate(flops=10**9, bytes_accessed=10 * 10**6, transcendentals=0),
        name="panel",
    )(info, panel_count, tgt_a, tgt_b, panel, *panel_in, mt)

    l_back = [swap(l_parts[m], "narrow", m) for m in masks]
    x_back = [swap(x_parts[m], "narrow", m) for m in masks]

    got = swap(send, "narrow", 1)
    half = blocks // 4
    upper = lambda u, n: u[n, half:]
    lower = lambda u, n: u[n, :half]
    send_a = upper(keep, 0) + upper(got, 0)
    send_b = upper(keep, 1) + upper(got, 1)
    keep_a = lower(keep, 0) + lower(got, 0)
    keep_b = lower(keep, 1) + lower(got, 1)
    for n, (box, at) in ((1, (l_back, 1)), (2, (x_back, 1))):
        send_a, send_b, box[at] = lax.optimization_barrier((send_a, send_b, box[at]))
        got_a = swap(send_a, *steps_a[n])
        got_b = swap(send_b, *steps_b[n])
        half = half // 2
        if n == 1:
            send_a, send_b = keep_a[half:] + got_a[half:], keep_b[half:] + got_b[half:]
            keep_a, keep_b = keep_a[:half] + got_a[:half], keep_b[:half] + got_b[:half]
    rest = steps_a[3:]
    take = lambda n, size: jnp.concatenate(
        [u[n * size : (n + 1) * size] + v[n * size : (n + 1) * size] for u, v in ((keep_a, got_a), (keep_b, got_b))],
        axis=1,
    )
    while len(rest) > 2:
        got = swap(take(1, half), *rest.pop(0))
        keep_a = take(0, half) + got
        half = half // 2
        keep_a, keep_b = keep_a[:, : B // 2], keep_a[:, B // 2 :]
        got_a, got_b = jnp.zeros_like(keep_a), jnp.zeros_like(keep_b)
    onward, stay = take(3, T_DEV), take(2, T_DEV)
    onward, stay, l_back[2] = lax.optimization_barrier((onward, stay, l_back[2]))
    onward = take(1, T_DEV) + swap(onward, *rest[0])
    stay = swap(stay, *rest[0])
    onward, x_back[2], x_back[0] = lax.optimization_barrier((onward, x_back[2], x_back[0]))
    updated = ancestor - (take(0, T_DEV) + stay + swap(onward, *rest[1]))

    def give_back(own_part, others):
        back = [own_part] + others
        out = jnp.zeros((NB,) + own_part.shape, jnp.float32)
        for m in range(NB):
            out = lax.dynamic_update_index_in_dim(out, back[m], me ^ m, 0)
        return out

    return (give_back(l_parts[0], l_back), give_back(x_parts[0], x_back), updated)


def solution(mesh):
    placed = (
        P("wide", None, "narrow"),
        P("wide", None, "narrow"),
        P("wide"),
        P("wide", None),
        P("wide"),
        P(("wide", "narrow"), None, None),
    )
    return jax.shard_map(
        local,
        mesh=mesh,
        in_specs=placed,
        out_specs=(
            P("wide", None, "narrow"),
            P("wide", None, "narrow"),
            P(("wide", "narrow"), None, None),
        ),
        check_vma=False,
    )
```

```python
import jax
import jax.numpy as jnp
import numpy as np
from jax import lax
from jax.experimental import pallas as pl
from jax.experimental.pallas import tpu as pltpu
from jax.sharding import PartitionSpec as P

W = 512
B = 128
P_SIZE = 8
T_DEV = 2
NB = W // B
NPAIR = P_SIZE * (P_SIZE + 1) // 2
HIGHEST = lax.Precision.HIGHEST


def dot_nt(a, b):
    return lax.dot_general(
        a, b, (((1,), (1,)), ((), ())), precision=HIGHEST, preferred_element_type=jnp.float32
    )


def dot_nn(a, b):
    return lax.dot_general(
        a, b, (((1,), (0,)), ((), ())), precision=HIGHEST, preferred_element_type=jnp.float32
    )


def lane_of(x, c):
    return jnp.broadcast_to(x[:, c : c + 1], x.shape)


def row_of(x, r):
    return jnp.broadcast_to(x[r : r + 1, :], x.shape)


def inverse_factor(block):
    sub = lax.broadcasted_iota(jnp.int32, (8, B), 0)
    lane = lax.broadcasted_iota(jnp.int32, (8, B), 1)
    total, strip = B // 8, 2
    rows = [block[8 * q : 8 * q + 8, :] for q in range(total)]
    done = [None] * total
    for b in range(0, total, strip):
        mine = range(b, b + strip)
        near = range(b + strip, min(b + 2 * strip, total))
        far = range(b + 2 * strip, total)
        in_strip = (lane >= 8 * b) & (lane < 8 * (b + strip))
        ahead = {q: [lane_of(rows[q], 8 * b + m) for m in range(8 * strip)] for q in near}
        for p in mine:
            lo = 8 * p
            own = (lane >= lo) & (lane < lo + 8)
            cols = [lane_of(rows[p], lo + m) for m in range(8)]
            others = [q for q in mine if q != p]
            mult = {q: [lane_of(rows[q], lo + m) for m in range(8)] for q in others}
            work = jnp.where(own, (lane - lo == sub).astype(jnp.float32), rows[p])
            final = jnp.zeros((8, B), jnp.float32)
            for k in range(0, 8, 2):
                f0, f1 = cols[k], cols[k + 1]
                a, h, c = row_of(f0, k), row_of(f0, k + 1), row_of(f1, k + 1)
                det = a * c - h * h
                recip = 1.0 / det
                ar, hr, cr = a * recip, h * recip, c * recip
                first, second = sub == k, sub == k + 1

                def eliminate(v):
                    r0, r1 = row_of(v, k), row_of(v, k + 1)
                    s0, s1 = cr * r0 - hr * r1, ar * r1 - hr * r0
                    return r0, r1, jnp.where(first, s0, jnp.where(second, s1, v - f0 * s0 - f1 * s1))

                for m in range(k + 2, 8):
                    cols[m] = eliminate(cols[m])[2]
                r0, r1, work = eliminate(work)
                root = lax.rsqrt(a)
                lower = (a * r1 - h * r0) * (root * lax.rsqrt(det))
                final = jnp.where(first, r0 * root, jnp.where(second, lower, final))
            done[p] = jnp.where(lane <= sub + lo, final, 0.0)
            rows[p] = work
            lines = [row_of(work, m) for m in range(8)]
            for q in others:
                new = jnp.where(own, 0.0, rows[q])
                for m in range(8):
                    new = new - mult[q][m] * lines[m]
                rows[q] = new
        lines = [row_of(rows[q], m) for q in mine for m in range(8)]
        for q in near:
            parts = [ahead[q][m] * lines[m] for m in range(4)]
            for m in range(4, 8 * strip):
                parts[m % 4] = parts[m % 4] + ahead[q][m] * lines[m]
            rows[q] = jnp.where(in_strip, 0.0, rows[q]) - ((parts[0] + parts[1]) + (parts[2] + parts[3]))
        if far:
            stack = jnp.concatenate([rows[q] for q in far], axis=0)
            lane_far = lax.broadcasted_iota(jnp.int32, stack.shape, 1)
            in_far = (lane_far >= 8 * b) & (lane_far < 8 * (b + strip))
            zero = jnp.zeros((8, B), jnp.float32)
            tall = jnp.concatenate([rows[q] if q in mine else zero for q in range(total)], axis=0)
            stack = jnp.where(in_far, 0.0, stack) - dot_nn(jnp.where(in_far, stack, 0.0), tall)
            for n, q in enumerate(far):
                rows[q] = stack[8 * n : 8 * n + 8]
    return jnp.concatenate(done, axis=0)


def split_bf16(v):
    high = v.astype(jnp.bfloat16)
    return high, (v - high.astype(jnp.float32)).astype(jnp.bfloat16)


def dot3(left, right, contract):
    dot = lambda a, b: lax.dot_general(
        a, b, (contract, ((), ())), preferred_element_type=jnp.float32
    )
    return dot(left[0], right[0]) + (dot(left[0], right[1]) + dot(left[1], right[0]))


def cut_kernel(info, blocks, near, far_a, far_b, sems):
    me = info[0]
    half = pl.ds((me // 2) * (W // 2), W // 2)
    copies = [
        pltpu.make_async_copy(blocks.at[me ^ 2, half], far_a, sems.at[0]),
        pltpu.make_async_copy(blocks.at[me ^ 3, half], far_b, sems.at[1]),
        pltpu.make_async_copy(blocks.at[me ^ 1], near, sems.at[2]),
    ]
    for c in copies:
        c.start()
    for c in copies:
        c.wait()


def factor_kernel(info, own_ref, r1, r2, r3, l0, l1, l2, l3, mt, a, l, sems):
    me = info[0]
    side = me // 2
    far_rows = pl.ds((1 - side) * (W // 2), W // 2)
    places = [a.at[me], a.at[me ^ 1], a.at[me ^ 2, far_rows], a.at[me ^ 3, far_rows]]
    ins = [own_ref.at[me], r1, r2, r3]
    copies = [pltpu.make_async_copy(ins[m], places[m], sems.at[m]) for m in range(NB)]
    for c in copies:
        c.start()
    for c in copies:
        c.wait()

    @pl.when(side == 1)
    def _():
        for j in range(NB // 2):
            for i in range(NB // 2, NB):
                a[j, pl.ds(i * B, B), :] = a[i, pl.ds(j * B, B), :].T

    row = lax.broadcasted_iota(jnp.int32, (B, B), 0)
    col = lax.broadcasted_iota(jnp.int32, (B, B), 1)
    l[...] = jnp.zeros_like(l)
    mt[...] = jnp.zeros_like(mt)
    eye = (row == col).astype(jnp.float32)
    for k in range(NB):
        here = pl.ds(k * B, B)
        inv = inverse_factor(a[k, here, :])
        l[k, here, :] = jnp.where(row >= col, dot_nt(a[k, here, :], inv), 0.0)
        for i in range(k + 1, NB):
            below = dot_nt(a[k, pl.ds(i * B, B), :], inv)
            l[k, pl.ds(i * B, B), :] = below
            for j in range(k + 1, i + 1):
                a[j, pl.ds(i * B, B), :] -= dot_nt(below, l[k, pl.ds(j * B, B), :])
        mt[k, here, :] = dot_nt(eye, inv)
        for i in range(k):
            total = dot_nt(mt[i, pl.ds(i * B, B), :], l[i, here, :])
            for j in range(i + 1, k):
                total = total + dot_nt(mt[j, pl.ds(i * B, B), :], l[j, here, :])
            mt[k, pl.ds(i * B, B), :] = dot_nt(-total, inv)
    outs = [l0, l1, l2, l3]
    copies = [pltpu.make_async_copy(l.at[me ^ m], outs[m], sems.at[m]) for m in range(NB)]
    for c in copies:
        c.start()
    for c in copies:
        c.wait()


def panel_kernel(
    info, counts, tgt_a, tgt_b, own_ref, r1, r2, r3, mt, l3, x0, x1, x2, x3, keep, send, xh, xl
):
    me = info[0]
    count = counts[me]
    rows = P_SIZE * B
    ins = [own_ref.at[me], r1, r2, r3]
    outs = [x0, x1, x2, x3]
    x3[pl.ds(rows, W), :] = l3[...]
    live = lax.broadcasted_iota(jnp.int32, (rows, B), 0) < count * B
    parts = [split_bf16(jnp.where(live, ref[...], 0.0)) for ref in ins]
    left = [jnp.concatenate([part[n] for part in parts], axis=1) for n in range(2)]
    for c in range(0, NB, 2):
        right = [
            jnp.concatenate([mt[me ^ m, pl.ds((me ^ k) * B, B), :] for m in (c, c + 1)], axis=1)
            for k in range(NB)
        ]
        got = dot3(left, split_bf16(jnp.concatenate(right, axis=0)), ((1,), (0,)))
        outs[c][pl.ds(0, rows), :] = got[:, :B]
        outs[c + 1][pl.ds(0, rows), :] = got[:, B:]
        high, low = split_bf16(got)
        xh[:, pl.ds(c * B, 2 * B)] = high
        xl[:, pl.ds(c * B, 2 * B)] = low

    keep[...] = jnp.zeros_like(keep)
    send[...] = jnp.zeros_like(send)
    half, strip = keep.shape[1:3]
    for j in range(0, P_SIZE, 2):

        @pl.when(j < count)
        def _():
            left = (xh[pl.ds(j * B, rows - j * B), :], xl[pl.ds(j * B, rows - j * B), :])
            right = (xh[pl.ds(j * B, 2 * B), :], xl[pl.ds(j * B, 2 * B), :])
            got = dot3(left, right, ((1,), (1,)))
            for i in range(j, P_SIZE):
                for n in range(2 if i > j else 1):
                    block = got[(i - j) * B : (i - j + 1) * B, n * B : (n + 1) * B]
                    pair = i * (i + 1) // 2 + j + n
                    away = (tgt_a[pair] >= half).astype(jnp.float32)
                    for stream, tgt in enumerate((tgt_a, tgt_b)):
                        at = lax.rem(tgt[pair], half)
                        piece = block[stream * strip : (stream + 1) * strip]
                        keep[stream, at] += piece * (1.0 - away)
                        send[stream, at] += piece * away


SMEM = pl.BlockSpec(memory_space=pltpu.SMEM)
ANY = pl.BlockSpec(memory_space=pl.ANY)
VMEM = pl.BlockSpec(memory_space=pltpu.VMEM)


def xor_pairs(size, mask):
    return [(i, i ^ mask) for i in range(size)]


def log2(n):
    return n.bit_length() - 1


def swap(x, axis, mask):
    return lax.ppermute(x, axis, xor_pairs(lax.axis_size(axis), mask))


def relative_index(owner, slot, wide_me, narrow_me, steps):
    away = {"wide": owner ^ wide_me, "narrow": (slot // T_DEV) ^ narrow_me}
    index = jnp.zeros_like(owner)
    for axis, mask in steps:
        index = index * 2 + ((away[axis] // mask) & 1)
    return index * T_DEV + slot % T_DEV


def local(diag_block, panel, panel_count, pair_owner, pair_slot, ancestor):
    narrow_count = lax.axis_size("narrow")
    wide_count = lax.axis_size("wide")
    me = lax.axis_index("narrow")
    wide_me = lax.axis_index("wide")
    assert narrow_count == NB and diag_block.shape[0] == NB
    masks = range(1, NB)
    own = lambda x, m: lax.dynamic_index_in_dim(x, me ^ m, 0, keepdims=False)
    info = me.astype(jnp.int32).reshape(1)
    cut = [jax.ShapeDtypeStruct((rows, B), jnp.float32) for rows in (W, W // 2, W // 2)]
    cut = pl.pallas_call(
        cut_kernel,
        out_shape=cut,
        in_specs=[SMEM, pl.BlockSpec(memory_space=pltpu.HBM)],
        out_specs=[VMEM] * 3,
        scratch_shapes=[pltpu.SemaphoreType.DMA((3,))],
        compiler_params=pltpu.CompilerParams(vmem_limit_bytes=8 * 2**20),
        cost_estimate=pl.CostEstimate(flops=0, bytes_accessed=2**20, transcendentals=0),
        name="cut",
    )(info, diag_block)
    diag_in = [swap(part, "narrow", m) for m, part in zip(masks, cut)]
    panel_out = [own(panel, m) for m in masks]
    diag_in, panel_out = lax.optimization_barrier((diag_in, panel_out))
    panel_in = [swap(panel_out[m - 1], "narrow", m) for m in masks]

    narrow_steps = [("narrow", 1 << b) for b in range(log2(narrow_count))]
    wide_steps = [("wide", 1 << b) for b in range(log2(wide_count))]
    first, last = narrow_steps[:1], wide_steps[2:] + narrow_steps[1:]
    steps_a = first + wide_steps[:2] + last
    steps_b = first + wide_steps[1::-1] + last
    owner = lax.dynamic_slice_in_dim(pair_owner[:, 0], me * NPAIR, NPAIR)
    slot = lax.dynamic_slice_in_dim(pair_slot, me * NPAIR, NPAIR)
    tgt_a = relative_index(owner, slot, wide_me, me, steps_a)
    tgt_b = relative_index(owner, slot, wide_me, me, steps_b)

    slab = jax.ShapeDtypeStruct((W, B), jnp.float32)
    *l_parts, mt = pl.pallas_call(
        factor_kernel,
        out_shape=[slab] * NB + [jax.ShapeDtypeStruct((NB, W, B), jnp.float32)],
        in_specs=[SMEM] + [ANY] * NB,
        out_specs=[ANY] * NB + [VMEM],
        scratch_shapes=[pltpu.VMEM((NB, W, B), jnp.float32)] * 2 + [pltpu.SemaphoreType.DMA((NB,))],
        compiler_params=pltpu.CompilerParams(vmem_limit_bytes=32 * 2**20),
        cost_estimate=pl.CostEstimate(flops=2 * 10**8, bytes_accessed=4 * 10**6, transcendentals=0),
        name="factor",
    )(info, diag_block, *diag_in)

    rows = P_SIZE * B
    blocks = wide_count * narrow_count * T_DEV
    slab = jax.ShapeDtypeStruct((rows, B), jnp.float32)
    longer = jax.ShapeDtypeStruct((rows + W, B), jnp.float32)
    part = jax.ShapeDtypeStruct((2, blocks // 2, B // 2, B), jnp.float32)
    *x_parts, keep, send = pl.pallas_call(
        panel_kernel,
        out_shape=[slab] * (NB - 1) + [longer, part, part],
        in_specs=[SMEM] * 4 + [VMEM] * (NB + 2),
        out_specs=[VMEM] * (NB + 2),
        scratch_shapes=[pltpu.VMEM((rows, W), jnp.bfloat16)] * 2,
        compiler_params=pltpu.CompilerParams(vmem_limit_bytes=20 * 2**20 + 4 * blocks * B * B),
        cost_estimate=pl.CostEstimate(flops=10**9, bytes_accessed=10 * 10**6, transcendentals=0),
        name="panel",
    )(info, panel_count, tgt_a, tgt_b, panel, *panel_in, mt, l_parts[3])

    l_back = [swap(l_parts[m], "narrow", m) for m in (1, 2)]
    x_back = [swap(x_parts[m], "narrow", m) for m in masks]

    send, l_back[1] = lax.optimization_barrier((send, l_back[1]))
    got = swap(send, "narrow", 1)
    half = blocks // 4
    upper = lambda u, n: u[n, half:]
    lower = lambda u, n: u[n, :half]
    send_a = upper(keep, 0) + upper(got, 0)
    send_b = upper(keep, 1) + upper(got, 1)
    keep_a = lower(keep, 0) + lower(got, 0)
    keep_b = lower(keep, 1) + lower(got, 1)
    for n in (1, 2):
        if n == 2:
            send_a, send_b, x_back[1] = lax.optimization_barrier((send_a, send_b, x_back[1]))
        else:
            send_a, send_b = lax.optimization_barrier((send_a, send_b))
        got_a = swap(send_a, *steps_a[n])
        got_b = swap(send_b, *steps_b[n])
        half = half // 2
        if n == 1:
            send_a, send_b = keep_a[half:] + got_a[half:], keep_b[half:] + got_b[half:]
            keep_a, keep_b = keep_a[:half] + got_a[:half], keep_b[:half] + got_b[:half]
    rest = steps_a[3:]
    take = lambda n, size: jnp.concatenate(
        [u[n * size : (n + 1) * size] + v[n * size : (n + 1) * size] for u, v in ((keep_a, got_a), (keep_b, got_b))],
        axis=1,
    )
    while len(rest) > 2:
        got = swap(take(1, half), *rest.pop(0))
        keep_a = take(0, half) + got
        half = half // 2
        keep_a, keep_b = keep_a[:, : B // 2], keep_a[:, B // 2 :]
        got_a, got_b = jnp.zeros_like(keep_a), jnp.zeros_like(keep_b)
    (_, wide_mask), (_, narrow_mask) = rest
    both = wide_mask * narrow_count + narrow_mask
    got = [
        lax.ppermute(take(3, T_DEV), ("wide", "narrow"), xor_pairs(wide_count * narrow_count, both)),
        swap(take(2, T_DEV), *rest[0]),
        swap(take(1, T_DEV), *rest[1]),
    ]
    got, x_back[2], x_back[0] = lax.optimization_barrier((got, x_back[2], x_back[0]))
    l_back.append(x_back[2][rows:])
    x_back[2] = x_back[2][:rows]
    updated = ancestor - (take(0, T_DEV) + (got[0] + (got[1] + got[2])))

    def give_back(own_part, others):
        back = [own_part] + others
        out = jnp.zeros((NB,) + own_part.shape, jnp.float32)
        for m in range(NB):
            out = lax.dynamic_update_index_in_dim(out, back[m], me ^ m, 0)
        return out

    return (give_back(l_parts[0], l_back), give_back(x_parts[0], x_back), updated)


def solution(mesh):
    placed = (
        P("wide", None, "narrow"),
        P("wide", None, "narrow"),
        P("wide"),
        P("wide", None),
        P("wide"),
        P(("wide", "narrow"), None, None),
    )
    return jax.shard_map(
        local,
        mesh=mesh,
        in_specs=placed,
        out_specs=(
            P("wide", None, "narrow"),
            P("wide", None, "narrow"),
            P(("wide", "narrow"), None, None),
        ),
        check_vma=False,
    )
```

```python
import jax
import jax.numpy as jnp
import numpy as np
from jax import lax
from jax.experimental import pallas as pl
from jax.experimental.pallas import tpu as pltpu
from jax.sharding import PartitionSpec as P

W = 512
B = 128
P_SIZE = 8
T_DEV = 2
NB = W // B
NPAIR = P_SIZE * (P_SIZE + 1) // 2
HIGHEST = lax.Precision.HIGHEST


def dot_nt(a, b):
    return lax.dot_general(
        a, b, (((1,), (1,)), ((), ())), precision=HIGHEST, preferred_element_type=jnp.float32
    )


def dot_nn(a, b):
    return lax.dot_general(
        a, b, (((1,), (0,)), ((), ())), precision=HIGHEST, preferred_element_type=jnp.float32
    )


def lane_of(x, c):
    return jnp.broadcast_to(x[:, c : c + 1], x.shape)


def row_of(x, r):
    return jnp.broadcast_to(x[r : r + 1, :], x.shape)


def inverse_factor(block):
    sub = lax.broadcasted_iota(jnp.int32, (8, B), 0)
    lane = lax.broadcasted_iota(jnp.int32, (8, B), 1)
    total, strip = B // 8, 2
    rows = [block[8 * q : 8 * q + 8, :] for q in range(total)]
    done = [None] * total
    for b in range(0, total, strip):
        mine = range(b, b + strip)
        near = range(b + strip, min(b + 2 * strip, total))
        far = range(b + 2 * strip, total)
        in_strip = (lane >= 8 * b) & (lane < 8 * (b + strip))
        ahead = {q: [lane_of(rows[q], 8 * b + m) for m in range(8 * strip)] for q in near}
        for p in mine:
            lo = 8 * p
            own = (lane >= lo) & (lane < lo + 8)
            cols = [lane_of(rows[p], lo + m) for m in range(8)]
            others = [q for q in mine if q != p]
            mult = {q: [lane_of(rows[q], lo + m) for m in range(8)] for q in others}
            work = jnp.where(own, (lane - lo == sub).astype(jnp.float32), rows[p])
            final = jnp.zeros((8, B), jnp.float32)
            for k in range(0, 8, 2):
                f0, f1 = cols[k], cols[k + 1]
                a, h, c = row_of(f0, k), row_of(f0, k + 1), row_of(f1, k + 1)
                det = a * c - h * h
                recip = 1.0 / det
                ar, hr, cr = a * recip, h * recip, c * recip
                first, second = sub == k, sub == k + 1

                def eliminate(v):
                    r0, r1 = row_of(v, k), row_of(v, k + 1)
                    s0, s1 = cr * r0 - hr * r1, ar * r1 - hr * r0
                    return r0, r1, jnp.where(first, s0, jnp.where(second, s1, v - f0 * s0 - f1 * s1))

                for m in range(k + 2, 8):
                    cols[m] = eliminate(cols[m])[2]
                r0, r1, work = eliminate(work)
                root = lax.rsqrt(a)
                lower = (a * r1 - h * r0) * (root * lax.rsqrt(det))
                final = jnp.where(first, r0 * root, jnp.where(second, lower, final))
            done[p] = jnp.where(lane <= sub + lo, final, 0.0)
            rows[p] = work
            lines = [row_of(work, m) for m in range(8)]
            for q in others:
                new = jnp.where(own, 0.0, rows[q])
                for m in range(8):
                    new = new - mult[q][m] * lines[m]
                rows[q] = new
        lines = [row_of(rows[q], m) for q in mine for m in range(8)]
        for q in near:
            parts = [ahead[q][m] * lines[m] for m in range(4)]
            for m in range(4, 8 * strip):
                parts[m % 4] = parts[m % 4] + ahead[q][m] * lines[m]
            rows[q] = jnp.where(in_strip, 0.0, rows[q]) - ((parts[0] + parts[1]) + (parts[2] + parts[3]))
        if far:
            stack = jnp.concatenate([rows[q] for q in far], axis=0)
            lane_far = lax.broadcasted_iota(jnp.int32, stack.shape, 1)
            in_far = (lane_far >= 8 * b) & (lane_far < 8 * (b + strip))
            zero = jnp.zeros((8, B), jnp.float32)
            tall = jnp.concatenate([rows[q] if q in mine else zero for q in range(total)], axis=0)
            stack = jnp.where(in_far, 0.0, stack) - dot_nn(jnp.where(in_far, stack, 0.0), tall)
            for n, q in enumerate(far):
                rows[q] = stack[8 * n : 8 * n + 8]
    return jnp.concatenate(done, axis=0)


def split_bf16(v):
    high = v.astype(jnp.bfloat16)
    return high, (v - high.astype(jnp.float32)).astype(jnp.bfloat16)


def dot3(left, right, contract):
    dot = lambda a, b: lax.dot_general(
        a, b, (contract, ((), ())), preferred_element_type=jnp.float32
    )
    return dot(left[0], right[0]) + (dot(left[0], right[1]) + dot(left[1], right[0]))


def cut_kernel(info, blocks, near, far_a, far_b, sems):
    me = info[0]
    half = pl.ds((me // 2) * (W // 2), W // 2)
    copies = [
        pltpu.make_async_copy(blocks.at[me ^ 2, half], far_a, sems.at[0]),
        pltpu.make_async_copy(blocks.at[me ^ 3, half], far_b, sems.at[1]),
        pltpu.make_async_copy(blocks.at[me ^ 1], near, sems.at[2]),
    ]
    for c in copies:
        c.start()
    for c in copies:
        c.wait()


def factor_kernel(info, own_ref, r1, r2, r3, l0, l1, l2, l3a, l3b, mt, a, l, sems):
    me = info[0]
    side = me // 2
    far_rows = pl.ds((1 - side) * (W // 2), W // 2)
    places = [a.at[me], a.at[me ^ 1], a.at[me ^ 2, far_rows], a.at[me ^ 3, far_rows]]
    ins = [own_ref.at[me], r1, r2, r3]
    copies = [pltpu.make_async_copy(ins[m], places[m], sems.at[m]) for m in range(NB)]
    for c in copies:
        c.start()
    for c in copies:
        c.wait()

    @pl.when(side == 1)
    def _():
        for j in range(NB // 2):
            for i in range(NB // 2, NB):
                a[j, pl.ds(i * B, B), :] = a[i, pl.ds(j * B, B), :].T

    row = lax.broadcasted_iota(jnp.int32, (B, B), 0)
    col = lax.broadcasted_iota(jnp.int32, (B, B), 1)
    l[...] = jnp.zeros_like(l)
    mt[...] = jnp.zeros_like(mt)
    eye = (row == col).astype(jnp.float32)
    for k in range(NB):
        here = pl.ds(k * B, B)
        inv = inverse_factor(a[k, here, :])
        l[k, here, :] = jnp.where(row >= col, dot_nt(a[k, here, :], inv), 0.0)
        for i in range(k + 1, NB):
            below = dot_nt(a[k, pl.ds(i * B, B), :], inv)
            l[k, pl.ds(i * B, B), :] = below
            for j in range(k + 1, i + 1):
                a[j, pl.ds(i * B, B), :] -= dot_nt(below, l[k, pl.ds(j * B, B), :])
        mt[k, here, :] = dot_nt(eye, inv)
        for i in range(k):
            total = dot_nt(mt[i, pl.ds(i * B, B), :], l[i, here, :])
            for j in range(i + 1, k):
                total = total + dot_nt(mt[j, pl.ds(i * B, B), :], l[j, here, :])
            mt[k, pl.ds(i * B, B), :] = dot_nt(-total, inv)
    copies = [pltpu.make_async_copy(l.at[me ^ m], out, sems.at[m]) for m, out in enumerate((l0, l1, l2))]
    for n, out in enumerate((l3a, l3b)):
        piece = l.at[me ^ 3, pl.ds(n * (W // 2), W // 2)]
        copies.append(pltpu.make_async_copy(piece, out, sems.at[3 + n]))
    for c in copies:
        c.start()
    for c in copies:
        c.wait()


def add_pairs(xh, xl, tgt, stream, keep, send):
    keep[...] = jnp.zeros_like(keep)
    send[...] = jnp.zeros_like(send)
    half, strip = keep.shape[:2]
    for j in range(0, P_SIZE, 2):
        places = [pl.ds(i * B + stream * strip, strip) for i in range(j, P_SIZE)]
        left = [jnp.concatenate([ref[at, :] for at in places], axis=0) for ref in (xh, xl)]
        right = [ref[pl.ds(j * B, 2 * B), :] for ref in (xh, xl)]
        got = dot3(left, right, ((1,), (1,)))
        for i in range(j, P_SIZE):
            for n in range(2 if i > j else 1):
                piece = got[(i - j) * strip : (i - j + 1) * strip, n * B : (n + 1) * B]
                where = tgt[i * (i + 1) // 2 + j + n]
                away = (where >= half).astype(jnp.float32)
                at = lax.rem(where, half)
                keep[at] += piece * (1.0 - away)
                send[at] += piece * away


def panel_kernel(info, counts, tgt, own_ref, r1, r2, r3, mt, l3b, x0, x1, x2, x3, xh, xl, keep, send):
    me = info[0]
    count = counts[me]
    rows = P_SIZE * B
    ins = [own_ref.at[me], r1, r2, r3]
    outs = [x0, x1, x2, x3]
    x3[pl.ds(rows, W // 2), :] = l3b[...]
    live = lax.broadcasted_iota(jnp.int32, (rows, B), 0) < count * B
    parts = [split_bf16(jnp.where(live, ref[...], 0.0)) for ref in ins]
    left = [jnp.concatenate([part[n] for part in parts], axis=1) for n in range(2)]
    for c in range(0, NB, 2):
        right = [
            jnp.concatenate([mt[me ^ m, pl.ds((me ^ k) * B, B), :] for m in (c, c + 1)], axis=1)
            for k in range(NB)
        ]
        got = dot3(left, split_bf16(jnp.concatenate(right, axis=0)), ((1,), (0,)))
        outs[c][pl.ds(0, rows), :] = got[:, :B]
        outs[c + 1][pl.ds(0, rows), :] = got[:, B:]
        high, low = split_bf16(got)
        xh[:, pl.ds(c * B, 2 * B)] = high
        xl[:, pl.ds(c * B, 2 * B)] = low
    add_pairs(xh, xl, tgt, 0, keep, send)


def second_kernel(tgt, xh, xl, keep, send):
    add_pairs(xh, xl, tgt, 1, keep, send)


SMEM = pl.BlockSpec(memory_space=pltpu.SMEM)
ANY = pl.BlockSpec(memory_space=pl.ANY)
VMEM = pl.BlockSpec(memory_space=pltpu.VMEM)


def xor_pairs(size, mask):
    return [(i, i ^ mask) for i in range(size)]


def log2(n):
    return n.bit_length() - 1


def swap(x, axis, mask):
    return lax.ppermute(x, axis, xor_pairs(lax.axis_size(axis), mask))


def relative_index(owner, slot, wide_me, narrow_me, steps):
    away = {"wide": owner ^ wide_me, "narrow": (slot // T_DEV) ^ narrow_me}
    index = jnp.zeros_like(owner)
    for axis, mask in steps:
        index = index * 2 + ((away[axis] // mask) & 1)
    return index * T_DEV + slot % T_DEV


def local(diag_block, panel, panel_count, pair_owner, pair_slot, ancestor):
    narrow_count = lax.axis_size("narrow")
    wide_count = lax.axis_size("wide")
    me = lax.axis_index("narrow")
    wide_me = lax.axis_index("wide")
    assert narrow_count == NB and diag_block.shape[0] == NB
    masks = range(1, NB)
    own = lambda x, m: lax.dynamic_index_in_dim(x, me ^ m, 0, keepdims=False)
    info = me.astype(jnp.int32).reshape(1)
    cut = [jax.ShapeDtypeStruct((rows, B), jnp.float32) for rows in (W, W // 2, W // 2)]
    cut = pl.pallas_call(
        cut_kernel,
        out_shape=cut,
        in_specs=[SMEM, pl.BlockSpec(memory_space=pltpu.HBM)],
        out_specs=[VMEM] * 3,
        scratch_shapes=[pltpu.SemaphoreType.DMA((3,))],
        compiler_params=pltpu.CompilerParams(vmem_limit_bytes=8 * 2**20),
        cost_estimate=pl.CostEstimate(flops=0, bytes_accessed=2**20, transcendentals=0),
        name="cut",
    )(info, diag_block)
    diag_in = [swap(part, "narrow", m) for m, part in zip(masks, cut)]
    panel_out = [own(panel, m) for m in masks]
    diag_in, panel_out = lax.optimization_barrier((diag_in, panel_out))
    panel_in = [swap(panel_out[m - 1], "narrow", m) for m in masks]

    narrow_steps = [("narrow", 1 << b) for b in range(log2(narrow_count))]
    wide_steps = [("wide", 1 << b) for b in range(log2(wide_count))]
    first, last = narrow_steps[:1], wide_steps[2:] + narrow_steps[1:]
    steps_a = first + wide_steps[:2] + last
    steps_b = first + wide_steps[1::-1] + last
    owner = lax.dynamic_slice_in_dim(pair_owner[:, 0], me * NPAIR, NPAIR)
    slot = lax.dynamic_slice_in_dim(pair_slot, me * NPAIR, NPAIR)
    tgt_a = relative_index(owner, slot, wide_me, me, steps_a)
    tgt_b = relative_index(owner, slot, wide_me, me, steps_b)

    slab = jax.ShapeDtypeStruct((W, B), jnp.float32)
    low = jax.ShapeDtypeStruct((W // 2, B), jnp.float32)
    *l_parts, mt = pl.pallas_call(
        factor_kernel,
        out_shape=[slab] * (NB - 1) + [low, low, jax.ShapeDtypeStruct((NB, W, B), jnp.float32)],
        in_specs=[SMEM] + [ANY] * NB,
        out_specs=[ANY] * (NB + 1) + [VMEM],
        scratch_shapes=[pltpu.VMEM((NB, W, B), jnp.float32)] * 2 + [pltpu.SemaphoreType.DMA((NB + 1,))],
        compiler_params=pltpu.CompilerParams(vmem_limit_bytes=32 * 2**20),
        cost_estimate=pl.CostEstimate(flops=2 * 10**8, bytes_accessed=4 * 10**6, transcendentals=0),
        name="factor",
    )(info, diag_block, *diag_in)

    rows = P_SIZE * B
    blocks = wide_count * narrow_count * T_DEV
    slab = jax.ShapeDtypeStruct((rows, B), jnp.float32)
    longer = jax.ShapeDtypeStruct((rows + W // 2, B), jnp.float32)
    split = jax.ShapeDtypeStruct((rows, W), jnp.bfloat16)
    part = jax.ShapeDtypeStruct((blocks // 2, B // 2, B), jnp.float32)
    room = pltpu.CompilerParams(vmem_limit_bytes=20 * 2**20 + 4 * blocks * B * B)
    *x_parts, xh, xl, keep_a, send_a = pl.pallas_call(
        panel_kernel,
        out_shape=[slab] * (NB - 1) + [longer, split, split, part, part],
        in_specs=[SMEM] * 3 + [VMEM] * (NB + 2),
        out_specs=[VMEM] * (NB + 4),
        compiler_params=room,
        cost_estimate=pl.CostEstimate(flops=10**9, bytes_accessed=10 * 10**6, transcendentals=0),
        name="panel",
    )(info, panel_count, tgt_a, panel, *panel_in, mt, l_parts[4])
    keep_b, send_b = pl.pallas_call(
        second_kernel,
        out_shape=[part, part],
        in_specs=[SMEM] + [VMEM] * 2,
        out_specs=[VMEM] * 2,
        compiler_params=room,
        cost_estimate=pl.CostEstimate(flops=10**6, bytes_accessed=10**4, transcendentals=0),
        name="second",
    )(tgt_b, xh, xl)

    l_back = [swap(l_parts[m], "narrow", m) for m in (1, 2, 3)]
    x_back = [swap(x_parts[m], "narrow", m) for m in masks]

    got_a = swap(send_a, "narrow", 1)
    send_b, l_back[1] = lax.optimization_barrier((send_b, l_back[1]))
    got_b = swap(send_b, "narrow", 1)
    half = blocks // 4
    send_a, send_b = keep_a[half:] + got_a[half:], keep_b[half:] + got_b[half:]
    keep_a, keep_b = keep_a[:half] + got_a[:half], keep_b[:half] + got_b[:half]
    got_a = swap(send_a, *steps_a[1])
    send_b, l_back[2] = lax.optimization_barrier((send_b, l_back[2]))
    got_b = swap(send_b, *steps_b[1])
    half = half // 2
    send_a, send_b = keep_a[half:] + got_a[half:], keep_b[half:] + got_b[half:]
    keep_a, keep_b = keep_a[:half] + got_a[:half], keep_b[:half] + got_b[:half]
    send_a, send_b, x_back[1] = lax.optimization_barrier((send_a, send_b, x_back[1]))
    got_a = swap(send_a, *steps_a[2])
    got_b = swap(send_b, *steps_b[2])
    half = half // 2
    rest = steps_a[3:]
    take = lambda n, size: jnp.concatenate(
        [u[n * size : (n + 1) * size] + v[n * size : (n + 1) * size] for u, v in ((keep_a, got_a), (keep_b, got_b))],
        axis=1,
    )
    while len(rest) > 2:
        got = swap(take(1, half), *rest.pop(0))
        keep_a = take(0, half) + got
        half = half // 2
        keep_a, keep_b = keep_a[:, : B // 2], keep_a[:, B // 2 :]
        got_a, got_b = jnp.zeros_like(keep_a), jnp.zeros_like(keep_b)
    (_, wide_mask), (_, narrow_mask) = rest
    both = wide_mask * narrow_count + narrow_mask
    got = [
        lax.ppermute(take(3, T_DEV), ("wide", "narrow"), xor_pairs(wide_count * narrow_count, both)),
        swap(take(2, T_DEV), *rest[0]),
        swap(take(1, T_DEV), *rest[1]),
    ]
    got, x_back[2], x_back[0] = lax.optimization_barrier((got, x_back[2], x_back[0]))
    l_back[2] = jnp.concatenate([l_back[2], x_back[2][rows:]], axis=0)
    x_back[2] = x_back[2][:rows]
    updated = ancestor - (take(0, T_DEV) + (got[0] + (got[1] + got[2])))

    def give_back(own_part, others):
        back = [own_part] + others
        out = jnp.zeros((NB,) + own_part.shape, jnp.float32)
        for m in range(NB):
            out = lax.dynamic_update_index_in_dim(out, back[m], me ^ m, 0)
        return out

    return (give_back(l_parts[0], l_back), give_back(x_parts[0], x_back), updated)


def solution(mesh):
    placed = (
        P("wide", None, "narrow"),
        P("wide", None, "narrow"),
        P("wide"),
        P("wide", None),
        P("wide"),
        P(("wide", "narrow"), None, None),
    )
    return jax.shard_map(
        local,
        mesh=mesh,
        in_specs=placed,
        out_specs=(
            P("wide", None, "narrow"),
            P("wide", None, "narrow"),
            P(("wide", "narrow"), None, None),
        ),
        check_vma=False,
    )
```

```python
import jax
import jax.numpy as jnp
import numpy as np
from jax import lax
from jax.experimental import pallas as pl
from jax.experimental.pallas import tpu as pltpu
from jax.sharding import PartitionSpec as P

W = 512
B = 128
P_SIZE = 8
T_DEV = 2
NB = W // B
NPAIR = P_SIZE * (P_SIZE + 1) // 2
HIGHEST = lax.Precision.HIGHEST


def dot_nt(a, b):
    return lax.dot_general(
        a, b, (((1,), (1,)), ((), ())), precision=HIGHEST, preferred_element_type=jnp.float32
    )


def dot_nn(a, b):
    return lax.dot_general(
        a, b, (((1,), (0,)), ((), ())), precision=HIGHEST, preferred_element_type=jnp.float32
    )


def lane_of(x, c):
    return jnp.broadcast_to(x[:, c : c + 1], x.shape)


def row_of(x, r):
    return jnp.broadcast_to(x[r : r + 1, :], x.shape)


def inverse_factor(block):
    sub = lax.broadcasted_iota(jnp.int32, (8, B), 0)
    lane = lax.broadcasted_iota(jnp.int32, (8, B), 1)
    total, strip = B // 8, 2
    rows = [block[8 * q : 8 * q + 8, :] for q in range(total)]
    done = [None] * total
    for b in range(0, total, strip):
        mine = range(b, b + strip)
        near = range(b + strip, min(b + 2 * strip, total))
        far = range(b + 2 * strip, total)
        in_strip = (lane >= 8 * b) & (lane < 8 * (b + strip))
        ahead = {q: [lane_of(rows[q], 8 * b + m) for m in range(8 * strip)] for q in near}
        for p in mine:
            lo = 8 * p
            own = (lane >= lo) & (lane < lo + 8)
            cols = [lane_of(rows[p], lo + m) for m in range(8)]
            others = [q for q in mine if q != p]
            mult = {q: [lane_of(rows[q], lo + m) for m in range(8)] for q in others}
            work = jnp.where(own, (lane - lo == sub).astype(jnp.float32), rows[p])
            final = jnp.zeros((8, B), jnp.float32)
            for k in range(0, 8, 2):
                f0, f1 = cols[k], cols[k + 1]
                a, h, c = row_of(f0, k), row_of(f0, k + 1), row_of(f1, k + 1)
                det = a * c - h * h
                recip = 1.0 / det
                ar, hr, cr = a * recip, h * recip, c * recip
                first, second = sub == k, sub == k + 1

                def eliminate(v):
                    r0, r1 = row_of(v, k), row_of(v, k + 1)
                    s0, s1 = cr * r0 - hr * r1, ar * r1 - hr * r0
                    return r0, r1, jnp.where(first, s0, jnp.where(second, s1, v - f0 * s0 - f1 * s1))

                for m in range(k + 2, 8):
                    cols[m] = eliminate(cols[m])[2]
                r0, r1, work = eliminate(work)
                root = lax.rsqrt(a)
                lower = (a * r1 - h * r0) * (root * lax.rsqrt(det))
                final = jnp.where(first, r0 * root, jnp.where(second, lower, final))
            done[p] = jnp.where(lane <= sub + lo, final, 0.0)
            rows[p] = work
            lines = [row_of(work, m) for m in range(8)]
            for q in others:
                new = jnp.where(own, 0.0, rows[q])
                for m in range(8):
                    new = new - mult[q][m] * lines[m]
                rows[q] = new
        lines = [row_of(rows[q], m) for q in mine for m in range(8)]
        for q in near:
            parts = [ahead[q][m] * lines[m] for m in range(4)]
            for m in range(4, 8 * strip):
                parts[m % 4] = parts[m % 4] + ahead[q][m] * lines[m]
            rows[q] = jnp.where(in_strip, 0.0, rows[q]) - ((parts[0] + parts[1]) + (parts[2] + parts[3]))
        if far:
            stack = jnp.concatenate([rows[q] for q in far], axis=0)
            lane_far = lax.broadcasted_iota(jnp.int32, stack.shape, 1)
            in_far = (lane_far >= 8 * b) & (lane_far < 8 * (b + strip))
            zero = jnp.zeros((8, B), jnp.float32)
            tall = jnp.concatenate([rows[q] if q in mine else zero for q in range(total)], axis=0)
            stack = jnp.where(in_far, 0.0, stack) - dot_nn(jnp.where(in_far, stack, 0.0), tall)
            for n, q in enumerate(far):
                rows[q] = stack[8 * n : 8 * n + 8]
    return jnp.concatenate(done, axis=0)


def split_bf16(v):
    high = v.astype(jnp.bfloat16)
    return high, (v - high.astype(jnp.float32)).astype(jnp.bfloat16)


def dot3(left, right, contract):
    dot = lambda a, b: lax.dot_general(
        a, b, (contract, ((), ())), preferred_element_type=jnp.float32
    )
    return dot(left[0], right[0]) + (dot(left[0], right[1]) + dot(left[1], right[0]))


def cut_kernel(info, blocks, near, far_a, far_b, sems):
    me = info[0]
    half = pl.ds((me // 2) * (W // 2), W // 2)
    copies = [
        pltpu.make_async_copy(blocks.at[me ^ 2, half], far_a, sems.at[0]),
        pltpu.make_async_copy(blocks.at[me ^ 3, half], far_b, sems.at[1]),
        pltpu.make_async_copy(blocks.at[me ^ 1], near, sems.at[2]),
    ]
    for c in copies:
        c.start()
    for c in copies:
        c.wait()


def factor_kernel(info, own_ref, r1, r2, r3, l0, l1, l2, l3a, l3b, mt, a, l, sems):
    me = info[0]
    side = me // 2
    far_rows = pl.ds((1 - side) * (W // 2), W // 2)
    places = [a.at[me], a.at[me ^ 1], a.at[me ^ 2, far_rows], a.at[me ^ 3, far_rows]]
    ins = [own_ref.at[me], r1, r2, r3]
    copies = [pltpu.make_async_copy(ins[m], places[m], sems.at[m]) for m in range(NB)]
    for c in copies:
        c.start()
    for c in copies:
        c.wait()

    @pl.when(side == 1)
    def _():
        for j in range(NB // 2):
            for i in range(NB // 2, NB):
                a[j, pl.ds(i * B, B), :] = a[i, pl.ds(j * B, B), :].T

    row = lax.broadcasted_iota(jnp.int32, (B, B), 0)
    col = lax.broadcasted_iota(jnp.int32, (B, B), 1)
    l[...] = jnp.zeros_like(l)
    mt[...] = jnp.zeros_like(mt)
    eye = (row == col).astype(jnp.float32)
    for k in range(NB):
        here = pl.ds(k * B, B)
        inv = inverse_factor(a[k, here, :])
        l[k, here, :] = jnp.where(row >= col, dot_nt(a[k, here, :], inv), 0.0)
        for i in range(k + 1, NB):
            below = dot_nt(a[k, pl.ds(i * B, B), :], inv)
            l[k, pl.ds(i * B, B), :] = below
            for j in range(k + 1, i + 1):
                a[j, pl.ds(i * B, B), :] -= dot_nt(below, l[k, pl.ds(j * B, B), :])
        mt[k, here, :] = dot_nt(eye, inv)
        for i in range(k):
            total = dot_nt(mt[i, pl.ds(i * B, B), :], l[i, here, :])
            for j in range(i + 1, k):
                total = total + dot_nt(mt[j, pl.ds(i * B, B), :], l[j, here, :])
            mt[k, pl.ds(i * B, B), :] = dot_nt(-total, inv)
    copies = [pltpu.make_async_copy(l.at[me ^ m], out, sems.at[m]) for m, out in enumerate((l0, l1, l2))]
    for n, out in enumerate((l3a, l3b)):
        piece = l.at[me ^ 3, pl.ds(n * (W // 2), W // 2)]
        copies.append(pltpu.make_async_copy(piece, out, sems.at[3 + n]))
    for c in copies:
        c.start()
    for c in copies:
        c.wait()


def panel_kernel(
    info, counts, tgt_a, tgt_b, own_ref, r1, r2, r3, mt, l3a, x0, x1, x2, x3a, x3b, keep, send, xh, xl
):
    me = info[0]
    count = counts[me]
    rows = P_SIZE * B
    ins = [own_ref.at[me], r1, r2, r3]
    lead = x3a.shape[0]
    x3b[pl.ds(rows - lead, W // 2), :] = l3a[...]
    live = lax.broadcasted_iota(jnp.int32, (rows, B), 0) < count * B
    parts = [split_bf16(jnp.where(live, ref[...], 0.0)) for ref in ins]
    left = [jnp.concatenate([part[n] for part in parts], axis=1) for n in range(2)]
    for c in range(0, NB, 2):
        right = [
            jnp.concatenate([mt[me ^ m, pl.ds((me ^ k) * B, B), :] for m in (c, c + 1)], axis=1)
            for k in range(NB)
        ]
        got = dot3(left, split_bf16(jnp.concatenate(right, axis=0)), ((1,), (0,)))
        if c == 0:
            x0[...] = got[:, :B]
            x1[...] = got[:, B:]
        else:
            x2[...] = got[:, :B]
            x3a[...] = got[:lead, B:]
            x3b[pl.ds(0, rows - lead), :] = got[lead:, B:]
        high, low = split_bf16(got)
        xh[:, pl.ds(c * B, 2 * B)] = high
        xl[:, pl.ds(c * B, 2 * B)] = low

    keep[...] = jnp.zeros_like(keep)
    send[...] = jnp.zeros_like(send)
    half, strip = keep.shape[1:3]
    for j in range(0, P_SIZE, 2):

        @pl.when(j < count)
        def _():
            left = (xh[pl.ds(j * B, rows - j * B), :], xl[pl.ds(j * B, rows - j * B), :])
            right = (xh[pl.ds(j * B, 2 * B), :], xl[pl.ds(j * B, 2 * B), :])
            got = dot3(left, right, ((1,), (1,)))
            for i in range(j, P_SIZE):
                for n in range(2 if i > j else 1):
                    block = got[(i - j) * B : (i - j + 1) * B, n * B : (n + 1) * B]
                    pair = i * (i + 1) // 2 + j + n
                    away = (tgt_a[pair] >= half).astype(jnp.float32)
                    for stream, tgt in enumerate((tgt_a, tgt_b)):
                        at = lax.rem(tgt[pair], half)
                        piece = block[stream * strip : (stream + 1) * strip]
                        keep[stream, at] += piece * (1.0 - away)
                        send[stream, at] += piece * away


SMEM = pl.BlockSpec(memory_space=pltpu.SMEM)
ANY = pl.BlockSpec(memory_space=pl.ANY)
VMEM = pl.BlockSpec(memory_space=pltpu.VMEM)


def xor_pairs(size, mask):
    return [(i, i ^ mask) for i in range(size)]


def log2(n):
    return n.bit_length() - 1


def swap(x, axis, mask):
    return lax.ppermute(x, axis, xor_pairs(lax.axis_size(axis), mask))


def relative_index(owner, slot, wide_me, narrow_me, steps):
    away = {"wide": owner ^ wide_me, "narrow": (slot // T_DEV) ^ narrow_me}
    index = jnp.zeros_like(owner)
    for axis, mask in steps:
        index = index * 2 + ((away[axis] // mask) & 1)
    return index * T_DEV + slot % T_DEV


def local(diag_block, panel, panel_count, pair_owner, pair_slot, ancestor):
    narrow_count = lax.axis_size("narrow")
    wide_count = lax.axis_size("wide")
    me = lax.axis_index("narrow")
    wide_me = lax.axis_index("wide")
    assert narrow_count == NB and diag_block.shape[0] == NB
    masks = range(1, NB)
    own = lambda x, m: lax.dynamic_index_in_dim(x, me ^ m, 0, keepdims=False)
    info = me.astype(jnp.int32).reshape(1)
    cut = [jax.ShapeDtypeStruct((rows, B), jnp.float32) for rows in (W, W // 2, W // 2)]
    cut = pl.pallas_call(
        cut_kernel,
        out_shape=cut,
        in_specs=[SMEM, pl.BlockSpec(memory_space=pltpu.HBM)],
        out_specs=[VMEM] * 3,
        scratch_shapes=[pltpu.SemaphoreType.DMA((3,))],
        compiler_params=pltpu.CompilerParams(vmem_limit_bytes=8 * 2**20),
        cost_estimate=pl.CostEstimate(flops=0, bytes_accessed=2**20, transcendentals=0),
        name="cut",
    )(info, diag_block)
    diag_in = [swap(part, "narrow", m) for m, part in zip(masks, cut)]
    panel_out = [own(panel, m) for m in masks]
    diag_in, panel_out = lax.optimization_barrier((diag_in, panel_out))
    panel_in = [swap(panel_out[m - 1], "narrow", m) for m in masks]

    narrow_steps = [("narrow", 1 << b) for b in range(log2(narrow_count))]
    wide_steps = [("wide", 1 << b) for b in range(log2(wide_count))]
    first, last = narrow_steps[:1], wide_steps[2:] + narrow_steps[1:]
    steps_a = first + wide_steps[:2] + last
    steps_b = first + wide_steps[1::-1] + last
    owner = lax.dynamic_slice_in_dim(pair_owner[:, 0], me * NPAIR, NPAIR)
    slot = lax.dynamic_slice_in_dim(pair_slot, me * NPAIR, NPAIR)
    tgt_a = relative_index(owner, slot, wide_me, me, steps_a)
    tgt_b = relative_index(owner, slot, wide_me, me, steps_b)

    slab = jax.ShapeDtypeStruct((W, B), jnp.float32)
    low = jax.ShapeDtypeStruct((W // 2, B), jnp.float32)
    *l_parts, mt = pl.pallas_call(
        factor_kernel,
        out_shape=[slab] * (NB - 1) + [low, low, jax.ShapeDtypeStruct((NB, W, B), jnp.float32)],
        in_specs=[SMEM] + [ANY] * NB,
        out_specs=[ANY] * (NB + 1) + [VMEM],
        scratch_shapes=[pltpu.VMEM((NB, W, B), jnp.float32)] * 2 + [pltpu.SemaphoreType.DMA((NB + 1,))],
        compiler_params=pltpu.CompilerParams(vmem_limit_bytes=16 * 2**20),
        cost_estimate=pl.CostEstimate(flops=2 * 10**8, bytes_accessed=4 * 10**6, transcendentals=0),
        name="factor",
    )(info, diag_block, *diag_in)

    rows = P_SIZE * B
    blocks = wide_count * narrow_count * T_DEV
    lead = rows // 4
    slab, short, longer = [
        jax.ShapeDtypeStruct((n, B), jnp.float32) for n in (rows, lead, rows - lead + W // 2)
    ]
    part = jax.ShapeDtypeStruct((2, blocks // 2, B // 2, B), jnp.float32)
    home, near, far_c, far_a, far_b, keep, send = pl.pallas_call(
        panel_kernel,
        out_shape=[slab] * 3 + [short, longer, part, part],
        in_specs=[SMEM] * 4 + [VMEM] * (NB + 2),
        out_specs=[VMEM] * 7,
        scratch_shapes=[pltpu.VMEM((rows, W), jnp.bfloat16)] * 2,
        compiler_params=pltpu.CompilerParams(vmem_limit_bytes=16 * 2**20 + 4 * blocks * B * B),
        cost_estimate=pl.CostEstimate(flops=10**9, bytes_accessed=10 * 10**6, transcendentals=0),
        name="panel",
    )(info, panel_count, tgt_a, tgt_b, panel, *panel_in, mt, l_parts[3])

    l_back = [swap(l_parts[m], "narrow", m) for m in (1, 2)]
    near = swap(near, "narrow", 1)
    far_a = swap(far_a, "narrow", 3)
    far_b = swap(far_b, "narrow", 3)
    far_c = swap(far_c, "narrow", 2)

    send, l_back[1] = lax.optimization_barrier((send, l_back[1]))
    got = swap(send, "narrow", 1)
    half = blocks // 4
    upper = lambda u, n: u[n, half:]
    lower = lambda u, n: u[n, :half]
    send_a = upper(keep, 0) + upper(got, 0)
    send_b = upper(keep, 1) + upper(got, 1)
    keep_a = lower(keep, 0) + lower(got, 0)
    keep_b = lower(keep, 1) + lower(got, 1)
    for n in (1, 2):
        if n == 2:
            send_a, send_b, far_b, late = lax.optimization_barrier((send_a, send_b, far_b, l_parts[4]))
            l_back.append(swap(late, "narrow", 3))
        else:
            send_a, send_b, far_a = lax.optimization_barrier((send_a, send_b, far_a))
        got_a = swap(send_a, *steps_a[n])
        got_b = swap(send_b, *steps_b[n])
        half = half // 2
        if n == 1:
            send_a, send_b = keep_a[half:] + got_a[half:], keep_b[half:] + got_b[half:]
            keep_a, keep_b = keep_a[:half] + got_a[:half], keep_b[:half] + got_b[:half]
    rest = steps_a[3:]
    take = lambda n, size: jnp.concatenate(
        [u[n * size : (n + 1) * size] + v[n * size : (n + 1) * size] for u, v in ((keep_a, got_a), (keep_b, got_b))],
        axis=1,
    )
    while len(rest) > 2:
        got = swap(take(1, half), *rest.pop(0))
        keep_a = take(0, half) + got
        half = half // 2
        keep_a, keep_b = keep_a[:, : B // 2], keep_a[:, B // 2 :]
        got_a, got_b = jnp.zeros_like(keep_a), jnp.zeros_like(keep_b)
    (_, wide_mask), (_, narrow_mask) = rest
    both = wide_mask * narrow_count + narrow_mask
    got = [
        lax.ppermute(take(3, T_DEV), ("wide", "narrow"), xor_pairs(wide_count * narrow_count, both)),
        swap(take(2, T_DEV), *rest[0]),
        swap(take(1, T_DEV), *rest[1]),
    ]
    got, far_c, near, l_back[2] = lax.optimization_barrier((got, far_c, near, l_back[2]))
    updated = ancestor - (take(0, T_DEV) + (got[0] + (got[1] + got[2])))

    def assemble(height, pieces):
        out = jnp.zeros((NB, height, B), jnp.float32)
        for m, row, piece in pieces:
            out = lax.dynamic_update_slice(out, piece[None], (me ^ m, row, 0))
        return out

    factor = assemble(
        W,
        [
            (0, 0, l_parts[0]),
            (1, 0, l_back[0]),
            (2, 0, l_back[1]),
            (3, 0, far_b[rows - lead :]),
            (3, W // 2, l_back[2]),
        ],
    )
    lower_panel = assemble(
        rows,
        [(0, 0, home), (1, 0, near), (2, 0, far_c), (3, 0, far_a), (3, lead, far_b[: rows - lead])],
    )
    return (factor, lower_panel, updated)


def solution(mesh):
    placed = (
        P("wide", None, "narrow"),
        P("wide", None, "narrow"),
        P("wide"),
        P("wide", None),
        P("wide"),
        P(("wide", "narrow"), None, None),
    )
    return jax.shard_map(
        local,
        mesh=mesh,
        in_specs=placed,
        out_specs=(
            P("wide", None, "narrow"),
            P("wide", None, "narrow"),
            P(("wide", "narrow"), None, None),
        ),
        check_vma=False,
    )
```

```python
import jax
import jax.numpy as jnp
import numpy as np
from jax import lax
from jax.experimental import pallas as pl
from jax.experimental.pallas import tpu as pltpu
from jax.sharding import PartitionSpec as P

W = 512
B = 128
P_SIZE = 8
T_DEV = 2
NB = W // B
NPAIR = P_SIZE * (P_SIZE + 1) // 2
HIGHEST = lax.Precision.HIGHEST


def dot_nt(a, b):
    return lax.dot_general(
        a, b, (((1,), (1,)), ((), ())), precision=HIGHEST, preferred_element_type=jnp.float32
    )


def dot_nn(a, b):
    return lax.dot_general(
        a, b, (((1,), (0,)), ((), ())), precision=HIGHEST, preferred_element_type=jnp.float32
    )


def lane_of(x, c):
    return jnp.broadcast_to(x[:, c : c + 1], x.shape)


def row_of(x, r):
    return jnp.broadcast_to(x[r : r + 1, :], x.shape)


def inverse_factor(block):
    sub = lax.broadcasted_iota(jnp.int32, (8, B), 0)
    lane = lax.broadcasted_iota(jnp.int32, (8, B), 1)
    total, strip = B // 8, 2
    rows = [block[8 * q : 8 * q + 8, :] for q in range(total)]
    done = [None] * total
    for b in range(0, total, strip):
        mine = range(b, b + strip)
        near = range(b + strip, min(b + 2 * strip, total))
        far = range(b + 2 * strip, total)
        in_strip = (lane >= 8 * b) & (lane < 8 * (b + strip))
        ahead = {q: [lane_of(rows[q], 8 * b + m) for m in range(8 * strip)] for q in near}
        for p in mine:
            lo = 8 * p
            own = (lane >= lo) & (lane < lo + 8)
            cols = [lane_of(rows[p], lo + m) for m in range(8)]
            others = [q for q in mine if q != p]
            mult = {q: [lane_of(rows[q], lo + m) for m in range(8)] for q in others}
            work = jnp.where(own, (lane - lo == sub).astype(jnp.float32), rows[p])
            final = jnp.zeros((8, B), jnp.float32)
            for k in range(0, 8, 2):
                f0, f1 = cols[k], cols[k + 1]
                a, h, c = row_of(f0, k), row_of(f0, k + 1), row_of(f1, k + 1)
                det = a * c - h * h
                recip = 1.0 / det
                ar, hr, cr = a * recip, h * recip, c * recip
                first, second = sub == k, sub == k + 1

                def eliminate(v):
                    r0, r1 = row_of(v, k), row_of(v, k + 1)
                    s0, s1 = cr * r0 - hr * r1, ar * r1 - hr * r0
                    return r0, r1, jnp.where(first, s0, jnp.where(second, s1, v - f0 * s0 - f1 * s1))

                for m in range(k + 2, 8):
                    cols[m] = eliminate(cols[m])[2]
                r0, r1, work = eliminate(work)
                root = lax.rsqrt(a)
                lower = (a * r1 - h * r0) * (root * lax.rsqrt(det))
                final = jnp.where(first, r0 * root, jnp.where(second, lower, final))
            done[p] = jnp.where(lane <= sub + lo, final, 0.0)
            rows[p] = work
            lines = [row_of(work, m) for m in range(8)]
            for q in others:
                new = jnp.where(own, 0.0, rows[q])
                for m in range(8):
                    new = new - mult[q][m] * lines[m]
                rows[q] = new
        lines = [row_of(rows[q], m) for q in mine for m in range(8)]
        for q in near:
            parts = [ahead[q][m] * lines[m] for m in range(4)]
            for m in range(4, 8 * strip):
                parts[m % 4] = parts[m % 4] + ahead[q][m] * lines[m]
            rows[q] = jnp.where(in_strip, 0.0, rows[q]) - ((parts[0] + parts[1]) + (parts[2] + parts[3]))
        if far:
            stack = jnp.concatenate([rows[q] for q in far], axis=0)
            lane_far = lax.broadcasted_iota(jnp.int32, stack.shape, 1)
            in_far = (lane_far >= 8 * b) & (lane_far < 8 * (b + strip))
            zero = jnp.zeros((8, B), jnp.float32)
            tall = jnp.concatenate([rows[q] if q in mine else zero for q in range(total)], axis=0)
            stack = jnp.where(in_far, 0.0, stack) - dot_nn(jnp.where(in_far, stack, 0.0), tall)
            for n, q in enumerate(far):
                rows[q] = stack[8 * n : 8 * n + 8]
    return jnp.concatenate(done, axis=0)


def split_bf16(v):
    high = v.astype(jnp.bfloat16)
    return high, (v - high.astype(jnp.float32)).astype(jnp.bfloat16)


def dot3(left, right, contract):
    dot = lambda a, b: lax.dot_general(
        a, b, (contract, ((), ())), preferred_element_type=jnp.float32
    )
    return dot(left[0], right[0]) + (dot(left[0], right[1]) + dot(left[1], right[0]))


def cut_kernel(info, blocks, near, far_a, far_b, sems):
    me = info[0]
    half = pl.ds((me // 2) * (W // 2), W // 2)
    copies = [
        pltpu.make_async_copy(blocks.at[me ^ 2, half], far_a, sems.at[0]),
        pltpu.make_async_copy(blocks.at[me ^ 3, half], far_b, sems.at[1]),
        pltpu.make_async_copy(blocks.at[me ^ 1], near, sems.at[2]),
    ]
    for c in copies:
        c.start()
    for c in copies:
        c.wait()


def factor_kernel(info, own_ref, r1, r2, r3, l0, l1, l2a, l2b, l3, mt, a, l, sems):
    me = info[0]
    side = me // 2
    far_rows = pl.ds((1 - side) * (W // 2), W // 2)
    places = [a.at[me], a.at[me ^ 1], a.at[me ^ 2, far_rows], a.at[me ^ 3, far_rows]]
    ins = [own_ref.at[me], r1, r2, r3]
    copies = [pltpu.make_async_copy(ins[m], places[m], sems.at[m]) for m in range(NB)]
    for c in copies:
        c.start()
    for c in copies:
        c.wait()

    @pl.when(side == 1)
    def _():
        for j in range(NB // 2):
            for i in range(NB // 2, NB):
                a[j, pl.ds(i * B, B), :] = a[i, pl.ds(j * B, B), :].T

    row = lax.broadcasted_iota(jnp.int32, (B, B), 0)
    col = lax.broadcasted_iota(jnp.int32, (B, B), 1)
    l[...] = jnp.zeros_like(l)
    mt[...] = jnp.zeros_like(mt)
    eye = (row == col).astype(jnp.float32)
    for k in range(NB):
        here = pl.ds(k * B, B)
        inv = inverse_factor(a[k, here, :])
        l[k, here, :] = jnp.where(row >= col, dot_nt(a[k, here, :], inv), 0.0)
        for i in range(k + 1, NB):
            below = dot_nt(a[k, pl.ds(i * B, B), :], inv)
            l[k, pl.ds(i * B, B), :] = below
            for j in range(k + 1, i + 1):
                a[j, pl.ds(i * B, B), :] -= dot_nt(below, l[k, pl.ds(j * B, B), :])
        mt[k, here, :] = dot_nt(eye, inv)
        for i in range(k):
            total = dot_nt(mt[i, pl.ds(i * B, B), :], l[i, here, :])
            for j in range(i + 1, k):
                total = total + dot_nt(mt[j, pl.ds(i * B, B), :], l[j, here, :])
            mt[k, pl.ds(i * B, B), :] = dot_nt(-total, inv)
    half = [pl.ds(n * (W // 2), W // 2) for n in range(2)]
    pieces = [l.at[me], l.at[me ^ 1], l.at[me ^ 2, half[0]], l.at[me ^ 2, half[1]], l.at[me ^ 3]]
    copies = [
        pltpu.make_async_copy(piece, out, sems.at[n])
        for n, (piece, out) in enumerate(zip(pieces, (l0, l1, l2a, l2b, l3)))
    ]
    for c in copies:
        c.start()
    for c in copies:
        c.wait()


def panel_kernel(
    info, counts, tgt_a, tgt_b, own_ref, r1, r2, r3, mt, l2b, x0, x1, x2, x3, keep, send, xh, xl, p, sems
):
    me = info[0]
    count = counts[me]
    rows = P_SIZE * B
    copies = [
        pltpu.make_async_copy(ref, p.at[m], sems.at[m]) for m, ref in enumerate((own_ref.at[me], r1, r2, r3))
    ]
    for copy in copies:
        copy.start()
    keep[...] = jnp.zeros_like(keep)
    send[...] = jnp.zeros_like(send)
    outs = [x0, x1, x2, x3]
    x2[pl.ds(rows, W // 2), :] = l2b[...]
    for copy in copies:
        copy.wait()
    live = lax.broadcasted_iota(jnp.int32, (rows, B), 0) < count * B
    parts = [split_bf16(jnp.where(live, p[m], 0.0)) for m in range(NB)]
    left = [jnp.concatenate([part[n] for part in parts], axis=1) for n in range(2)]
    for c in range(0, NB, 2):
        right = [
            jnp.concatenate([mt[me ^ m, pl.ds((me ^ k) * B, B), :] for m in (c, c + 1)], axis=1)
            for k in range(NB)
        ]
        got = dot3(left, split_bf16(jnp.concatenate(right, axis=0)), ((1,), (0,)))
        outs[c][pl.ds(0, rows), :] = got[:, :B]
        outs[c + 1][pl.ds(0, rows), :] = got[:, B:]
        high, low = split_bf16(got)
        xh[:, pl.ds(c * B, 2 * B)] = high
        xl[:, pl.ds(c * B, 2 * B)] = low

    half, strip = keep.shape[1:3]
    for j in range(0, P_SIZE, 2):

        @pl.when(j < count)
        def _():
            left = (xh[pl.ds(j * B, rows - j * B), :], xl[pl.ds(j * B, rows - j * B), :])
            right = (xh[pl.ds(j * B, 2 * B), :], xl[pl.ds(j * B, 2 * B), :])
            got = dot3(left, right, ((1,), (1,)))
            for i in range(j, P_SIZE):
                for n in range(2 if i > j else 1):
                    block = got[(i - j) * B : (i - j + 1) * B, n * B : (n + 1) * B]
                    pair = i * (i + 1) // 2 + j + n
                    away = (tgt_a[pair] >= half).astype(jnp.float32)
                    for stream, tgt in enumerate((tgt_a, tgt_b)):
                        at = lax.rem(tgt[pair], half)
                        piece = block[stream * strip : (stream + 1) * strip]
                        keep[stream, at] += piece * (1.0 - away)
                        send[stream, at] += piece * away


SMEM = pl.BlockSpec(memory_space=pltpu.SMEM)
ANY = pl.BlockSpec(memory_space=pl.ANY)
VMEM = pl.BlockSpec(memory_space=pltpu.VMEM)


def xor_pairs(size, mask):
    return [(i, i ^ mask) for i in range(size)]


def log2(n):
    return n.bit_length() - 1


def swap(x, axis, mask):
    return lax.ppermute(x, axis, xor_pairs(lax.axis_size(axis), mask))


def relative_index(owner, slot, wide_me, narrow_me, steps):
    away = {"wide": owner ^ wide_me, "narrow": (slot // T_DEV) ^ narrow_me}
    index = jnp.zeros_like(owner)
    for axis, mask in steps:
        index = index * 2 + ((away[axis] // mask) & 1)
    return index * T_DEV + slot % T_DEV


def local(diag_block, panel, panel_count, pair_owner, pair_slot, ancestor):
    narrow_count = lax.axis_size("narrow")
    wide_count = lax.axis_size("wide")
    me = lax.axis_index("narrow")
    wide_me = lax.axis_index("wide")
    assert narrow_count == NB and diag_block.shape[0] == NB
    masks = range(1, NB)
    own = lambda x, m: lax.dynamic_index_in_dim(x, me ^ m, 0, keepdims=False)
    info = me.astype(jnp.int32).reshape(1)
    cut = [jax.ShapeDtypeStruct((rows, B), jnp.float32) for rows in (W, W // 2, W // 2)]
    cut = pl.pallas_call(
        cut_kernel,
        out_shape=cut,
        in_specs=[SMEM, pl.BlockSpec(memory_space=pltpu.HBM)],
        out_specs=[VMEM] * 3,
        scratch_shapes=[pltpu.SemaphoreType.DMA((3,))],
        compiler_params=pltpu.CompilerParams(vmem_limit_bytes=8 * 2**20),
        cost_estimate=pl.CostEstimate(flops=0, bytes_accessed=0, transcendentals=0),
        name="cut",
    )(info, diag_block)
    diag_in = [swap(part, "narrow", m) for m, part in zip(masks, cut)]
    panel_out = [own(panel, m) for m in masks]
    diag_in, panel_out = lax.optimization_barrier((diag_in, panel_out))
    panel_in = [swap(panel_out[m - 1], "narrow", m) for m in masks]

    narrow_steps = [("narrow", 1 << b) for b in range(log2(narrow_count))]
    wide_steps = [("wide", 1 << b) for b in range(log2(wide_count))]
    first, last = narrow_steps[:1], wide_steps[2:] + narrow_steps[1:]
    steps_a = first + wide_steps[:2] + last
    steps_b = first + wide_steps[1::-1] + last
    owner = lax.dynamic_slice_in_dim(pair_owner[:, 0], me * NPAIR, NPAIR)
    slot = lax.dynamic_slice_in_dim(pair_slot, me * NPAIR, NPAIR)
    tgt_a = relative_index(owner, slot, wide_me, me, steps_a)
    tgt_b = relative_index(owner, slot, wide_me, me, steps_b)

    slab = jax.ShapeDtypeStruct((W, B), jnp.float32)
    low = jax.ShapeDtypeStruct((W // 2, B), jnp.float32)
    *l_parts, mt = pl.pallas_call(
        factor_kernel,
        out_shape=[slab, slab, low, low, slab, jax.ShapeDtypeStruct((NB, W, B), jnp.float32)],
        in_specs=[SMEM] + [ANY] * NB,
        out_specs=[ANY] * (NB + 1) + [VMEM],
        scratch_shapes=[pltpu.VMEM((NB, W, B), jnp.float32)] * 2 + [pltpu.SemaphoreType.DMA((NB + 1,))],
        compiler_params=pltpu.CompilerParams(vmem_limit_bytes=16 * 2**20),
        cost_estimate=pl.CostEstimate(flops=2 * 10**8, bytes_accessed=4 * 10**6, transcendentals=0),
        name="factor",
    )(info, diag_block, *diag_in)

    rows = P_SIZE * B
    blocks = wide_count * narrow_count * T_DEV
    slab, longer = [jax.ShapeDtypeStruct((n, B), jnp.float32) for n in (rows, rows + W // 2)]
    part = jax.ShapeDtypeStruct((2, blocks // 2, B // 2, B), jnp.float32)
    home, near, far_2, far_3, keep, send = pl.pallas_call(
        panel_kernel,
        out_shape=[slab, slab, longer, slab, part, part],
        in_specs=[SMEM] * 4 + [ANY] * NB + [VMEM] * 2,
        out_specs=[VMEM] * 6,
        scratch_shapes=[pltpu.VMEM((rows, W), jnp.bfloat16)] * 2
        + [pltpu.VMEM((NB, rows, B), jnp.float32), pltpu.SemaphoreType.DMA((NB,))],
        compiler_params=pltpu.CompilerParams(vmem_limit_bytes=16 * 2**20 + 4 * blocks * B * B),
        cost_estimate=pl.CostEstimate(flops=10**9, bytes_accessed=10 * 10**6, transcendentals=0),
        name="panel",
    )(info, panel_count, tgt_a, tgt_b, panel, *panel_in, mt, l_parts[3])

    near_l, far_l2, far_l3 = [swap(l_parts[n], "narrow", m) for n, m in ((1, 1), (2, 2), (4, 3))]
    near = swap(near, "narrow", 1)
    far_2 = swap(far_2, "narrow", 2)
    far_3 = swap(far_3, "narrow", 3)

    send, far_l3 = lax.optimization_barrier((send, far_l3))
    got = swap(send, "narrow", 1)
    half = blocks // 4
    upper = lambda u, n: u[n, half:]
    lower = lambda u, n: u[n, :half]
    send_a = upper(keep, 0) + upper(got, 0)
    send_b = upper(keep, 1) + upper(got, 1)
    keep_a = lower(keep, 0) + lower(got, 0)
    keep_b = lower(keep, 1) + lower(got, 1)
    for n in (1, 2):
        if n == 2:
            send_a, send_b, far_3 = lax.optimization_barrier((send_a, send_b, far_3))
        else:
            send_a, send_b, far_l2 = lax.optimization_barrier((send_a, send_b, far_l2))
        got_a = swap(send_a, *steps_a[n])
        got_b = swap(send_b, *steps_b[n])
        half = half // 2
        if n == 1:
            send_a, send_b = keep_a[half:] + got_a[half:], keep_b[half:] + got_b[half:]
            keep_a, keep_b = keep_a[:half] + got_a[:half], keep_b[:half] + got_b[:half]
    rest = steps_a[3:]
    take = lambda n, size: jnp.concatenate(
        [u[n * size : (n + 1) * size] + v[n * size : (n + 1) * size] for u, v in ((keep_a, got_a), (keep_b, got_b))],
        axis=1,
    )
    while len(rest) > 2:
        got = swap(take(1, half), *rest.pop(0))
        keep_a = take(0, half) + got
        half = half // 2
        keep_a, keep_b = keep_a[:, : B // 2], keep_a[:, B // 2 :]
        got_a, got_b = jnp.zeros_like(keep_a), jnp.zeros_like(keep_b)
    (_, wide_mask), (_, narrow_mask) = rest
    both = wide_mask * narrow_count + narrow_mask
    got = [
        lax.ppermute(take(3, T_DEV), ("wide", "narrow"), xor_pairs(wide_count * narrow_count, both)),
        swap(take(2, T_DEV), *rest[0]),
        swap(take(1, T_DEV), *rest[1]),
    ]
    got, far_2, near = lax.optimization_barrier((got, far_2, near))
    updated = ancestor - (take(0, T_DEV) + (got[0] + (got[1] + got[2])))

    def assemble(height, pieces):
        out = jnp.zeros((NB, height, B), jnp.float32)
        for m, row, piece in pieces:
            out = lax.dynamic_update_slice(out, piece[None], (me ^ m, row, 0))
        return out

    factor = assemble(
        W, [(0, 0, l_parts[0]), (1, 0, near_l), (3, 0, far_l3), (2, 0, far_l2), (2, W // 2, far_2[rows:])]
    )
    lower_panel = assemble(rows, [(0, 0, home), (1, 0, near), (3, 0, far_3), (2, 0, far_2[:rows])])
    return (factor, lower_panel, updated)


def solution(mesh):
    placed = (
        P("wide", None, "narrow"),
        P("wide", None, "narrow"),
        P("wide"),
        P("wide", None),
        P("wide"),
        P(("wide", "narrow"), None, None),
    )
    return jax.shard_map(
        local,
        mesh=mesh,
        in_specs=placed,
        out_specs=(
            P("wide", None, "narrow"),
            P("wide", None, "narrow"),
            P(("wide", "narrow"), None, None),
        ),
        check_vma=False,
    )
```

```python
import jax
import jax.numpy as jnp
import numpy as np
from jax import lax
from jax.experimental import pallas as pl
from jax.experimental.pallas import tpu as pltpu
from jax.sharding import PartitionSpec as P

W = 512
B = 128
P_SIZE = 8
T_DEV = 2
NB = W // B
NPAIR = P_SIZE * (P_SIZE + 1) // 2
HIGHEST = lax.Precision.HIGHEST


def dot_nt(a, b):
    return lax.dot_general(
        a, b, (((1,), (1,)), ((), ())), precision=HIGHEST, preferred_element_type=jnp.float32
    )


def dot_nn(a, b):
    return lax.dot_general(
        a, b, (((1,), (0,)), ((), ())), precision=HIGHEST, preferred_element_type=jnp.float32
    )


def lane_of(x, c):
    return jnp.broadcast_to(x[:, c : c + 1], x.shape)


def row_of(x, r):
    return jnp.broadcast_to(x[r : r + 1, :], x.shape)


def inverse_factor(block):
    sub = lax.broadcasted_iota(jnp.int32, (8, B), 0)
    lane = lax.broadcasted_iota(jnp.int32, (8, B), 1)
    total, strip = B // 8, 2
    rows = [block[8 * q : 8 * q + 8, :] for q in range(total)]
    done = [None] * total
    for b in range(0, total, strip):
        mine = range(b, b + strip)
        near = range(b + strip, min(b + 2 * strip, total))
        far = range(b + 2 * strip, total)
        in_strip = (lane >= 8 * b) & (lane < 8 * (b + strip))
        ahead = {q: [lane_of(rows[q], 8 * b + m) for m in range(8 * strip)] for q in near}
        for p in mine:
            lo = 8 * p
            own = (lane >= lo) & (lane < lo + 8)
            cols = [lane_of(rows[p], lo + m) for m in range(8)]
            others = [q for q in mine if q != p]
            mult = {q: [lane_of(rows[q], lo + m) for m in range(8)] for q in others}
            work = jnp.where(own, (lane - lo == sub).astype(jnp.float32), rows[p])
            final = jnp.zeros((8, B), jnp.float32)
            for k in range(0, 8, 2):
                f0, f1 = cols[k], cols[k + 1]
                a, h, c = row_of(f0, k), row_of(f0, k + 1), row_of(f1, k + 1)
                det = a * c - h * h
                recip = 1.0 / det
                ar, hr, cr = a * recip, h * recip, c * recip
                first, second = sub == k, sub == k + 1

                def eliminate(v):
                    r0, r1 = row_of(v, k), row_of(v, k + 1)
                    s0, s1 = cr * r0 - hr * r1, ar * r1 - hr * r0
                    return r0, r1, jnp.where(first, s0, jnp.where(second, s1, v - f0 * s0 - f1 * s1))

                for m in range(k + 2, 8):
                    cols[m] = eliminate(cols[m])[2]
                r0, r1, work = eliminate(work)
                root = lax.rsqrt(a)
                lower = (a * r1 - h * r0) * (root * lax.rsqrt(det))
                final = jnp.where(first, r0 * root, jnp.where(second, lower, final))
            done[p] = jnp.where(lane <= sub + lo, final, 0.0)
            rows[p] = work
            lines = [row_of(work, m) for m in range(8)]
            for q in others:
                new = jnp.where(own, 0.0, rows[q])
                for m in range(8):
                    new = new - mult[q][m] * lines[m]
                rows[q] = new
        lines = [row_of(rows[q], m) for q in mine for m in range(8)]
        for q in near:
            parts = [ahead[q][m] * lines[m] for m in range(4)]
            for m in range(4, 8 * strip):
                parts[m % 4] = parts[m % 4] + ahead[q][m] * lines[m]
            rows[q] = jnp.where(in_strip, 0.0, rows[q]) - ((parts[0] + parts[1]) + (parts[2] + parts[3]))
        if far:
            stack = jnp.concatenate([rows[q] for q in far], axis=0)
            lane_far = lax.broadcasted_iota(jnp.int32, stack.shape, 1)
            in_far = (lane_far >= 8 * b) & (lane_far < 8 * (b + strip))
            zero = jnp.zeros((8, B), jnp.float32)
            tall = jnp.concatenate([rows[q] if q in mine else zero for q in range(total)], axis=0)
            stack = jnp.where(in_far, 0.0, stack) - dot_nn(jnp.where(in_far, stack, 0.0), tall)
            for n, q in enumerate(far):
                rows[q] = stack[8 * n : 8 * n + 8]
    return jnp.concatenate(done, axis=0)


def split_bf16(v):
    high = v.astype(jnp.bfloat16)
    return high, (v - high.astype(jnp.float32)).astype(jnp.bfloat16)


def dot3(left, right, contract):
    dot = lambda a, b: lax.dot_general(
        a, b, (contract, ((), ())), preferred_element_type=jnp.float32
    )
    return dot(left[0], right[0]) + (dot(left[0], right[1]) + dot(left[1], right[0]))


def cut_kernel(info, blocks, near, far_a, far_b, sems):
    me = info[0]
    half = pl.ds((me // 2) * (W // 2), W // 2)
    copies = [
        pltpu.make_async_copy(blocks.at[me ^ 2, half], far_a, sems.at[0]),
        pltpu.make_async_copy(blocks.at[me ^ 3, half], far_b, sems.at[1]),
        pltpu.make_async_copy(blocks.at[me ^ 1], near, sems.at[2]),
    ]
    for c in copies:
        c.start()
    for c in copies:
        c.wait()


def factor_kernel(info, own_ref, r1, r2, r3, l0, l1, l2, l3, mt, a, l, sems):
    me = info[0]
    side = me // 2
    far_rows = pl.ds((1 - side) * (W // 2), W // 2)
    places = [a.at[me], a.at[me ^ 1], a.at[me ^ 2, far_rows], a.at[me ^ 3, far_rows]]
    ins = [own_ref.at[me], r1, r2, r3]
    copies = [pltpu.make_async_copy(ins[m], places[m], sems.at[m]) for m in range(NB)]
    for c in copies:
        c.start()
    for c in copies:
        c.wait()

    @pl.when(side == 1)
    def _():
        for j in range(NB // 2):
            for i in range(NB // 2, NB):
                a[j, pl.ds(i * B, B), :] = a[i, pl.ds(j * B, B), :].T

    row = lax.broadcasted_iota(jnp.int32, (B, B), 0)
    col = lax.broadcasted_iota(jnp.int32, (B, B), 1)
    l[...] = jnp.zeros_like(l)
    mt[...] = jnp.zeros_like(mt)
    eye = (row == col).astype(jnp.float32)
    for k in range(NB):
        here = pl.ds(k * B, B)
        inv = inverse_factor(a[k, here, :])
        l[k, here, :] = jnp.where(row >= col, dot_nt(a[k, here, :], inv), 0.0)
        for i in range(k + 1, NB):
            below = dot_nt(a[k, pl.ds(i * B, B), :], inv)
            l[k, pl.ds(i * B, B), :] = below
            for j in range(k + 1, i + 1):
                a[j, pl.ds(i * B, B), :] -= dot_nt(below, l[k, pl.ds(j * B, B), :])
        mt[k, here, :] = dot_nt(eye, inv)
        for i in range(k):
            total = dot_nt(mt[i, pl.ds(i * B, B), :], l[i, here, :])
            for j in range(i + 1, k):
                total = total + dot_nt(mt[j, pl.ds(i * B, B), :], l[j, here, :])
            mt[k, pl.ds(i * B, B), :] = dot_nt(-total, inv)
    outs = [l0, l1, l2, l3]
    copies = [pltpu.make_async_copy(l.at[me ^ m], outs[m], sems.at[m]) for m in range(NB)]
    for c in copies:
        c.start()
    for c in copies:
        c.wait()


def masked_split(ref, count):
    rows = ref.shape[0]
    live = lax.broadcasted_iota(jnp.int32, (rows, B), 0) < count * B
    return split_bf16(jnp.where(live, ref[...], 0.0))


def inverse_rows(mt, me, blocks, c):
    rows = [
        jnp.concatenate([mt[me ^ m, pl.ds((me ^ k) * B, B), :] for m in (c, c + 1)], axis=1) for k in blocks
    ]
    return split_bf16(jnp.concatenate(rows, axis=0))


def early_kernel(info, counts, own_ref, r1, r2, mt, acc, *sums):
    me = info[0]
    parts = [masked_split(ref, counts[me]) for ref in (own_ref.at[me], r1, r2)]
    left = [jnp.concatenate([part[n] for part in parts], axis=1) for n in range(2)]
    for c in range(0, NB, 2):
        acc[:, pl.ds(c * B, 2 * B)] = dot3(left, inverse_rows(mt, me, range(NB - 1), c), ((1,), (0,)))
    for ref in sums:
        ref[...] = jnp.zeros_like(ref)


def panel_kernel(info, counts, tgt_a, tgt_b, r3, mt, l3, acc, *rest):
    x0, x1, x2, x3, keep, send, xh, xl = rest[-8:]
    if len(rest) == 8:
        keep[...] = jnp.zeros_like(keep)
        send[...] = jnp.zeros_like(send)
    me = info[0]
    count = counts[me]
    rows = P_SIZE * B
    outs = [x0, x1, x2, x3]
    x3[pl.ds(rows, W), :] = l3[...]
    left = masked_split(r3, count)
    for c in range(0, NB, 2):
        got = acc[:, pl.ds(c * B, 2 * B)] + dot3(left, inverse_rows(mt, me, [NB - 1], c), ((1,), (0,)))
        outs[c][pl.ds(0, rows), :] = got[:, :B]
        outs[c + 1][pl.ds(0, rows), :] = got[:, B:]
        high, low = split_bf16(got)
        xh[:, pl.ds(c * B, 2 * B)] = high
        xl[:, pl.ds(c * B, 2 * B)] = low

    half, strip = keep.shape[1:3]
    for j in range(0, P_SIZE, 2):

        @pl.when(j < count)
        def _():
            left = (xh[pl.ds(j * B, rows - j * B), :], xl[pl.ds(j * B, rows - j * B), :])
            right = (xh[pl.ds(j * B, 2 * B), :], xl[pl.ds(j * B, 2 * B), :])
            got = dot3(left, right, ((1,), (1,)))
            for i in range(j, P_SIZE):
                for n in range(2 if i > j else 1):
                    block = got[(i - j) * B : (i - j + 1) * B, n * B : (n + 1) * B]
                    pair = i * (i + 1) // 2 + j + n
                    away = (tgt_a[pair] >= half).astype(jnp.float32)
                    for stream, tgt in enumerate((tgt_a, tgt_b)):
                        at = lax.rem(tgt[pair], half)
                        piece = block[stream * strip : (stream + 1) * strip]
                        keep[stream, at] += piece * (1.0 - away)
                        send[stream, at] += piece * away


SMEM = pl.BlockSpec(memory_space=pltpu.SMEM)
ANY = pl.BlockSpec(memory_space=pl.ANY)
VMEM = pl.BlockSpec(memory_space=pltpu.VMEM)


def xor_pairs(size, mask):
    return [(i, i ^ mask) for i in range(size)]


def log2(n):
    return n.bit_length() - 1


def swap(x, axis, mask):
    return lax.ppermute(x, axis, xor_pairs(lax.axis_size(axis), mask))


def relative_index(owner, slot, wide_me, narrow_me, steps):
    away = {"wide": owner ^ wide_me, "narrow": (slot // T_DEV) ^ narrow_me}
    index = jnp.zeros_like(owner)
    for axis, mask in steps:
        index = index * 2 + ((away[axis] // mask) & 1)
    return index * T_DEV + slot % T_DEV


def local(diag_block, panel, panel_count, pair_owner, pair_slot, ancestor):
    narrow_count = lax.axis_size("narrow")
    wide_count = lax.axis_size("wide")
    me = lax.axis_index("narrow")
    wide_me = lax.axis_index("wide")
    assert narrow_count == NB and diag_block.shape[0] == NB
    masks = range(1, NB)
    own = lambda x, m: lax.dynamic_index_in_dim(x, me ^ m, 0, keepdims=False)
    info = me.astype(jnp.int32).reshape(1)
    cut = [jax.ShapeDtypeStruct((rows, B), jnp.float32) for rows in (W, W // 2, W // 2)]
    cut = pl.pallas_call(
        cut_kernel,
        out_shape=cut,
        in_specs=[SMEM, pl.BlockSpec(memory_space=pltpu.HBM)],
        out_specs=[VMEM] * 3,
        scratch_shapes=[pltpu.SemaphoreType.DMA((3,))],
        compiler_params=pltpu.CompilerParams(vmem_limit_bytes=8 * 2**20),
        cost_estimate=pl.CostEstimate(flops=0, bytes_accessed=2**20, transcendentals=0),
        name="cut",
    )(info, diag_block)
    diag_in = [swap(part, "narrow", m) for m, part in zip(masks, cut)]
    panel_out = [own(panel, m) for m in masks]
    diag_in, panel_out = lax.optimization_barrier((diag_in, panel_out))
    panel_in = [swap(panel_out[m - 1], "narrow", m) for m in masks]

    narrow_steps = [("narrow", 1 << b) for b in range(log2(narrow_count))]
    wide_steps = [("wide", 1 << b) for b in range(log2(wide_count))]
    first, last = narrow_steps[:1], wide_steps[2:] + narrow_steps[1:]
    steps_a = first + wide_steps[:2] + last
    steps_b = first + wide_steps[1::-1] + last
    owner = lax.dynamic_slice_in_dim(pair_owner[:, 0], me * NPAIR, NPAIR)
    slot = lax.dynamic_slice_in_dim(pair_slot, me * NPAIR, NPAIR)
    tgt_a = relative_index(owner, slot, wide_me, me, steps_a)
    tgt_b = relative_index(owner, slot, wide_me, me, steps_b)

    slab = jax.ShapeDtypeStruct((W, B), jnp.float32)
    *l_parts, mt = pl.pallas_call(
        factor_kernel,
        out_shape=[slab] * NB + [jax.ShapeDtypeStruct((NB, W, B), jnp.float32)],
        in_specs=[SMEM] + [ANY] * NB,
        out_specs=[ANY] * NB + [VMEM],
        scratch_shapes=[pltpu.VMEM((NB, W, B), jnp.float32)] * 2 + [pltpu.SemaphoreType.DMA((NB,))],
        compiler_params=pltpu.CompilerParams(vmem_limit_bytes=32 * 2**20),
        cost_estimate=pl.CostEstimate(flops=2 * 10**8, bytes_accessed=4 * 10**6, transcendentals=0),
        name="factor",
    )(info, diag_block, *diag_in)

    rows = P_SIZE * B
    blocks = wide_count * narrow_count * T_DEV
    slab = jax.ShapeDtypeStruct((rows, B), jnp.float32)
    longer = jax.ShapeDtypeStruct((rows + W, B), jnp.float32)
    part = jax.ShapeDtypeStruct((2, blocks // 2, B // 2, B), jnp.float32)
    room = pltpu.CompilerParams(vmem_limit_bytes=20 * 2**20 + 4 * blocks * B * B)
    sums = 2 if blocks * B * B * 4 <= 8 * 2**20 else 0
    acc, *empty = pl.pallas_call(
        early_kernel,
        out_shape=[jax.ShapeDtypeStruct((rows, W), jnp.float32)] + [part] * sums,
        in_specs=[SMEM] * 2 + [VMEM] * 4,
        out_specs=[VMEM] * (1 + sums),
        compiler_params=room,
        cost_estimate=pl.CostEstimate(flops=5 * 10**8, bytes_accessed=10 * 10**6, transcendentals=0),
        name="early",
    )(info, panel_count, panel, *panel_in[:2], mt)
    *x_parts, keep, send = pl.pallas_call(
        panel_kernel,
        out_shape=[slab] * (NB - 1) + [longer, part, part],
        in_specs=[SMEM] * 4 + [VMEM] * (4 + sums),
        out_specs=[VMEM] * (NB + 2),
        scratch_shapes=[pltpu.VMEM((rows, W), jnp.bfloat16)] * 2,
        input_output_aliases={8 + n: NB + n for n in range(sums)},
        compiler_params=room,
        cost_estimate=pl.CostEstimate(flops=10**9, bytes_accessed=10 * 10**6, transcendentals=0),
        name="panel",
    )(info, panel_count, tgt_a, tgt_b, panel_in[2], mt, l_parts[3], acc, *empty)

    l_back = [swap(l_parts[m], "narrow", m) for m in (1, 2)]
    x_back = [swap(x_parts[m], "narrow", m) for m in masks]

    send, l_back[1] = lax.optimization_barrier((send, l_back[1]))
    got = swap(send, "narrow", 1)
    half = blocks // 4
    upper = lambda u, n: u[n, half:]
    lower = lambda u, n: u[n, :half]
    send_a = upper(keep, 0) + upper(got, 0)
    send_b = upper(keep, 1) + upper(got, 1)
    keep_a = lower(keep, 0) + lower(got, 0)
    keep_b = lower(keep, 1) + lower(got, 1)
    for n in (1, 2):
        if n == 2:
            send_a, send_b, x_back[1] = lax.optimization_barrier((send_a, send_b, x_back[1]))
        else:
            send_a, send_b = lax.optimization_barrier((send_a, send_b))
        got_a = swap(send_a, *steps_a[n])
        got_b = swap(send_b, *steps_b[n])
        half = half // 2
        if n == 1:
            send_a, send_b = keep_a[half:] + got_a[half:], keep_b[half:] + got_b[half:]
            keep_a, keep_b = keep_a[:half] + got_a[:half], keep_b[:half] + got_b[:half]
    rest = steps_a[3:]
    take = lambda n, size: jnp.concatenate(
        [u[n * size : (n + 1) * size] + v[n * size : (n + 1) * size] for u, v in ((keep_a, got_a), (keep_b, got_b))],
        axis=1,
    )
    while len(rest) > 2:
        got = swap(take(1, half), *rest.pop(0))
        keep_a = take(0, half) + got
        half = half // 2
        keep_a, keep_b = keep_a[:, : B // 2], keep_a[:, B // 2 :]
        got_a, got_b = jnp.zeros_like(keep_a), jnp.zeros_like(keep_b)
    (_, wide_mask), (_, narrow_mask) = rest
    both = wide_mask * narrow_count + narrow_mask
    got = [
        lax.ppermute(take(3, T_DEV), ("wide", "narrow"), xor_pairs(wide_count * narrow_count, both)),
        swap(take(2, T_DEV), *rest[0]),
        swap(take(1, T_DEV), *rest[1]),
    ]
    got, x_back[2], x_back[0] = lax.optimization_barrier((got, x_back[2], x_back[0]))
    l_back.append(x_back[2][rows:])
    x_back[2] = x_back[2][:rows]
    updated = ancestor - (take(0, T_DEV) + (got[0] + (got[1] + got[2])))

    def give_back(own_part, others):
        back = [own_part] + others
        out = jnp.zeros((NB,) + own_part.shape, jnp.float32)
        for m in range(NB):
            out = lax.dynamic_update_index_in_dim(out, back[m], me ^ m, 0)
        return out

    return (give_back(l_parts[0], l_back), give_back(x_parts[0], x_back), updated)


def solution(mesh):
    placed = (
        P("wide", None, "narrow"),
        P("wide", None, "narrow"),
        P("wide"),
        P("wide", None),
        P("wide"),
        P(("wide", "narrow"), None, None),
    )
    return jax.shard_map(
        local,
        mesh=mesh,
        in_specs=placed,
        out_specs=(
            P("wide", None, "narrow"),
            P("wide", None, "narrow"),
            P(("wide", "narrow"), None, None),
        ),
        check_vma=False,
    )
```

```python
import jax
import jax.numpy as jnp
import numpy as np
from jax import lax
from jax.experimental import pallas as pl
from jax.experimental.pallas import tpu as pltpu
from jax.sharding import PartitionSpec as P

W = 512
B = 128
P_SIZE = 8
T_DEV = 2
NB = W // B
NPAIR = P_SIZE * (P_SIZE + 1) // 2
HIGHEST = lax.Precision.HIGHEST


def dot_nt(a, b):
    return lax.dot_general(
        a, b, (((1,), (1,)), ((), ())), precision=HIGHEST, preferred_element_type=jnp.float32
    )


def dot_nn(a, b):
    return lax.dot_general(
        a, b, (((1,), (0,)), ((), ())), precision=HIGHEST, preferred_element_type=jnp.float32
    )


def lane_of(x, c):
    return jnp.broadcast_to(x[:, c : c + 1], x.shape)


def row_of(x, r):
    return jnp.broadcast_to(x[r : r + 1, :], x.shape)


def inverse_factor(block):
    sub = lax.broadcasted_iota(jnp.int32, (8, B), 0)
    lane = lax.broadcasted_iota(jnp.int32, (8, B), 1)
    total, strip = B // 8, 2
    rows = [block[8 * q : 8 * q + 8, :] for q in range(total)]
    done = [None] * total
    for b in range(0, total, strip):
        mine = range(b, b + strip)
        near = range(b + strip, min(b + 2 * strip, total))
        far = range(b + 2 * strip, total)
        in_strip = (lane >= 8 * b) & (lane < 8 * (b + strip))
        ahead = {q: [lane_of(rows[q], 8 * b + m) for m in range(8 * strip)] for q in near}
        for p in mine:
            lo = 8 * p
            own = (lane >= lo) & (lane < lo + 8)
            cols = [lane_of(rows[p], lo + m) for m in range(8)]
            others = [q for q in mine if q != p]
            mult = {q: [lane_of(rows[q], lo + m) for m in range(8)] for q in others}
            work = jnp.where(own, (lane - lo == sub).astype(jnp.float32), rows[p])
            final = jnp.zeros((8, B), jnp.float32)
            for k in range(0, 8, 2):
                f0, f1 = cols[k], cols[k + 1]
                a, h, c = row_of(f0, k), row_of(f0, k + 1), row_of(f1, k + 1)
                det = a * c - h * h
                recip = 1.0 / det
                ar, hr, cr = a * recip, h * recip, c * recip
                first, second = sub == k, sub == k + 1

                def eliminate(v):
                    r0, r1 = row_of(v, k), row_of(v, k + 1)
                    s0, s1 = cr * r0 - hr * r1, ar * r1 - hr * r0
                    return r0, r1, jnp.where(first, s0, jnp.where(second, s1, v - f0 * s0 - f1 * s1))

                for m in range(k + 2, 8):
                    cols[m] = eliminate(cols[m])[2]
                r0, r1, work = eliminate(work)
                root = lax.rsqrt(a)
                lower = (a * r1 - h * r0) * (root * lax.rsqrt(det))
                final = jnp.where(first, r0 * root, jnp.where(second, lower, final))
            done[p] = jnp.where(lane <= sub + lo, final, 0.0)
            rows[p] = work
            lines = [row_of(work, m) for m in range(8)]
            for q in others:
                new = jnp.where(own, 0.0, rows[q])
                for m in range(8):
                    new = new - mult[q][m] * lines[m]
                rows[q] = new
        lines = [row_of(rows[q], m) for q in mine for m in range(8)]
        for q in near:
            parts = [ahead[q][m] * lines[m] for m in range(4)]
            for m in range(4, 8 * strip):
                parts[m % 4] = parts[m % 4] + ahead[q][m] * lines[m]
            rows[q] = jnp.where(in_strip, 0.0, rows[q]) - ((parts[0] + parts[1]) + (parts[2] + parts[3]))
        if far:
            stack = jnp.concatenate([rows[q] for q in far], axis=0)
            lane_far = lax.broadcasted_iota(jnp.int32, stack.shape, 1)
            in_far = (lane_far >= 8 * b) & (lane_far < 8 * (b + strip))
            zero = jnp.zeros((8, B), jnp.float32)
            tall = jnp.concatenate([rows[q] if q in mine else zero for q in range(total)], axis=0)
            stack = jnp.where(in_far, 0.0, stack) - dot_nn(jnp.where(in_far, stack, 0.0), tall)
            for n, q in enumerate(far):
                rows[q] = stack[8 * n : 8 * n + 8]
    return jnp.concatenate(done, axis=0)


def split_bf16(v):
    high = v.astype(jnp.bfloat16)
    return high, (v - high.astype(jnp.float32)).astype(jnp.bfloat16)


def dot3(left, right, contract):
    dot = lambda a, b: lax.dot_general(
        a, b, (contract, ((), ())), preferred_element_type=jnp.float32
    )
    return dot(left[0], right[0]) + (dot(left[0], right[1]) + dot(left[1], right[0]))


def cut_kernel(info, blocks, near, far_a, far_b, sems):
    me = info[0]
    half = pl.ds((me // 2) * (W // 2), W // 2)
    copies = [
        pltpu.make_async_copy(blocks.at[me ^ 2, half], far_a, sems.at[0]),
        pltpu.make_async_copy(blocks.at[me ^ 3, half], far_b, sems.at[1]),
        pltpu.make_async_copy(blocks.at[me ^ 1], near, sems.at[2]),
    ]
    for c in copies:
        c.start()
    for c in copies:
        c.wait()


def factor_kernel(info, own_ref, r1, r2, r3, l0, l1, l2, l3, mt, a, l, sems):
    me = info[0]
    side = me // 2
    far_rows = pl.ds((1 - side) * (W // 2), W // 2)
    places = [a.at[me], a.at[me ^ 1], a.at[me ^ 2, far_rows], a.at[me ^ 3, far_rows]]
    ins = [own_ref.at[me], r1, r2, r3]
    copies = [pltpu.make_async_copy(ins[m], places[m], sems.at[m]) for m in range(NB)]
    for c in copies:
        c.start()
    for c in copies:
        c.wait()

    @pl.when(side == 1)
    def _():
        for j in range(NB // 2):
            for i in range(NB // 2, NB):
                a[j, pl.ds(i * B, B), :] = a[i, pl.ds(j * B, B), :].T

    row = lax.broadcasted_iota(jnp.int32, (B, B), 0)
    col = lax.broadcasted_iota(jnp.int32, (B, B), 1)
    l[...] = jnp.zeros_like(l)
    mt[...] = jnp.zeros_like(mt)
    eye = (row == col).astype(jnp.float32)
    for k in range(NB):
        here = pl.ds(k * B, B)
        inv = inverse_factor(a[k, here, :])
        l[k, here, :] = jnp.where(row >= col, dot_nt(a[k, here, :], inv), 0.0)
        for i in range(k + 1, NB):
            below = dot_nt(a[k, pl.ds(i * B, B), :], inv)
            l[k, pl.ds(i * B, B), :] = below
            for j in range(k + 1, i + 1):
                a[j, pl.ds(i * B, B), :] -= dot_nt(below, l[k, pl.ds(j * B, B), :])
        mt[k, here, :] = dot_nt(eye, inv)
        for i in range(k):
            total = dot_nt(mt[i, pl.ds(i * B, B), :], l[i, here, :])
            for j in range(i + 1, k):
                total = total + dot_nt(mt[j, pl.ds(i * B, B), :], l[j, here, :])
            mt[k, pl.ds(i * B, B), :] = dot_nt(-total, inv)
    outs = [l0, l1, l2, l3]
    copies = [pltpu.make_async_copy(l.at[me ^ m], outs[m], sems.at[m]) for m in range(NB)]
    for c in copies:
        c.start()
    for c in copies:
        c.wait()


def masked_split(ref, count):
    rows = ref.shape[0]
    live = lax.broadcasted_iota(jnp.int32, (rows, B), 0) < count * B
    return split_bf16(jnp.where(live, ref[...], 0.0))


def inverse_rows(mt, me, blocks, c):
    rows = [
        jnp.concatenate([mt[me ^ m, pl.ds((me ^ k) * B, B), :] for m in (c, c + 1)], axis=1) for k in blocks
    ]
    return split_bf16(jnp.concatenate(rows, axis=0))


def early_kernel(info, counts, own_ref, r1, r2, mt, acc, *sums):
    me = info[0]
    parts = [masked_split(ref, counts[me]) for ref in (own_ref.at[me], r1, r2)]
    left = [jnp.concatenate([part[n] for part in parts], axis=1) for n in range(2)]
    for c in range(0, NB, 2):
        acc[:, pl.ds(c * B, 2 * B)] = dot3(left, inverse_rows(mt, me, range(NB - 1), c), ((1,), (0,)))
    for ref in sums:
        ref[...] = jnp.zeros_like(ref)


def panel_kernel(info, counts, tgt_a, tgt_b, r3, mt, l3, acc, *rest):
    x0, x1, x2, x3, keep, send, xh, xl = rest[-8:]
    if len(rest) == 8:
        keep[...] = jnp.zeros_like(keep)
        send[...] = jnp.zeros_like(send)
    me = info[0]
    count = counts[me]
    rows = P_SIZE * B
    outs = [x0, x1, x2, x3]
    x3[pl.ds(rows, W), :] = l3[...]
    left = masked_split(r3, count)
    for c in range(0, NB, 2):
        got = acc[:, pl.ds(c * B, 2 * B)] + dot3(left, inverse_rows(mt, me, [NB - 1], c), ((1,), (0,)))
        outs[c][pl.ds(0, rows), :] = got[:, :B]
        outs[c + 1][pl.ds(0, rows), :] = got[:, B:]
        high, low = split_bf16(got)
        xh[:, pl.ds(c * B, 2 * B)] = high
        xl[:, pl.ds(c * B, 2 * B)] = low

    half, strip = keep.shape[1:3]
    for j in range(0, P_SIZE, 2):

        @pl.when(j < count)
        def _():
            left = (xh[pl.ds(j * B, rows - j * B), :], xl[pl.ds(j * B, rows - j * B), :])
            right = (xh[pl.ds(j * B, 2 * B), :], xl[pl.ds(j * B, 2 * B), :])
            got = dot3(left, right, ((1,), (1,)))
            for i in range(j, P_SIZE):
                for n in range(2 if i > j else 1):
                    block = got[(i - j) * B : (i - j + 1) * B, n * B : (n + 1) * B]
                    pair = i * (i + 1) // 2 + j + n
                    away = (tgt_a[pair] >= half).astype(jnp.float32)
                    for stream, tgt in enumerate((tgt_a, tgt_b)):
                        at = lax.rem(tgt[pair], half)
                        piece = block[stream * strip : (stream + 1) * strip]
                        keep[stream, at] += piece * (1.0 - away)
                        send[stream, at] += piece * away


SMEM = pl.BlockSpec(memory_space=pltpu.SMEM)
ANY = pl.BlockSpec(memory_space=pl.ANY)
VMEM = pl.BlockSpec(memory_space=pltpu.VMEM)


def xor_pairs(size, mask):
    return [(i, i ^ mask) for i in range(size)]


def log2(n):
    return n.bit_length() - 1


def swap(x, axis, mask):
    return lax.ppermute(x, axis, xor_pairs(lax.axis_size(axis), mask))


def relative_index(owner, slot, wide_me, narrow_me, steps):
    away = {"wide": owner ^ wide_me, "narrow": (slot // T_DEV) ^ narrow_me}
    index = jnp.zeros_like(owner)
    for axis, mask in steps:
        index = index * 2 + ((away[axis] // mask) & 1)
    return index * T_DEV + slot % T_DEV


def local(diag_block, panel, panel_count, pair_owner, pair_slot, ancestor):
    narrow_count = lax.axis_size("narrow")
    wide_count = lax.axis_size("wide")
    me = lax.axis_index("narrow")
    wide_me = lax.axis_index("wide")
    assert narrow_count == NB and diag_block.shape[0] == NB
    masks = range(1, NB)
    own = lambda x, m: lax.dynamic_index_in_dim(x, me ^ m, 0, keepdims=False)
    info = me.astype(jnp.int32).reshape(1)
    cut = [jax.ShapeDtypeStruct((rows, B), jnp.float32) for rows in (W, W // 2, W // 2)]
    cut = pl.pallas_call(
        cut_kernel,
        out_shape=cut,
        in_specs=[SMEM, pl.BlockSpec(memory_space=pltpu.HBM)],
        out_specs=[ANY] * 3,
        scratch_shapes=[pltpu.SemaphoreType.DMA((3,))],
        compiler_params=pltpu.CompilerParams(vmem_limit_bytes=2 * 2**20),
        cost_estimate=pl.CostEstimate(flops=0, bytes_accessed=2**20, transcendentals=0),
        name="cut",
    )(info, diag_block)
    diag_in = [swap(part, "narrow", m) for m, part in zip(masks, cut)]
    panel_out = [own(panel, m) for m in masks]
    diag_in, panel_out = lax.optimization_barrier((diag_in, panel_out))
    panel_in = [swap(panel_out[m - 1], "narrow", m) for m in masks]

    narrow_steps = [("narrow", 1 << b) for b in range(log2(narrow_count))]
    wide_steps = [("wide", 1 << b) for b in range(log2(wide_count))]
    first, last = narrow_steps[:1], wide_steps[2:] + narrow_steps[1:]
    steps_a = first + wide_steps[:2] + last
    steps_b = first + wide_steps[1::-1] + last
    owner = lax.dynamic_slice_in_dim(pair_owner[:, 0], me * NPAIR, NPAIR)
    slot = lax.dynamic_slice_in_dim(pair_slot, me * NPAIR, NPAIR)
    tgt_a = relative_index(owner, slot, wide_me, me, steps_a)
    tgt_b = relative_index(owner, slot, wide_me, me, steps_b)

    slab = jax.ShapeDtypeStruct((W, B), jnp.float32)
    *l_parts, mt = pl.pallas_call(
        factor_kernel,
        out_shape=[slab] * NB + [jax.ShapeDtypeStruct((NB, W, B), jnp.float32)],
        in_specs=[SMEM] + [ANY] * NB,
        out_specs=[ANY] * NB + [VMEM],
        scratch_shapes=[pltpu.VMEM((NB, W, B), jnp.float32)] * 2 + [pltpu.SemaphoreType.DMA((NB,))],
        compiler_params=pltpu.CompilerParams(vmem_limit_bytes=12 * 2**20),
        cost_estimate=pl.CostEstimate(flops=2 * 10**8, bytes_accessed=4 * 10**6, transcendentals=0),
        name="factor",
    )(info, diag_block, *diag_in)

    rows = P_SIZE * B
    blocks = wide_count * narrow_count * T_DEV
    slab = jax.ShapeDtypeStruct((rows, B), jnp.float32)
    longer = jax.ShapeDtypeStruct((rows + W, B), jnp.float32)
    part = jax.ShapeDtypeStruct((2, blocks // 2, B // 2, B), jnp.float32)
    room = pltpu.CompilerParams(vmem_limit_bytes=16 * 2**20 + 4 * blocks * B * B)
    sums = 0
    acc, *empty = pl.pallas_call(
        early_kernel,
        out_shape=[jax.ShapeDtypeStruct((rows, W), jnp.float32)] + [part] * sums,
        in_specs=[SMEM] * 2 + [VMEM] * 4,
        out_specs=[VMEM] * (1 + sums),
        compiler_params=room,
        cost_estimate=pl.CostEstimate(flops=5 * 10**8, bytes_accessed=10 * 10**6, transcendentals=0),
        name="early",
    )(info, panel_count, panel, *panel_in[:2], mt)
    *x_parts, keep, send = pl.pallas_call(
        panel_kernel,
        out_shape=[slab] * (NB - 1) + [longer, part, part],
        in_specs=[SMEM] * 4 + [VMEM] * (4 + sums),
        out_specs=[VMEM] * (NB + 2),
        scratch_shapes=[pltpu.VMEM((rows, W), jnp.bfloat16)] * 2,
        input_output_aliases={8 + n: NB + n for n in range(sums)},
        compiler_params=room,
        cost_estimate=pl.CostEstimate(flops=10**9, bytes_accessed=10 * 10**6, transcendentals=0),
        name="panel",
    )(info, panel_count, tgt_a, tgt_b, panel_in[2], mt, l_parts[3], acc, *empty)

    l_back = [swap(l_parts[m], "narrow", m) for m in (1, 2)]
    x_back = [swap(x_parts[m], "narrow", m) for m in masks]

    send, l_back[1] = lax.optimization_barrier((send, l_back[1]))
    got = swap(send, "narrow", 1)
    half = blocks // 4
    upper = lambda u, n: u[n, half:]
    lower = lambda u, n: u[n, :half]
    send_a = upper(keep, 0) + upper(got, 0)
    send_b = upper(keep, 1) + upper(got, 1)
    keep_a = lower(keep, 0) + lower(got, 0)
    keep_b = lower(keep, 1) + lower(got, 1)
    for n in (1, 2):
        if n == 2:
            send_a, send_b, x_back[1] = lax.optimization_barrier((send_a, send_b, x_back[1]))
        else:
            send_a, send_b = lax.optimization_barrier((send_a, send_b))
        got_a = swap(send_a, *steps_a[n])
        got_b = swap(send_b, *steps_b[n])
        half = half // 2
        if n == 1:
            send_a, send_b = keep_a[half:] + got_a[half:], keep_b[half:] + got_b[half:]
            keep_a, keep_b = keep_a[:half] + got_a[:half], keep_b[:half] + got_b[:half]
    rest = steps_a[3:]
    take = lambda n, size: jnp.concatenate(
        [u[n * size : (n + 1) * size] + v[n * size : (n + 1) * size] for u, v in ((keep_a, got_a), (keep_b, got_b))],
        axis=1,
    )
    while len(rest) > 2:
        got = swap(take(1, half), *rest.pop(0))
        keep_a = take(0, half) + got
        half = half // 2
        keep_a, keep_b = keep_a[:, : B // 2], keep_a[:, B // 2 :]
        got_a, got_b = jnp.zeros_like(keep_a), jnp.zeros_like(keep_b)
    (_, wide_mask), (_, narrow_mask) = rest
    both = wide_mask * narrow_count + narrow_mask
    got = [
        lax.ppermute(take(3, T_DEV), ("wide", "narrow"), xor_pairs(wide_count * narrow_count, both)),
        swap(take(2, T_DEV), *rest[0]),
        swap(take(1, T_DEV), *rest[1]),
    ]
    got, x_back[2], x_back[0] = lax.optimization_barrier((got, x_back[2], x_back[0]))
    l_back.append(x_back[2][rows:])
    x_back[2] = x_back[2][:rows]
    updated = ancestor - (take(0, T_DEV) + (got[0] + (got[1] + got[2])))

    def give_back(own_part, others):
        back = [own_part] + others
        out = jnp.zeros((NB,) + own_part.shape, jnp.float32)
        for m in range(NB):
            out = lax.dynamic_update_index_in_dim(out, back[m], me ^ m, 0)
        return out

    return (give_back(l_parts[0], l_back), give_back(x_parts[0], x_back), updated)


def solution(mesh):
    placed = (
        P("wide", None, "narrow"),
        P("wide", None, "narrow"),
        P("wide"),
        P("wide", None),
        P("wide"),
        P(("wide", "narrow"), None, None),
    )
    return jax.shard_map(
        local,
        mesh=mesh,
        in_specs=placed,
        out_specs=(
            P("wide", None, "narrow"),
            P("wide", None, "narrow"),
            P(("wide", "narrow"), None, None),
        ),
        check_vma=False,
    )
```

```python
import jax
import jax.numpy as jnp
import numpy as np
from jax import lax
from jax.experimental import pallas as pl
from jax.experimental.pallas import tpu as pltpu
from jax.sharding import PartitionSpec as P

W = 512
B = 128
P_SIZE = 8
T_DEV = 2
NB = W // B
NPAIR = P_SIZE * (P_SIZE + 1) // 2
HIGHEST = lax.Precision.HIGHEST


def dot_nt(a, b):
    return lax.dot_general(
        a, b, (((1,), (1,)), ((), ())), precision=HIGHEST, preferred_element_type=jnp.float32
    )


def dot_nn(a, b):
    return lax.dot_general(
        a, b, (((1,), (0,)), ((), ())), precision=HIGHEST, preferred_element_type=jnp.float32
    )


def lane_of(x, c):
    return jnp.broadcast_to(x[:, c : c + 1], x.shape)


def row_of(x, r):
    return jnp.broadcast_to(x[r : r + 1, :], x.shape)


def inverse_factor(block):
    sub = lax.broadcasted_iota(jnp.int32, (8, B), 0)
    lane = lax.broadcasted_iota(jnp.int32, (8, B), 1)
    total, strip = B // 8, 2
    rows = [block[8 * q : 8 * q + 8, :] for q in range(total)]
    done = [None] * total
    for b in range(0, total, strip):
        mine = range(b, b + strip)
        near = range(b + strip, min(b + 2 * strip, total))
        far = range(b + 2 * strip, total)
        in_strip = (lane >= 8 * b) & (lane < 8 * (b + strip))
        ahead = {q: [lane_of(rows[q], 8 * b + m) for m in range(8 * strip)] for q in near}
        for p in mine:
            lo = 8 * p
            own = (lane >= lo) & (lane < lo + 8)
            cols = [lane_of(rows[p], lo + m) for m in range(8)]
            others = [q for q in mine if q != p]
            mult = {q: [lane_of(rows[q], lo + m) for m in range(8)] for q in others}
            work = jnp.where(own, (lane - lo == sub).astype(jnp.float32), rows[p])
            final = jnp.zeros((8, B), jnp.float32)
            for k in range(0, 8, 2):
                f0, f1 = cols[k], cols[k + 1]
                a, h, c = row_of(f0, k), row_of(f0, k + 1), row_of(f1, k + 1)
                det = a * c - h * h
                recip = 1.0 / det
                ar, hr, cr = a * recip, h * recip, c * recip
                first, second = sub == k, sub == k + 1

                def eliminate(v):
                    r0, r1 = row_of(v, k), row_of(v, k + 1)
                    s0, s1 = cr * r0 - hr * r1, ar * r1 - hr * r0
                    return r0, r1, jnp.where(first, s0, jnp.where(second, s1, v - f0 * s0 - f1 * s1))

                for m in range(k + 2, 8):
                    cols[m] = eliminate(cols[m])[2]
                r0, r1, work = eliminate(work)
                root = lax.rsqrt(a)
                lower = (a * r1 - h * r0) * (root * lax.rsqrt(det))
                final = jnp.where(first, r0 * root, jnp.where(second, lower, final))
            done[p] = jnp.where(lane <= sub + lo, final, 0.0)
            rows[p] = work
            lines = [row_of(work, m) for m in range(8)]
            for q in others:
                new = jnp.where(own, 0.0, rows[q])
                for m in range(8):
                    new = new - mult[q][m] * lines[m]
                rows[q] = new
        lines = [row_of(rows[q], m) for q in mine for m in range(8)]
        for q in near:
            parts = [ahead[q][m] * lines[m] for m in range(4)]
            for m in range(4, 8 * strip):
                parts[m % 4] = parts[m % 4] + ahead[q][m] * lines[m]
            rows[q] = jnp.where(in_strip, 0.0, rows[q]) - ((parts[0] + parts[1]) + (parts[2] + parts[3]))
        if far:
            stack = jnp.concatenate([rows[q] for q in far], axis=0)
            lane_far = lax.broadcasted_iota(jnp.int32, stack.shape, 1)
            in_far = (lane_far >= 8 * b) & (lane_far < 8 * (b + strip))
            zero = jnp.zeros((8, B), jnp.float32)
            tall = jnp.concatenate([rows[q] if q in mine else zero for q in range(total)], axis=0)
            stack = jnp.where(in_far, 0.0, stack) - dot_nn(jnp.where(in_far, stack, 0.0), tall)
            for n, q in enumerate(far):
                rows[q] = stack[8 * n : 8 * n + 8]
    return jnp.concatenate(done, axis=0)


def split_bf16(v):
    high = v.astype(jnp.bfloat16)
    return high, (v - high.astype(jnp.float32)).astype(jnp.bfloat16)


def dot3(left, right, contract):
    dot = lambda a, b: lax.dot_general(
        a, b, (contract, ((), ())), preferred_element_type=jnp.float32
    )
    return dot(left[0], right[0]) + (dot(left[0], right[1]) + dot(left[1], right[0]))


def cut_kernel(info, blocks, near, far_a, far_b, sems):
    me = info[0]
    half = pl.ds((me // 2) * (W // 2), W // 2)
    copies = [
        pltpu.make_async_copy(blocks.at[me ^ 2, half], far_a, sems.at[0]),
        pltpu.make_async_copy(blocks.at[me ^ 3, half], far_b, sems.at[1]),
        pltpu.make_async_copy(blocks.at[me ^ 1], near, sems.at[2]),
    ]
    for c in copies:
        c.start()
    for c in copies:
        c.wait()


def factor_kernel(info, own_ref, r1, r2, r3, l0, l1, l2, l3, mt, a, l, sems):
    me = info[0]
    side = me // 2
    far_rows = pl.ds((1 - side) * (W // 2), W // 2)
    places = [a.at[me], a.at[me ^ 1], a.at[me ^ 2, far_rows], a.at[me ^ 3, far_rows]]
    ins = [own_ref.at[me], r1, r2, r3]
    copies = [pltpu.make_async_copy(ins[m], places[m], sems.at[m]) for m in range(NB)]
    for c in copies:
        c.start()
    for c in copies:
        c.wait()

    @pl.when(side == 1)
    def _():
        for j in range(NB // 2):
            for i in range(NB // 2, NB):
                a[j, pl.ds(i * B, B), :] = a[i, pl.ds(j * B, B), :].T

    row = lax.broadcasted_iota(jnp.int32, (B, B), 0)
    col = lax.broadcasted_iota(jnp.int32, (B, B), 1)
    l[...] = jnp.zeros_like(l)
    mt[...] = jnp.zeros_like(mt)
    eye = (row == col).astype(jnp.float32)
    for k in range(NB):
        here = pl.ds(k * B, B)
        inv = inverse_factor(a[k, here, :])
        l[k, here, :] = jnp.where(row >= col, dot_nt(a[k, here, :], inv), 0.0)
        for i in range(k + 1, NB):
            below = dot_nt(a[k, pl.ds(i * B, B), :], inv)
            l[k, pl.ds(i * B, B), :] = below
            for j in range(k + 1, i + 1):
                a[j, pl.ds(i * B, B), :] -= dot_nt(below, l[k, pl.ds(j * B, B), :])
        mt[k, here, :] = dot_nt(eye, inv)
        for i in range(k):
            total = dot_nt(mt[i, pl.ds(i * B, B), :], l[i, here, :])
            for j in range(i + 1, k):
                total = total + dot_nt(mt[j, pl.ds(i * B, B), :], l[j, here, :])
            mt[k, pl.ds(i * B, B), :] = dot_nt(-total, inv)
    outs = [l0, l1, l2, l3]
    copies = [pltpu.make_async_copy(l.at[me ^ m], outs[m], sems.at[m]) for m in range(NB)]
    for c in copies:
        c.start()
    for c in copies:
        c.wait()


def masked_split(ref, count):
    rows = ref.shape[0]
    live = lax.broadcasted_iota(jnp.int32, (rows, B), 0) < count * B
    return split_bf16(jnp.where(live, ref[...], 0.0))


def inverse_rows(mt, me, blocks, c):
    rows = [
        jnp.concatenate([mt[me ^ m, pl.ds((me ^ k) * B, B), :] for m in (c, c + 1)], axis=1) for k in blocks
    ]
    return split_bf16(jnp.concatenate(rows, axis=0))


def early_kernel(info, counts, own_ref, r1, mt, acc):
    me = info[0]
    parts = [masked_split(ref, counts[me]) for ref in (own_ref.at[me], r1)]
    left = [jnp.concatenate([part[n] for part in parts], axis=1) for n in range(2)]
    for c in range(0, NB, 2):
        acc[:, pl.ds(c * B, 2 * B)] = dot3(left, inverse_rows(mt, me, (0, 1), c), ((1,), (0,)))


def panel_kernel(info, counts, tgt_a, tgt_b, r2, r3, mt, l3, acc, x0, x1, x2, x3, keep, send, xh, xl):
    keep[...] = jnp.zeros_like(keep)
    send[...] = jnp.zeros_like(send)
    me = info[0]
    count = counts[me]
    rows = P_SIZE * B
    outs = [x0, x1, x2, x3]
    x3[pl.ds(rows, W), :] = l3[...]
    parts = [masked_split(ref, count) for ref in (r2, r3)]
    left = [jnp.concatenate([part[n] for part in parts], axis=1) for n in range(2)]
    for c in range(0, NB, 2):
        got = acc[:, pl.ds(c * B, 2 * B)] + dot3(left, inverse_rows(mt, me, (2, 3), c), ((1,), (0,)))
        outs[c][pl.ds(0, rows), :] = got[:, :B]
        outs[c + 1][pl.ds(0, rows), :] = got[:, B:]
        high, low = split_bf16(got)
        xh[:, pl.ds(c * B, 2 * B)] = high
        xl[:, pl.ds(c * B, 2 * B)] = low

    half, strip = keep.shape[1:3]
    for j in range(0, P_SIZE, 2):

        @pl.when(j < count)
        def _():
            left = (xh[pl.ds(j * B, rows - j * B), :], xl[pl.ds(j * B, rows - j * B), :])
            right = (xh[pl.ds(j * B, 2 * B), :], xl[pl.ds(j * B, 2 * B), :])
            got = dot3(left, right, ((1,), (1,)))
            for i in range(j, P_SIZE):
                for n in range(2 if i > j else 1):
                    block = got[(i - j) * B : (i - j + 1) * B, n * B : (n + 1) * B]
                    pair = i * (i + 1) // 2 + j + n
                    away = (tgt_a[pair] >= half).astype(jnp.float32)
                    for stream, tgt in enumerate((tgt_a, tgt_b)):
                        at = lax.rem(tgt[pair], half)
                        piece = block[stream * strip : (stream + 1) * strip]
                        keep[stream, at] += piece * (1.0 - away)
                        send[stream, at] += piece * away


SMEM = pl.BlockSpec(memory_space=pltpu.SMEM)
ANY = pl.BlockSpec(memory_space=pl.ANY)
VMEM = pl.BlockSpec(memory_space=pltpu.VMEM)


def xor_pairs(size, mask):
    return [(i, i ^ mask) for i in range(size)]


def log2(n):
    return n.bit_length() - 1


def swap(x, axis, mask):
    return lax.ppermute(x, axis, xor_pairs(lax.axis_size(axis), mask))


def relative_index(owner, slot, wide_me, narrow_me, steps):
    away = {"wide": owner ^ wide_me, "narrow": (slot // T_DEV) ^ narrow_me}
    index = jnp.zeros_like(owner)
    for axis, mask in steps:
        index = index * 2 + ((away[axis] // mask) & 1)
    return index * T_DEV + slot % T_DEV


def local(diag_block, panel, panel_count, pair_owner, pair_slot, ancestor):
    narrow_count = lax.axis_size("narrow")
    wide_count = lax.axis_size("wide")
    me = lax.axis_index("narrow")
    wide_me = lax.axis_index("wide")
    assert narrow_count == NB and diag_block.shape[0] == NB
    masks = range(1, NB)
    own = lambda x, m: lax.dynamic_index_in_dim(x, me ^ m, 0, keepdims=False)
    info = me.astype(jnp.int32).reshape(1)
    cut = [jax.ShapeDtypeStruct((rows, B), jnp.float32) for rows in (W, W // 2, W // 2)]
    cut = pl.pallas_call(
        cut_kernel,
        out_shape=cut,
        in_specs=[SMEM, pl.BlockSpec(memory_space=pltpu.HBM)],
        out_specs=[ANY] * 3,
        scratch_shapes=[pltpu.SemaphoreType.DMA((3,))],
        compiler_params=pltpu.CompilerParams(vmem_limit_bytes=2 * 2**20),
        cost_estimate=pl.CostEstimate(flops=0, bytes_accessed=2**20, transcendentals=0),
        name="cut",
    )(info, diag_block)
    diag_in = [swap(part, "narrow", m) for m, part in zip(masks, cut)]
    panel_out = [own(panel, m) for m in masks]
    diag_in, panel_out = lax.optimization_barrier((diag_in, panel_out))
    panel_in = [swap(panel_out[m - 1], "narrow", m) for m in masks]

    narrow_steps = [("narrow", 1 << b) for b in range(log2(narrow_count))]
    wide_steps = [("wide", 1 << b) for b in range(log2(wide_count))]
    first, last = narrow_steps[:1], wide_steps[2:] + narrow_steps[1:]
    steps_a = first + wide_steps[:2] + last
    steps_b = first + wide_steps[1::-1] + last
    owner = lax.dynamic_slice_in_dim(pair_owner[:, 0], me * NPAIR, NPAIR)
    slot = lax.dynamic_slice_in_dim(pair_slot, me * NPAIR, NPAIR)
    tgt_a = relative_index(owner, slot, wide_me, me, steps_a)
    tgt_b = relative_index(owner, slot, wide_me, me, steps_b)

    slab = jax.ShapeDtypeStruct((W, B), jnp.float32)
    *l_parts, mt = pl.pallas_call(
        factor_kernel,
        out_shape=[slab] * NB + [jax.ShapeDtypeStruct((NB, W, B), jnp.float32)],
        in_specs=[SMEM] + [ANY] * NB,
        out_specs=[ANY] * NB + [VMEM],
        scratch_shapes=[pltpu.VMEM((NB, W, B), jnp.float32)] * 2 + [pltpu.SemaphoreType.DMA((NB,))],
        compiler_params=pltpu.CompilerParams(vmem_limit_bytes=12 * 2**20),
        cost_estimate=pl.CostEstimate(flops=2 * 10**8, bytes_accessed=4 * 10**6, transcendentals=0),
        name="factor",
    )(info, diag_block, *diag_in)

    rows = P_SIZE * B
    blocks = wide_count * narrow_count * T_DEV
    slab = jax.ShapeDtypeStruct((rows, B), jnp.float32)
    longer = jax.ShapeDtypeStruct((rows + W, B), jnp.float32)
    part = jax.ShapeDtypeStruct((2, blocks // 2, B // 2, B), jnp.float32)
    room = pltpu.CompilerParams(vmem_limit_bytes=16 * 2**20 + 4 * blocks * B * B)
    acc = pl.pallas_call(
        early_kernel,
        out_shape=jax.ShapeDtypeStruct((rows, W), jnp.float32),
        in_specs=[SMEM] * 2 + [VMEM] * 3,
        out_specs=VMEM,
        compiler_params=room,
        cost_estimate=pl.CostEstimate(flops=5 * 10**8, bytes_accessed=10 * 10**6, transcendentals=0),
        name="early",
    )(info, panel_count, panel, panel_in[0], mt)
    *x_parts, keep, send = pl.pallas_call(
        panel_kernel,
        out_shape=[slab] * (NB - 1) + [longer, part, part],
        in_specs=[SMEM] * 4 + [VMEM] * 5,
        out_specs=[VMEM] * (NB + 2),
        scratch_shapes=[pltpu.VMEM((rows, W), jnp.bfloat16)] * 2,
        compiler_params=room,
        cost_estimate=pl.CostEstimate(flops=10**9, bytes_accessed=10 * 10**6, transcendentals=0),
        name="panel",
    )(info, panel_count, tgt_a, tgt_b, *panel_in[1:], mt, l_parts[3], acc)

    l_back = [swap(l_parts[m], "narrow", m) for m in (1, 2)]
    x_back = [swap(x_parts[m], "narrow", m) for m in masks]

    send, l_back[1] = lax.optimization_barrier((send, l_back[1]))
    got = swap(send, "narrow", 1)
    half = blocks // 4
    upper = lambda u, n: u[n, half:]
    lower = lambda u, n: u[n, :half]
    send_a = upper(keep, 0) + upper(got, 0)
    send_b = upper(keep, 1) + upper(got, 1)
    keep_a = lower(keep, 0) + lower(got, 0)
    keep_b = lower(keep, 1) + lower(got, 1)
    for n in (1, 2):
        if n == 2:
            send_a, send_b, x_back[1] = lax.optimization_barrier((send_a, send_b, x_back[1]))
        else:
            send_a, send_b = lax.optimization_barrier((send_a, send_b))
        got_a = swap(send_a, *steps_a[n])
        got_b = swap(send_b, *steps_b[n])
        half = half // 2
        if n == 1:
            send_a, send_b = keep_a[half:] + got_a[half:], keep_b[half:] + got_b[half:]
            keep_a, keep_b = keep_a[:half] + got_a[:half], keep_b[:half] + got_b[:half]
    rest = steps_a[3:]
    take = lambda n, size: jnp.concatenate(
        [u[n * size : (n + 1) * size] + v[n * size : (n + 1) * size] for u, v in ((keep_a, got_a), (keep_b, got_b))],
        axis=1,
    )
    while len(rest) > 2:
        got = swap(take(1, half), *rest.pop(0))
        keep_a = take(0, half) + got
        half = half // 2
        keep_a, keep_b = keep_a[:, : B // 2], keep_a[:, B // 2 :]
        got_a, got_b = jnp.zeros_like(keep_a), jnp.zeros_like(keep_b)
    (_, wide_mask), (_, narrow_mask) = rest
    both = wide_mask * narrow_count + narrow_mask
    got = [
        lax.ppermute(take(3, T_DEV), ("wide", "narrow"), xor_pairs(wide_count * narrow_count, both)),
        swap(take(2, T_DEV), *rest[0]),
        swap(take(1, T_DEV), *rest[1]),
    ]
    got, x_back[2], x_back[0] = lax.optimization_barrier((got, x_back[2], x_back[0]))
    l_back.append(x_back[2][rows:])
    x_back[2] = x_back[2][:rows]
    updated = ancestor - (take(0, T_DEV) + (got[0] + (got[1] + got[2])))

    def give_back(own_part, others):
        back = [own_part] + others
        out = jnp.zeros((NB,) + own_part.shape, jnp.float32)
        for m in range(NB):
            out = lax.dynamic_update_index_in_dim(out, back[m], me ^ m, 0)
        return out

    return (give_back(l_parts[0], l_back), give_back(x_parts[0], x_back), updated)


def solution(mesh):
    placed = (
        P("wide", None, "narrow"),
        P("wide", None, "narrow"),
        P("wide"),
        P("wide", None),
        P("wide"),
        P(("wide", "narrow"), None, None),
    )
    return jax.shard_map(
        local,
        mesh=mesh,
        in_specs=placed,
        out_specs=(
            P("wide", None, "narrow"),
            P("wide", None, "narrow"),
            P(("wide", "narrow"), None, None),
        ),
        check_vma=False,
    )
```
